32 devices in a mesh: dp: 8 (over z, x), mp: 4 (over y, core).
Axes of the slice: x: 2, y: 2, z: 4, core: 2. Of those that a mesh axis runs over, the one named last changes fastest.
Arguments:
- tokens: bfloat16 [4096, 1536], P(('dp', 'mp')), may hold values from -6 to 6
- caption: bfloat16 [8, 256, 4096], P('dp'), may hold values from -6 to 6
- condition: float32 [8, 1536], P('dp'), may hold values from -6 to 6
- cotangent: bfloat16 [4096, 1536], P(('dp', 'mp')), may hold values from -6 to 6
- qkv_weight: bfloat16 [3, 1536, 1536], P(None, 'dp', 'mp'), may hold values from -0.15625 to 0.15625
- proj_weight: bfloat16 [1536, 1536], P('mp', 'dp'), may hold values from -0.15625 to 0.15625
- text_weight: bfloat16 [2, 4096, 1536], P(None, 'dp', 'mp'), may hold values from -0.09375 to 0.09375
- ffn_weight: bfloat16 [2, 1536, 4096], P(None, 'dp', 'mp'), may hold values from -0.15625 to 0.15625
- down_weight: bfloat16 [4096, 1536], P('mp', 'dp'), may hold values from -0.09375 to 0.09375
- ada_weight: bfloat16 [1536, 6144], P('dp', 'mp'), may hold values from -0.15625 to 0.15625
- norm_gains: float32 [4, 1536], replicated, may hold values from 0.5 to 1.5
- head_gains: float32 [3, 1536], replicated, may hold values from 0.5 to 1.5
- ada_bias: float32 [6144], replicated, may hold values from -3 to 3
- cross_gate: float32 [24], replicated, may hold values from -1.5 to 1.5
- group_map: int32 [8], replicated, may hold values from 0 to 7, as said below
- grid_width: int32 [8], replicated, may hold values from 32 to 64, as said below
- caption_len: int32 [8], replicated, may hold values from 1 to 256, as said below
Outputs:
- block_out: bfloat16 [4096, 1536], P(('dp', 'mp'))
- grad_tokens: float32 [4096, 1536], P(('dp', 'mp'))
- grad_caption: float32 [8, 256, 4096], P('dp', None, 'mp')
- grad_condition: float32 [8, 1536], P('dp', 'mp')
- grad_qkv: float32 [3, 1536, 1536], P(None, 'dp', 'mp')
- grad_proj: float32 [1536, 1536], P('mp', 'dp')
- grad_text: float32 [2, 4096, 1536], P(None, 'dp', 'mp')
- grad_ffn: float32 [2, 1536, 4096], P(None, 'dp', 'mp')
- grad_down: float32 [4096, 1536], P('mp', 'dp')
- grad_ada: float32 [1536, 6144], P('dp', 'mp')
- grad_norms: float32 [4, 1536], replicated
- grad_heads: float32 [3, 1536], replicated
- grad_bias: float32 [6144], replicated
- grad_gate: float32 [24], replicated
The draws below stay inside these ranges and needn't reach their ends.
Inputs may be any that keep to these rules, and one draw needn't show every extreme that they name: `group_map`: entry i is the first data index of the group holding index i; groups are runs of 1 to 4 consecutive indices, and some group has exactly 4. `grid_width`: equal within a group; either 32 or 64. `caption_len`: some index has 256.
All inputs are finite; a program needn't handle non-finite values.
Results may differ from the reference program's by a relative error of at most 0.022.
Values may be sent and summed in bfloat16 or wider, within the bound.
No kernel may reach another device: no remote copies, remote signals or barrier semaphores. Data moves between devices by JAX's collectives and lax.ppermute only.
A program may use at most 192 MiB of HBM per device.

```python
import math
import jax
import jax.numpy as jnp
from jax import lax

D = 1536
HEADS = 24
HD = 64
FF = 4096
CD = 4096
CAP = 256
GMAX = 4
GRID = 32
TOK_DP = 512
TOKENS = 4096
N_DP = 8


def partition_firsts(key):
    size_key, pick_key = jax.random.split(key)
    run_sizes = jax.random.randint(size_key, (N_DP,), 1, GMAX + 1)
    forced = jax.random.randint(pick_key, (), 0, 2)
    run_sizes = jnp.where(jnp.arange(N_DP) == forced, GMAX, run_sizes)
    starts = jnp.cumsum(run_sizes) - run_sizes
    slot_ids = jnp.arange(N_DP)
    chosen = jnp.where(starts[None, :] <= slot_ids[:, None], starts[None, :], 0)
    return jnp.max(chosen, axis=1).astype(jnp.int32)


def draw_group_map(key, part):
    return partition_firsts(key)


def draw_grid_width(key, part):
    firsts = partition_firsts(key)
    key = jax.random.fold_in(key, 11)
    doubles = jax.random.randint(key, (N_DP,), 1, 3)
    return (GRID * doubles[firsts]).astype(jnp.int32)


def draw_caption_len(key, part):
    key = jax.random.fold_in(key, 23)
    len_key, pick_key = jax.random.split(key)
    lengths = jax.random.randint(len_key, (N_DP,), 1, CAP + 1)
    forced = jax.random.randint(pick_key, (), 0, N_DP)
    return jnp.where(jnp.arange(N_DP) == forced, CAP, lengths).astype(jnp.int32)


def raised(values, own_key, source, target, parts, factor):
    owner, partner = [(jnp.arange(values.shape[dim]) // (values.shape[dim] // parts)).reshape([-1 if axis == dim else 1 for axis in range(values.ndim)]) for dim in (source, target)]
    chosen = jax.random.permutation(own_key, parts)[partner]
    strong = (owner == chosen) | (owner == (partner + parts // 2) % parts)
    return jnp.where(strong, factor * values, values)


def level_of(stream_key, dims, cuts, smallest, high):
    level, own = 1.0, jax.random.fold_in(stream_key, 6)
    for position, blocks in cuts:
        heights = jnp.exp(jax.random.uniform(jax.random.fold_in(own, position), (blocks,), jnp.float32, smallest / len(cuts), high / len(cuts)))
        level = level * jnp.repeat(heights, dims[position] // blocks).reshape([-1 if axis == position else 1 for axis in range(len(dims))])
    return level


def centred(key, extent, width, reach, cuts=(), kind=jnp.bfloat16):
    values = width * jax.random.normal(key, extent, jnp.float32)
    if cuts:
        values = values * level_of(key, extent, cuts, -0.22, 0.18)
    return jnp.clip(values, -reach, reach).astype(kind)


def heavy_noise(key, extent, spread, limit, cuts, heavy, kind=jnp.bfloat16):
    entries = spread * jax.random.normal(key, extent, jnp.float32)
    if cuts:
        entries = entries * level_of(key, extent, cuts, -0.22, 0.18)
    return jnp.clip(raised(entries, jax.random.fold_in(key, 3), *heavy), -limit, limit).astype(kind)


def setup_inputs(seed: int = 0) -> dict:
    seeds = jax.random.split(jax.random.key(seed), 18)
    tokens = heavy_noise(seeds[0], (TOKENS, D), 1.0, 6.0, ((0, 32),), (0, 1, 32, 2.75))
    caption = heavy_noise(seeds[1], (N_DP, CAP, CD), 1.0, 6.0, ((0, 8),), (0, 2, 8, 2.0))
    condition = centred(seeds[2], (N_DP, D), 1.0, 6.0, ((0, 8),), jnp.float32)
    cotangent = centred(seeds[3], (TOKENS, D), 1.0, 6.0, ((0, 32),))
    qkv_weight = centred(seeds[4], (3, D, D), D ** -0.5, 0.15625, ((1, 8), (2, 4)))
    proj_weight = centred(seeds[5], (D, D), D ** -0.5, 0.15625, ((0, 4), (1, 8)))
    text_weight = centred(seeds[6], (2, CD, D), CD ** -0.5, 0.09375, ((1, 8), (2, 4)))
    ffn_weight = centred(seeds[7], (2, D, FF), D ** -0.5, 0.15625, ((1, 8), (2, 4)))
    down_weight = centred(seeds[8], (FF, D), FF ** -0.5, 0.09375, ((0, 4), (1, 8)))
    ada_weight = centred(seeds[9], (D, 4 * D), D ** -0.5, 0.15625, ((0, 8), (1, 4)))
    norm_gains = jnp.clip(1.0 + 0.1 * jax.random.normal(seeds[10], (4, D), jnp.float32), 0.5, 1.5)
    head_gains = jnp.clip(1.0 + 0.1 * jax.random.normal(seeds[11], (3, D), jnp.float32), 0.5, 1.5)
    ada_bias = centred(seeds[12], (4 * D,), 0.5, 3.0, (), jnp.float32)
    cross_gate = jnp.clip(jax.random.uniform(seeds[13], (HEADS,), jnp.float32, -1.5, 1.5), -1.5, 1.5)
    group_map = draw_group_map(jax.random.fold_in(seeds[17], 71), 0)
    grid_width = draw_grid_width(jax.random.fold_in(seeds[17], 71), 0)
    caption_len = draw_caption_len(jax.random.fold_in(seeds[17], 71), 0)
    return {"tokens": tokens, "caption": caption, "condition": condition, "cotangent": cotangent, "qkv_weight": qkv_weight, "proj_weight": proj_weight, "text_weight": text_weight, "ffn_weight": ffn_weight, "down_weight": down_weight, "ada_weight": ada_weight, "norm_gains": norm_gains, "head_gains": head_gains, "ada_bias": ada_bias, "cross_gate": cross_gate, "group_map": group_map, "grid_width": grid_width, "caption_len": caption_len}


EPS = 1e-06
NEG = -1e+30

@jax.custom_vjp
def low(v):
    return lax.optimization_barrier(v.astype(jnp.bfloat16)).astype(jnp.float32)

@jax.custom_vjp
def low_back(v):
    return v

def low_keep(v):
    return (low(v), None)

def low_pass(kept, grad):
    return (grad,)

def back_keep(v):
    return (v, None)

def back_low(kept, grad):
    return (low(grad),)
low.defvjp(low_keep, low_pass)
low_back.defvjp(back_keep, back_low)

def norm_rows(values, weights):
    return values * lax.rsqrt(lax.optimization_barrier(jnp.mean(values * values, axis=-1, keepdims=True)) + EPS) * weights

def angle_tables(positions, widths):
    quarter = HD // 4
    freqs = jnp.exp(jnp.arange(quarter).astype(jnp.float32) * (-math.log(10000.0) / quarter))
    row_pos = (positions // widths).astype(jnp.float32)
    col_pos = (positions % widths).astype(jnp.float32)
    return (row_pos[..., None] * freqs, col_pos[..., None] * freqs)

def rotate(values, row_ang, col_ang):
    quarter = values.shape[-1] // 4
    cos_row = jnp.cos(row_ang)[..., None, :]
    sin_row = jnp.sin(row_ang)[..., None, :]
    cos_col = jnp.cos(col_ang)[..., None, :]
    sin_col = jnp.sin(col_ang)[..., None, :]
    first_a = values[..., :quarter]
    first_b = values[..., quarter:2 * quarter]
    second_a = values[..., 2 * quarter:3 * quarter]
    second_b = values[..., 3 * quarter:]
    return jnp.concatenate([first_a * cos_row - first_b * sin_row, first_a * sin_row + first_b * cos_row, second_a * cos_col - second_b * sin_col, second_a * sin_col + second_b * cos_col], axis=-1)

def reference(tokens, caption, condition, cotangent, qkv_weight, proj_weight, text_weight, ffn_weight, down_weight, ada_weight, norm_gains, head_gains, ada_bias, cross_gate, group_map, grid_width, caption_len):
    highest = lax.Precision.HIGHEST
    score_scale = HD ** (-0.5)
    slot_ids = jnp.arange(N_DP, dtype=jnp.int32)
    padded_map = jnp.concatenate([group_map, jnp.full((GMAX,), -1, jnp.int32)])
    padded_len = jnp.concatenate([caption_len, jnp.ones((GMAX,), jnp.int32)])
    block_live = jnp.stack([padded_map[group_map + offset] == group_map for offset in range(GMAX)], axis=1)
    lengths = jnp.stack([padded_len[group_map + offset] for offset in range(GMAX)], axis=1)
    positions = (slot_ids - group_map)[:, None] * TOK_DP + jnp.arange(TOK_DP, dtype=jnp.int32)[None, :]
    row_ang, col_ang = angle_tables(positions, grid_width[:, None])
    key_slots = jnp.arange(CAP, dtype=jnp.int32)

    def project(values, matrix):
        return jnp.einsum('ntd,de->nte', values, matrix, precision=highest)

    def split_heads(values):
        return values.reshape(values.shape[0], values.shape[1], HEADS, HD)

    def forward(act_in, text_in, cond_in, qkv_mat, proj_mat, text_mat, ffn_mat, down_mat, ada_mat, norm_vec, head_vec, bias_vec, gate_vec):
        cond_low = low(jax.nn.silu(cond_in))
        modulation = low_back(jnp.dot(cond_low, ada_mat, precision=highest) + bias_vec)
        scale_attn, gate_attn, scale_ffn, gate_ffn = [modulation[:, None, piece_index * D:(piece_index + 1) * D] for piece_index in range(4)]
        act_rows = act_in.reshape(N_DP, TOK_DP, D)
        first_in = low(norm_rows(act_rows, norm_vec[0]) * (1.0 + scale_attn))
        query_pre = low_back(project(first_in, qkv_mat[0]))
        key_pre = low_back(project(first_in, qkv_mat[1]))
        value_b = split_heads(low_back(low(project(first_in, qkv_mat[2]))))
        query_b = low(rotate(norm_rows(split_heads(query_pre), head_vec[0].reshape(HEADS, HD)), row_ang, col_ang))
        key_b = low(rotate(norm_rows(split_heads(key_pre), head_vec[1].reshape(HEADS, HD)), row_ang, col_ang))
        text_key_pre = low_back(project(text_in, text_mat[0]))
        text_key = low(norm_rows(split_heads(text_key_pre), head_vec[2].reshape(HEADS, HD)))
        text_value = split_heads(low_back(low(project(text_in, text_mat[1]))))
        key_pad = jnp.concatenate([key_b, jnp.zeros((GMAX, TOK_DP, HEADS, HD), jnp.float32)])
        value_pad = jnp.concatenate([value_b, jnp.zeros((GMAX, TOK_DP, HEADS, HD), jnp.float32)])
        text_key_pad = jnp.concatenate([text_key, jnp.zeros((GMAX, CAP, HEADS, HD), jnp.float32)])
        text_value_pad = jnp.concatenate([text_value, jnp.zeros((GMAX, CAP, HEADS, HD), jnp.float32)])

        def one_slot(inputs):
            query_slot, start, live_row, length_row = inputs
            start = start.astype(jnp.int32)
            keys_win = lax.dynamic_slice_in_dim(key_pad, start, GMAX, 0).reshape(GMAX * TOK_DP, HEADS, HD)
            values_win = lax.dynamic_slice_in_dim(value_pad, start, GMAX, 0).reshape(GMAX * TOK_DP, HEADS, HD)
            self_live = jnp.repeat(live_row, TOK_DP)
            logits = low_back(jnp.einsum('qhe,khe->hqk', query_slot, keys_win, precision=highest) * score_scale)
            logits = jnp.where(self_live[None, None, :], logits, NEG)
            probs = low(jax.nn.softmax(logits, axis=-1))
            out_self = jnp.einsum('hqk,khe->qhe', probs, values_win, precision=highest)
            text_keys_win = lax.dynamic_slice_in_dim(text_key_pad, start, GMAX, 0).reshape(GMAX * CAP, HEADS, HD)
            text_values_win = lax.dynamic_slice_in_dim(text_value_pad, start, GMAX, 0).reshape(GMAX * CAP, HEADS, HD)
            text_live = (live_row[:, None] & (key_slots[None, :] < length_row[:, None])).reshape(GMAX * CAP)
            text_logits = low_back(jnp.einsum('qhe,khe->hqk', query_slot, text_keys_win, precision=highest) * score_scale)
            text_logits = jnp.where(text_live[None, None, :], text_logits, NEG)
            text_probs = low(jax.nn.softmax(text_logits, axis=-1))
            out_text = jnp.einsum('hqk,khe->qhe', text_probs, text_values_win, precision=highest)
            return out_self + jnp.tanh(gate_vec)[None, :, None] * out_text
        attn = lax.map(jax.checkpoint(one_slot), (query_b, group_map, block_live, lengths))
        attn_b = low_back(low(attn)).reshape(N_DP, TOK_DP, D)
        attn_proj = low_back(project(attn_b, proj_mat))
        middle = act_rows + jnp.tanh(gate_attn) * norm_rows(attn_proj, norm_vec[1])
        second_in = low(norm_rows(middle, norm_vec[2]) * (1.0 + scale_ffn))
        gate_pre = low_back(project(second_in, ffn_mat[0]))
        up_pre = low_back(project(second_in, ffn_mat[1]))
        hidden = low(jax.nn.silu(gate_pre) * up_pre)
        ffn_out = low_back(project(hidden, down_mat))
        result = middle + jnp.tanh(gate_ffn) * norm_rows(ffn_out, norm_vec[3])
        return result.reshape(N_DP * TOK_DP, D)
    primals = tuple((array_in.astype(jnp.float32) for array_in in (tokens, caption, condition, qkv_weight, proj_weight, text_weight, ffn_weight, down_weight, ada_weight, norm_gains, head_gains, ada_bias, cross_gate)))
    output, pullback = jax.vjp(forward, *primals)
    grads = pullback(cotangent.astype(jnp.float32))
    weight_scale = 1.0 / math.sqrt(TOKENS)
    cond_scale = 1.0 / math.sqrt(TOK_DP)
    return (output.astype(jnp.bfloat16), grads[0], grads[1], grads[2] * cond_scale, grads[3] * weight_scale, grads[4] * weight_scale, grads[5] * weight_scale, grads[6] * weight_scale, grads[7] * weight_scale, grads[8] * weight_scale, grads[9] * weight_scale, grads[10] * weight_scale, grads[11] * weight_scale, grads[12] * weight_scale)
```

```python
import functools
import math

import jax
import jax.numpy as jnp
from jax import lax
from jax.experimental import pallas as pl
from jax.experimental.pallas import tpu as pltpu
from jax.sharding import PartitionSpec as P

HEADS = 24
HD = 64
PAIR = 2 * HD
EPS = 1e-06
NEG = -1e30
SCALE = HD ** (-0.5)
BF = jnp.bfloat16
F32 = jnp.float32
NN = (((1,), (0,)), ((), ()))
NT = (((1,), (1,)), ((), ()))
TN = (((0,), (0,)), ((), ()))


def mm(left, right, dims):
    return lax.dot_general(left, right, dims, preferred_element_type=F32)


def exact(left, right, dims):
    return lax.dot_general(
        left, right, dims, preferred_element_type=F32, precision=lax.Precision.HIGHEST
    )


def ring_order(count):
    return list(range(0, count, 2)) + list(range(1, count, 2))[::-1]


def ring_pairs(count, step):
    order = ring_order(count)
    return [(order[k], order[(k + step) % count]) for k in range(count)]


def ring_gather(shard):
    count = lax.axis_size("dp")
    half = shard.shape[0] // 2
    first, second = [shard[:half]], [shard[half:]]
    for _ in range(count - 1):
        first.append(lax.ppermute(first[-1], "dp", ring_pairs(count, 1)))
        second.append(lax.ppermute(second[-1], "dp", ring_pairs(count, -1)))
    return first, second


def ring_scatter(first, second):
    count = lax.axis_size("dp")
    sums = []
    for own, step in ((first, 1), (second, -1)):
        total = own(1)
        for k in range(2, count + 1):
            moved = lax.ppermute(total.astype(BF), "dp", ring_pairs(count, step))
            total = moved.astype(F32) + own(k % count).astype(F32)
        sums.append(total)
    return sums


def swap(value, axis, bit):
    count = lax.axis_size(axis)
    return lax.ppermute(value, axis, [(i, i ^ bit) for i in range(count)])


def sum_all(value, axis):
    bit = 1
    while bit < lax.axis_size(axis):
        value = value + swap(value, axis, bit)
        bit *= 2
    return value


def gather_in_order(value, axis, index):
    bit = 1
    while bit < lax.axis_size(axis):
        other = swap(value, axis, bit)
        high = (index & bit) != 0
        value = jnp.concatenate(
            [jnp.where(high, other, value), jnp.where(high, value, other)], axis=0
        )
        bit *= 2
    return value


def rows_from_mp(value):
    far = swap(value, "mp", 2)
    near = swap(value, "mp", 1)
    return jnp.concatenate([value, near, far, swap(far, "mp", 1)], axis=0)


def sum_to_mp(value):
    count = value.shape[0] // 4
    blocks = [value[k * count : (k + 1) * count] for k in range(4)]
    far = blocks[2].astype(F32) + swap(blocks[3].astype(BF), "mp", 1).astype(F32)
    near = blocks[0].astype(F32) + swap(blocks[1].astype(BF), "mp", 1).astype(F32)
    return near + swap(far.astype(BF), "mp", 2).astype(F32)


def shifted(steps, keep=lambda i: True):
    count = lax.axis_size("dp")
    return [(i, i + steps) for i in range(count) if keep(i) and 0 <= i + steps < count]


def even(i):
    return i % 2 == 0


def odd(i):
    return i % 2 == 1


def send_sets(own, is_odd):
    beside = swap(own, "dp", 1)
    low = lax.ppermute(own, "dp", shifted(2))
    high = lax.ppermute(own, "dp", shifted(-2))
    across = swap(jnp.where(is_odd, low, high), "dp", 1)
    third = lax.ppermute(beside, "dp", shifted(-2, even) + shifted(2, odd))
    fourth = lax.ppermute(across, "dp", shifted(2, even) + shifted(-2, odd))
    return [own, beside, low, high, across, third, fourth]


def set_offsets(is_odd):
    sign = jnp.where(is_odd, -1, 1)
    return [0 * sign, sign, 0 * sign - 2, 0 * sign + 2, -sign, 3 * sign, -3 * sign]


def return_sets(grads, is_odd):
    own, beside, low, high, across, third, fourth = [grad.astype(F32) for grad in grads]
    across = across + lax.ppermute(
        fourth.astype(BF), "dp", shifted(-2, even) + shifted(2, odd)
    ).astype(F32)
    beside = beside + lax.ppermute(
        third.astype(BF), "dp", shifted(2, even) + shifted(-2, odd)
    ).astype(F32)
    crossed = swap(across.astype(BF), "dp", 1).astype(F32)
    low = low + jnp.where(is_odd, crossed, 0.0)
    high = high + jnp.where(is_odd, 0.0, crossed)
    return (
        own
        + swap(beside.astype(BF), "dp", 1).astype(F32)
        + lax.ppermute(low.astype(BF), "dp", shifted(-2)).astype(F32)
        + lax.ppermute(high.astype(BF), "dp", shifted(2)).astype(F32)
    )


def norm_rows(values, weights):
    return values * lax.rsqrt(jnp.mean(values * values, axis=-1, keepdims=True) + EPS) * weights


def modulate(values, weights, scales):
    return norm_rows(values, weights) * (1.0 + scales)


def gated_add(branch, weights, gates, resid):
    return resid + jnp.tanh(gates) * norm_rows(branch, weights)


def swiglu(gate_pre, up_pre):
    return jax.nn.silu(gate_pre) * up_pre


def lanes(rows):
    return lax.broadcasted_iota(jnp.int32, (rows, PAIR), 1)


def head_sum(values):
    low = lanes(values.shape[0]) < HD
    first = jnp.sum(jnp.where(low, values, 0.0), axis=-1, keepdims=True)
    second = jnp.sum(jnp.where(low, 0.0, values), axis=-1, keepdims=True)
    return jnp.where(low, first, second)


def partner(values):
    quarter = HD // 4
    first = (lanes(values.shape[0]) % (2 * quarter)) < quarter
    return jnp.where(
        first, pltpu.roll(values, PAIR - quarter, 1), pltpu.roll(values, quarter, 1)
    )


def normed(values):
    return values * lax.rsqrt(head_sum(values * values) / HD + EPS)


def prep_kernel(pre_ref, gains_ref, cos_ref, sin_ref, out_ref):
    width = out_ref.shape[1]
    rows = pre_ref.shape[0]
    cos, sin = cos_ref[...], sin_ref[...]
    for part in range(2):
        for start in range(0, width, PAIR):
            here = pl.ds(part * width + start, PAIR)
            turned = normed(pre_ref[:, here]) * gains_ref[part : part + 1, pl.ds(start, PAIR)]
            if part == 0:
                turned = turned * cos + partner(turned) * sin
                out_ref[pl.ds(0, rows), pl.ds(start, PAIR)] = turned.astype(BF)
            else:
                turned = turned * cos + partner(turned) * sin
                out_ref[pl.ds(rows, rows), pl.ds(start, PAIR)] = turned.astype(BF)
    out_ref[pl.ds(2 * rows, rows), :] = pre_ref[:, pl.ds(2 * width, width)].astype(BF)


def text_prep_kernel(pre_ref, gains_ref, out_ref):
    rows, width = pre_ref.shape[0], out_ref.shape[1]
    for start in range(0, width, PAIR):
        here = pl.ds(start, PAIR)
        value = normed(pre_ref[:, here]) * gains_ref[2:3, here]
        out_ref[pl.ds(0, rows), here] = value.astype(BF)
    out_ref[pl.ds(rows, rows), :] = pre_ref[:, pl.ds(width, width)].astype(BF)


def norm_back(pre, gains, grad):
    ratio = lax.rsqrt(head_sum(pre * pre) / HD + EPS)
    scaled = grad * gains
    grad_pre = ratio * scaled - pre * (ratio * ratio * ratio) * (head_sum(pre * scaled) / HD)
    return grad_pre, jnp.sum(grad * pre * ratio, axis=0, keepdims=True)


def prep_back_kernel(pre_ref, gains_ref, cos_ref, sin_ref, query_ref, set_ref, out_ref, head_ref):
    rows, width = query_ref.shape
    cos, sin = cos_ref[...], sin_ref[...]
    head_ref[...] = jnp.zeros_like(head_ref)
    for part in range(2):
        for start in range(0, width, PAIR):
            here = pl.ds(start, PAIR)
            there = pl.ds(part * width + start, PAIR)
            grad = query_ref[:, here] if part == 0 else set_ref[pl.ds(0, rows), here]
            grad = grad * cos - partner(grad) * sin
            grad_pre, grad_gain = norm_back(pre_ref[:, there], gains_ref[part : part + 1, here], grad)
            out_ref[:, there] = grad_pre.astype(BF)
            head_ref[part : part + 1, here] = grad_gain
    out_ref[:, pl.ds(2 * width, width)] = set_ref[pl.ds(rows, rows), :].astype(BF)


def text_back_kernel(pre_ref, gains_ref, set_ref, out_ref, head_ref):
    rows, width = pre_ref.shape[0], set_ref.shape[1]
    head_ref[...] = jnp.zeros_like(head_ref)
    for start in range(0, width, PAIR):
        here = pl.ds(start, PAIR)
        grad_pre, grad_gain = norm_back(
            pre_ref[:, here], gains_ref[2:3, here], set_ref[pl.ds(0, rows), here]
        )
        out_ref[:, here] = grad_pre.astype(BF)
        head_ref[0:1, here] = grad_gain
    out_ref[:, pl.ds(width, width)] = set_ref[pl.ds(rows, rows), :].astype(BF)


def split_pair(values):
    low = lanes(values.shape[0]) < HD
    zero = jnp.zeros_like(values)
    return jnp.where(low, values, zero), jnp.where(low, zero, values)


def forward_kernel(live_ref, gate_ref, query_ref, bias_ref, *refs):
    count = (len(refs) - 9) // 2
    self_refs, text_refs = refs[:count], refs[count : 2 * count]
    attn_ref, self_ref, text_ref, self_sum_ref, text_sum_ref = refs[2 * count : 2 * count + 5]
    totals = refs[2 * count + 5 :]
    rows = query_ref.shape[0]
    low = lanes(rows) < HD
    for total in totals:
        total[...] = jnp.zeros_like(total)

    for index in range(count):

        @pl.when(live_ref[index] > 0)
        def _(index=index):
            queries = split_pair(query_ref[...] * jnp.asarray(SCALE, BF))
            for slot, source in ((0, self_refs[index]), (1, text_refs[index])):
                depth = source.shape[0] // 2
                keys, values = source[pl.ds(0, depth), :], source[pl.ds(depth, depth), :]
                outs, sums = [], []
                for query in queries:
                    logits = mm(query, keys, NT)
                    if slot:
                        logits = logits + bias_ref[index : index + 1, :]
                    probs = jnp.exp(logits)
                    sums.append(jnp.sum(probs, axis=-1, keepdims=True))
                    outs.append(mm(probs.astype(BF), values, NN))
                totals[slot][...] += jnp.where(low, outs[0], outs[1])
                totals[2 + slot][...] += jnp.where(low, sums[0], sums[1])

    pair = pl.program_id(0)
    gate = jnp.where(low, gate_ref[2 * pair], gate_ref[2 * pair + 1])
    out_self = totals[0][...] / totals[2][...]
    out_text = totals[1][...] / totals[3][...]
    attn_ref[...] = (out_self + gate * out_text).astype(BF)
    self_ref[...] = out_self
    text_ref[...] = out_text
    self_sum_ref[...] = totals[2][...]
    text_sum_ref[...] = totals[3][...]


def backward_kernel(
    live_ref,
    gate_ref,
    query_ref,
    grad_ref,
    self_ref,
    text_ref,
    self_sum_ref,
    text_sum_ref,
    bias_ref,
    *refs,
):
    count = (len(refs) - 3) // 3
    self_refs, text_refs = refs[:count], refs[count : 2 * count]
    set_refs = refs[2 * count : 3 * count]
    query_grad_ref, gate_grad_ref, total = refs[3 * count :]
    rows = query_ref.shape[0]
    low = lanes(rows) < HD
    pair = pl.program_id(0)
    gates = (gate_ref[2 * pair], gate_ref[2 * pair + 1])
    wide = grad_ref[...].astype(F32)
    text_dot = head_sum(wide * text_ref[...])
    gate_grad_ref[...] = jnp.broadcast_to(
        jnp.sum(text_dot, axis=0, keepdims=True), gate_grad_ref.shape
    )
    delta_self = jnp.transpose(head_sum(wide * self_ref[...]))
    delta_text = jnp.transpose(jnp.where(low, gates[0], gates[1]) * text_dot)
    log_self = jnp.transpose(jnp.log(self_sum_ref[...]))
    log_text = jnp.transpose(jnp.log(text_sum_ref[...]))
    total[...] = jnp.zeros_like(total)

    for index in range(count):

        @pl.when(live_ref[index] > 0)
        def _(index=index):
            queries = split_pair(query_ref[...] * jnp.asarray(SCALE, BF))
            grads = split_pair(grad_ref[...])
            start = 0
            for slot, source in ((0, self_refs[index]), (1, text_refs[index])):
                depth = source.shape[0] // 2
                keys, values = source[pl.ds(0, depth), :], source[pl.ds(depth, depth), :]
                grad_query, grad_key, grad_value = [], [], []
                for head in range(2):
                    row = head * HD
                    logs = (log_text if slot else log_self)[row : row + 1, :]
                    delta = (delta_text if slot else delta_self)[row : row + 1, :]
                    logits = mm(keys, queries[head], NT)
                    if slot:
                        logits = logits + bias_ref[:, index : index + 1]
                    probs = jnp.exp(logits - logs)
                    value_part = mm(probs.astype(BF), grads[head], NN)
                    grad_probs = mm(values, grads[head], NT)
                    if slot:
                        value_part = value_part * gates[head]
                        grad_probs = grad_probs * gates[head]
                    grad_logits = (probs * (grad_probs - delta)).astype(BF)
                    grad_value.append(value_part)
                    grad_key.append(mm(grad_logits, queries[head], NN))
                    grad_query.append(mm(grad_logits, keys, TN))
                total[...] += jnp.where(low, grad_query[0], grad_query[1])
                set_refs[index][pl.ds(start, depth), :] = (grad_key[0] + grad_key[1]).astype(BF)
                set_refs[index][pl.ds(start + depth, depth), :] = (
                    grad_value[0] + grad_value[1]
                ).astype(BF)
                start += 2 * depth

        @pl.when(live_ref[index] == 0)
        def _(index=index):
            set_refs[index][...] = jnp.zeros_like(set_refs[index])

    query_grad_ref[...] = total[...] * SCALE


def params(limit=40):
    return pltpu.CompilerParams(vmem_limit_bytes=limit * 2**20)


def whole(kernel, outs, cost, *args):
    shapes = [jax.ShapeDtypeStruct(shape, dtype) for shape, dtype in outs]
    return pl.pallas_call(
        kernel,
        out_shape=shapes if len(shapes) > 1 else shapes[0],
        compiler_params=params(),
        cost_estimate=pl.CostEstimate(flops=cost, bytes_accessed=2 * cost // 10, transcendentals=0),
    )(*args)


def column(rows):
    return pl.BlockSpec((rows, PAIR), lambda pair: (0, pair))


def fixed(shape):
    return pl.BlockSpec(shape, lambda pair: (0, 0))


def attend_forward(live, gates, query, bias, self_sets, text_sets):
    rows, width = query.shape
    smem = pl.BlockSpec(memory_space=pltpu.SMEM)
    keys = self_sets[0].shape[0] // 2 + text_sets[0].shape[0] // 2
    return pl.pallas_call(
        forward_kernel,
        grid=(width // PAIR,),
        in_specs=[smem, smem, column(rows), fixed(bias.shape)]
        + [column(value.shape[0]) for value in self_sets + text_sets],
        out_specs=[column(rows)] * 5,
        out_shape=[jax.ShapeDtypeStruct((rows, width), BF)]
        + [jax.ShapeDtypeStruct((rows, width), F32)] * 4,
        scratch_shapes=[pltpu.VMEM((rows, PAIR), F32)] * 4,
        compiler_params=params(),
        cost_estimate=pl.CostEstimate(
            flops=4 * 4 * rows * keys * width * 4,
            bytes_accessed=20 * rows * width * 4,
            transcendentals=4 * rows * keys * width // HD,
        ),
    )(live, gates, query, bias, *self_sets, *text_sets)


def attend_backward(live, gates, query, grad, saved, bias, self_sets, text_sets):
    rows, width = query.shape
    smem = pl.BlockSpec(memory_space=pltpu.SMEM)
    depth = self_sets[0].shape[0] + text_sets[0].shape[0]
    outs = pl.pallas_call(
        backward_kernel,
        grid=(width // PAIR,),
        in_specs=[smem, smem]
        + [column(rows)] * 6
        + [fixed(bias.shape)]
        + [column(value.shape[0]) for value in self_sets + text_sets],
        out_specs=[column(depth)] * len(self_sets) + [column(rows), column(8)],
        out_shape=[jax.ShapeDtypeStruct((depth, width), BF)] * len(self_sets)
        + [jax.ShapeDtypeStruct((rows, width), F32), jax.ShapeDtypeStruct((8, width), F32)],
        scratch_shapes=[pltpu.VMEM((rows, PAIR), F32)],
        compiler_params=params(),
        cost_estimate=pl.CostEstimate(
            flops=10 * 4 * rows * depth // 2 * width * 4,
            bytes_accessed=40 * rows * width * 4,
            transcendentals=4 * rows * depth // 2 * width // HD,
        ),
    )(live, gates, query, grad, *saved, bias, *self_sets, *text_sets)
    return outs[: len(self_sets)], outs[-2], outs[-1]


def local(
    tokens,
    caption,
    condition,
    cotangent,
    qkv_weight,
    proj_weight,
    text_weight,
    ffn_weight,
    down_weight,
    ada_weight,
    norm_gains,
    head_gains,
    ada_bias,
    cross_gate,
    group_map,
    grid_width,
    caption_len,
):
    dp_count = lax.axis_size("dp")
    mp_count = lax.axis_size("mp")
    dp_index = lax.axis_index("dp")
    mp_index = lax.axis_index("mp")
    row_count, width = tokens.shape
    seq_len = row_count * mp_count
    local_width = qkv_weight.shape[2]
    local_heads = local_width // HD
    text_len, text_dim = caption.shape[1:]
    units = ffn_weight.shape[2]
    shard = qkv_weight.shape[1]
    weight_scale = 1.0 / math.sqrt(seq_len * dp_count)
    is_odd = (dp_index % 2) == 1
    ring_pos = jnp.where(is_odd, dp_count - 1 - dp_index // 2, dp_index // 2)
    order = jnp.asarray(ring_order(dp_count) * 2, jnp.int32)
    ahead = lax.dynamic_slice_in_dim(order, ring_pos, dp_count)
    behind = lax.dynamic_slice_in_dim(order[::-1], dp_count - 1 - ring_pos, dp_count)

    half = shard // 2
    inner = jnp.arange(half, dtype=jnp.int32)
    source = jnp.concatenate(
        [
            (behind[:, None] * shard + inner[None, :]).reshape(-1),
            (ahead[:, None] * shard + half + inner[None, :]).reshape(-1),
        ]
    )
    places = (lax.broadcasted_iota(jnp.int32, (width, width), 0) == source[None, :]).astype(BF)

    qkv_shard = jnp.transpose(qkv_weight, (1, 0, 2)).reshape(shard, 3 * local_width)
    rest_shard = jnp.concatenate(
        [proj_weight.T, jnp.transpose(ffn_weight, (1, 0, 2)).reshape(shard, 2 * units), down_weight.T],
        axis=1,
    )

    cond_low = jax.nn.silu(condition).astype(BF)
    cond_all = gather_in_order(cond_low, "dp", dp_index)
    cond_mine = lax.dynamic_slice_in_dim(cond_all, dp_index * shard, shard, axis=1)
    mod_all = sum_all(mm(cond_mine, ada_weight, NN), "dp")
    bias_part = lax.dynamic_slice_in_dim(ada_bias, mp_index * width, width)
    mod_part = lax.dynamic_slice_in_dim(mod_all, dp_index, 1, axis=0) + bias_part[None, :]
    vectors = jnp.concatenate([gather_in_order(mod_part, "mp", mp_index), norm_gains], axis=0)
    vectors = exact(vectors, places.astype(F32), NN)
    scale_attn, gate_attn, scale_ffn, gate_ffn = [vectors[k] for k in range(4)]
    gains = [vectors[4 + k] for k in range(4)]

    qkv_first, qkv_second = ring_gather(qkv_shard)
    qkv_full = jnp.concatenate(qkv_first + qkv_second, axis=0)

    act_rows = mm(tokens, places, NN)
    first_in, first_pull = jax.vjp(modulate, act_rows, gains[0], scale_attn)
    first_low = rows_from_mp(first_in.astype(BF))
    qkv_pre = mm(first_low, qkv_full, NN)

    text_shard = text_weight.shape[1]
    quarter_rows = text_len // mp_count
    my_rows = lax.dynamic_slice_in_dim(caption[0], mp_index * quarter_rows, quarter_rows, axis=0)
    pieces = []
    for step in range(dp_count):
        piece = lax.dynamic_slice_in_dim(my_rows, ahead[step] * text_shard, text_shard, axis=1)
        if step:
            piece = lax.ppermute(piece, "dp", ring_pairs(dp_count, step))
        pieces.append(piece[None])
    mine = jnp.concatenate(pieces, axis=0)
    far = swap(mine, "mp", 2)
    near = swap(mine, "mp", 1)
    last = swap(far, "mp", 1)
    text_all = jnp.concatenate([mine, near, far, last], axis=1).reshape(
        dp_count * text_len, text_shard
    )
    text_matrix = jnp.transpose(text_weight, (1, 0, 2)).reshape(text_shard, 2 * local_width)
    text_part = mm(text_all, text_matrix, NN).astype(BF).reshape(dp_count, text_len, 2 * local_width)
    text_pre = jnp.concatenate(
        ring_scatter(
            lambda k: text_part[k, :, :local_width],
            lambda k: text_part[(dp_count - k) % dp_count, :, local_width:],
        ),
        axis=1,
    )

    blocks = mp_index ^ jnp.arange(mp_count, dtype=jnp.int32)
    token_ids = (blocks[:, None] * row_count + jnp.arange(row_count, dtype=jnp.int32)).reshape(-1)
    text_ids = (blocks[:, None] * quarter_rows + jnp.arange(quarter_rows, dtype=jnp.int32)).reshape(-1)
    first_slot = group_map[dp_index]
    positions = (dp_index - first_slot) * seq_len + token_ids
    quarter = HD // 4
    lane = jnp.arange(PAIR, dtype=jnp.int32)
    freqs = jnp.exp((lane % quarter).astype(F32) * (-math.log(10000.0) / quarter))
    grid = grid_width[dp_index]
    place = jnp.where((lane % HD < HD // 2)[None, :], (positions // grid)[:, None], (positions % grid)[:, None])
    angles = place.astype(F32) * freqs[None, :]
    cos = jnp.cos(angles)
    sin = jnp.sin(angles) * jnp.where((lane % (2 * quarter)) < quarter, -1.0, 1.0)[None, :]
    local_gains = lax.dynamic_slice_in_dim(head_gains, mp_index * local_width, local_width, axis=1)
    tanh_gate = jnp.tanh(lax.dynamic_slice_in_dim(cross_gate, mp_index * local_heads, local_heads))

    live, biases = [], []
    for offset in set_offsets(is_odd):
        origin = dp_index + offset
        clipped = jnp.clip(origin, 0, dp_count - 1)
        live.append((origin == clipped) & (group_map[clipped] == first_slot))
        biases.append(jnp.where(text_ids < caption_len[clipped], 0.0, NEG))
    live = jnp.stack(live).astype(jnp.int32)
    bias = jnp.stack(biases + biases[:1]).astype(F32)

    prepared = whole(
        prep_kernel,
        [((3 * seq_len, local_width), BF)],
        20 * seq_len * 3 * local_width,
        qkv_pre,
        local_gains,
        cos,
        sin,
    )
    query = prepared[:seq_len]
    self_sets = send_sets(prepared[seq_len:], is_odd)
    text_set = whole(
        text_prep_kernel,
        [((2 * text_len, local_width), BF)],
        20 * text_len * 2 * local_width,
        text_pre,
        local_gains,
    )
    text_sets = send_sets(text_set, is_odd)
    attn_low, *saved = attend_forward(live, tanh_gate, query, bias, self_sets, text_sets)

    rest_first, rest_second = ring_gather(rest_shard)
    rest = rest_first + rest_second
    cuts = (0, local_width, local_width + 2 * units, local_width + 3 * units)
    proj_full, ffn_full, down_full = [
        jnp.concatenate([piece[:, low:high] for piece in rest], axis=0)
        for low, high in zip(cuts[:-1], cuts[1:])
    ]

    attn_rows = sum_to_mp(mm(attn_low, proj_full, NT))
    middle, middle_pull = jax.vjp(gated_add, attn_rows, gains[1], gate_attn, act_rows)
    second_in, second_pull = jax.vjp(modulate, middle, gains[2], scale_ffn)
    second_low = rows_from_mp(second_in.astype(BF))
    ffn_pre = mm(second_low, ffn_full, NN)
    hidden_f, swiglu_pull = jax.vjp(swiglu, ffn_pre[:, :units], ffn_pre[:, units:])
    hidden_low = hidden_f.astype(BF)
    ffn_rows = sum_to_mp(mm(hidden_low, down_full, NT))
    result, result_pull = jax.vjp(gated_add, ffn_rows, gains[3], gate_ffn, middle)
    result = mm(result.astype(BF), places, NT).astype(BF)

    grad_out = mm(cotangent, places, NN)
    grad_ffn_rows, grad_gain_four, grad_gate_ffn, grad_middle_a = result_pull(grad_out)
    grad_ffn_all = rows_from_mp(grad_ffn_rows.astype(BF))
    grad_hidden = mm(grad_ffn_all, down_full, NN)
    grad_gate_pre, grad_up_pre = swiglu_pull(grad_hidden)
    grad_pre_low = jnp.concatenate([grad_gate_pre, grad_up_pre], axis=1).astype(BF)
    grad_second = sum_to_mp(mm(grad_pre_low, ffn_full, NT))
    grad_down = mm(grad_ffn_all, hidden_low, TN).astype(BF)
    grad_ffn = mm(second_low, grad_pre_low, TN).astype(BF)
    grad_middle_b, grad_gain_three, grad_scale_ffn = second_pull(grad_second)
    grad_attn_rows, grad_gain_two, grad_gate_attn, grad_act_a = middle_pull(
        grad_middle_a + grad_middle_b
    )
    grad_attn_all = rows_from_mp(grad_attn_rows.astype(BF))
    grad_attn_low = mm(grad_attn_all, proj_full, NN).astype(BF)
    grad_proj = mm(grad_attn_all, attn_low, TN).astype(BF)

    def chunk(values, k):
        return values[k * half : (k + 1) * half]

    def scatter(values):
        def first(k):
            return jnp.concatenate([chunk(value, k) for value in values], axis=1)

        def second(k):
            return first(dp_count + k)

        return jnp.concatenate(ring_scatter(first, second), axis=0) * weight_scale

    ffn_sum = scatter([grad_ffn, grad_down])

    grad_sets, grad_query, gate_dots = attend_backward(
        live, tanh_gate, query, grad_attn_low, saved, bias.T, self_sets, text_sets
    )
    own_set = return_sets(grad_sets, is_odd)
    grad_qkv_low, head_two = whole(
        prep_back_kernel,
        [((seq_len, 3 * local_width), BF), ((8, local_width), F32)],
        20 * seq_len * 3 * local_width,
        qkv_pre,
        local_gains,
        cos,
        sin,
        grad_query,
        own_set[: 2 * seq_len],
    )
    grad_text_low, head_one = whole(
        text_back_kernel,
        [((text_len, 2 * local_width), BF), ((8, local_width), F32)],
        20 * text_len * 2 * local_width,
        text_pre,
        local_gains,
        own_set[2 * seq_len :],
    )
    grad_qkv = mm(first_low, grad_qkv_low, TN).astype(BF)
    attn_sum = scatter([grad_qkv, grad_proj])
    grad_first = sum_to_mp(mm(grad_qkv_low, qkv_full, NT))
    grad_act_b, grad_gain_one, grad_scale_attn = first_pull(grad_first)
    grad_tokens = exact(grad_act_a + grad_act_b, places.astype(F32), NT)

    key_rows, value_rows = [grad_text_low[:, :local_width]], [grad_text_low[:, local_width:]]
    for _ in range(dp_count - 1):
        key_rows.append(lax.ppermute(key_rows[-1], "dp", ring_pairs(dp_count, 1)))
        value_rows.append(lax.ppermute(value_rows[-1], "dp", ring_pairs(dp_count, -1)))
    value_rows = value_rows[:1] + value_rows[1:][::-1]
    text_rows = jnp.concatenate(
        [jnp.concatenate(key_rows, axis=0), jnp.concatenate(value_rows, axis=0)], axis=1
    )
    grad_text = mm(text_all, text_rows, TN) * weight_scale
    caption_part = mm(text_rows, text_matrix, NT).reshape(
        dp_count, mp_count, quarter_rows, text_shard
    )
    caption_part = jnp.transpose(caption_part, (1, 0, 2, 3)).reshape(
        mp_count * dp_count * quarter_rows, text_shard
    )
    caption_mine = sum_to_mp(caption_part).astype(BF).reshape(dp_count, quarter_rows, text_shard)
    columns = jnp.zeros((quarter_rows, text_dim), BF)
    for step in range(dp_count):
        piece = caption_mine[step]
        if step:
            piece = lax.ppermute(piece, "dp", ring_pairs(dp_count, -step))
        columns = lax.dynamic_update_slice_in_dim(columns, piece, ahead[step] * text_shard, 1)
    block = text_dim // mp_count
    grad_caption = jnp.zeros((text_len, block), F32)
    for bit in range(mp_count):
        other = mp_index ^ bit
        piece = lax.dynamic_slice_in_dim(columns, other * block, block, axis=1)
        if bit:
            piece = swap(piece, "mp", bit)
        grad_caption = lax.dynamic_update_slice_in_dim(
            grad_caption, piece.astype(F32), other * quarter_rows, 0
        )

    row_grads = jnp.stack(
        [
            grad_gain_one,
            grad_gain_two,
            grad_gain_three,
            grad_gain_four,
            grad_scale_attn,
            grad_gate_attn,
            grad_scale_ffn,
            grad_gate_ffn,
        ]
    )
    row_grads = exact(row_grads, places.astype(F32), NT)
    mod_sum = sum_all(row_grads[4:], "mp")
    grad_mod_low = lax.dynamic_slice_in_dim(mod_sum, mp_index, 1, axis=0).astype(BF)
    grad_mod_all = gather_in_order(grad_mod_low, "dp", dp_index)
    grad_ada = mm(cond_mine, grad_mod_all, TN) * weight_scale
    cond_part = mm(grad_mod_all, ada_weight, NT)
    zeros = functools.partial(jnp.zeros, dtype=F32)
    cond_rows = lax.dynamic_update_slice_in_dim(
        zeros((dp_count, width)), cond_part, dp_index * shard, 1
    )
    head_local = jnp.concatenate([head_two[:2], head_one[:1]], axis=0)
    head_rows = lax.dynamic_update_slice_in_dim(
        zeros((3, width)), head_local, mp_index * local_width, 1
    )
    bias_rows = jnp.where(
        jnp.arange(mp_count)[:, None] == mp_index, grad_mod_low.astype(F32), 0.0
    )
    gate_local = gate_dots[0].reshape(local_heads, HD)[:, 0] * (1.0 - tanh_gate * tanh_gate)
    gate_row = lax.dynamic_update_slice_in_dim(
        zeros((width,)), gate_local, mp_index * local_heads, 0
    )
    small = jnp.concatenate([row_grads[:4], head_rows, bias_rows, gate_row[None], cond_rows], axis=0)
    small = sum_all(sum_all(small, "mp"), "dp")
    cond_width = width // mp_count
    cond_sum = lax.dynamic_slice(small[12:], (dp_index, mp_index * cond_width), (1, cond_width))
    cond_cols = lax.dynamic_slice_in_dim(condition, mp_index * cond_width, cond_width, axis=1)
    silu_vals, silu_pull = jax.vjp(jax.nn.silu, cond_cols)
    grad_condition = silu_pull(cond_sum)[0] * (1.0 / math.sqrt(seq_len))
    scaled = small[:12] * weight_scale

    def parted(values, parts):
        return jnp.transpose(values.reshape(values.shape[0], parts, -1), (1, 0, 2))

    return (
        result,
        grad_tokens,
        grad_caption[None],
        grad_condition,
        parted(attn_sum[:, : 3 * local_width], 3),
        attn_sum[:, 3 * local_width :].T,
        parted(grad_text, 2),
        parted(ffn_sum[:, : 2 * units], 2),
        ffn_sum[:, 2 * units :].T,
        grad_ada,
        scaled[:4],
        scaled[4:7],
        scaled[7:11].reshape(-1),
        scaled[11, :HEADS],
    )


def solution(mesh):
    return jax.shard_map(
        local,
        mesh=mesh,
        in_specs=(
            P(("dp", "mp"), None),
            P("dp", None, None),
            P("dp", None),
            P(("dp", "mp"), None),
            P(None, "dp", "mp"),
            P("mp", "dp"),
            P(None, "dp", "mp"),
            P(None, "dp", "mp"),
            P("mp", "dp"),
            P("dp", "mp"),
            P(),
            P(),
            P(),
            P(),
            P(),
            P(),
            P(),
        ),
        out_specs=(
            P(("dp", "mp"), None),
            P(("dp", "mp"), None),
            P("dp", None, "mp"),
            P("dp", "mp"),
            P(None, "dp", "mp"),
            P("mp", "dp"),
            P(None, "dp", "mp"),
            P(None, "dp", "mp"),
            P("mp", "dp"),
            P("dp", "mp"),
            P(),
            P(),
            P(),
            P(),
        ),
        check_vma=False,
    )
```

```python
import functools
import math

import jax
import jax.numpy as jnp
from jax import lax
from jax.experimental import pallas as pl
from jax.experimental.pallas import tpu as pltpu
from jax.sharding import PartitionSpec as P

HEADS = 24
HD = 64
PAIR = 2 * HD
NEAR_PARTS = 3
EPS = 1e-06
NEG = -1e30
SCALE = HD ** (-0.5)
BF = jnp.bfloat16
F32 = jnp.float32
NN = (((1,), (0,)), ((), ()))
NT = (((1,), (1,)), ((), ()))
TN = (((0,), (0,)), ((), ()))


def mm(left, right, dims):
    return lax.dot_general(left, right, dims, preferred_element_type=F32)


def swap(value, axis, bit):
    count = lax.axis_size(axis)
    return lax.ppermute(value, axis, [(i, i ^ bit) for i in range(count)])


def all_bits(count):
    return [1 << k for k in range(count.bit_length() - 1)]


def after(value, *others):
    return lax.optimization_barrier((value,) + others)[0]


class Chain:
    def __init__(self, steps):
        self.steps, self.result = steps, None
        self.advance(None)

    def advance(self, arrived):
        try:
            self.wanted = self.steps.send(arrived)
        except StopIteration as end:
            self.wanted, self.result = None, end.value


class Links:
    def __init__(self):
        self.last = ()

    def stage(self, *chains, work=None):
        active = [chain for chain in chains if chain.wanted is not None]
        wanted = [item for chain in active for item in chain.wanted]
        values = [value for value, _, _ in wanted]
        if self.last and values:
            values = lax.optimization_barrier(tuple(values) + self.last)[: len(values)]
        moved = [
            lax.ppermute(value, axis, pairs) for value, (_, axis, pairs) in zip(values, wanted)
        ]
        made = work(lambda value: after(value, *self.last)) if work else ()
        moved, made = lax.optimization_barrier((moved, made))
        self.last = tuple(moved[:1]) or tuple(jax.tree.leaves(made)[:1])
        for chain in active:
            count = len(chain.wanted)
            chain.advance(moved[:count])
            moved = moved[count:]
        return made

    def finish_only(self, chain, others):
        while chain.wanted is not None:
            self.stage(chain, *others)

    def finish(self, *chains):
        while any(chain.wanted is not None for chain in chains):
            self.stage(*chains)


def swap_pairs(axis, bit):
    return [(i, i ^ bit) for i in range(lax.axis_size(axis))]


def crossed_bits():
    bits = all_bits(lax.axis_size("dp"))
    return bits, bits[1::-1] + bits[2:]


def bit_axis(bits, bit):
    return sum(other > bit for other in bits)


def in_order(high, own, other, axis):
    return jnp.stack([jnp.where(high, other, own), jnp.where(high, own, other)], axis=axis)


def halves(high, value, axis):
    zero, one = [lax.index_in_dim(value, k, axis, keepdims=False) for k in range(2)]
    return jnp.where(high, zero, one), jnp.where(high, one, zero)


def gather_blocks(pair, index):
    orders = [bits[::-1] for bits in crossed_bits()]
    values, done = list(pair), ([], [])
    for bits in zip(*orders):
        moved = yield [(value, "dp", swap_pairs("dp", bit)) for value, bit in zip(values, bits)]
        for side, bit in enumerate(bits):
            axis = bit_axis(done[side], bit)
            values[side] = in_order((index & bit) != 0, values[side], moved[side], axis)
            done[side].append(bit)
    return [value.reshape((-1,) + own.shape[1:]) for value, own in zip(values, pair)]


def scatter_blocks(pair, index):
    orders = crossed_bits()
    left = [list(bits) for bits in orders]
    values = [value.reshape((2,) * len(orders[0]) + value.shape[1:]) for value in pair]
    for bits in zip(*orders):
        sent, kept = [], []
        for side, bit in enumerate(bits):
            parts = halves((index & bit) != 0, values[side], bit_axis(left[side], bit))
            sent.append((parts[0].astype(BF), "dp", swap_pairs("dp", bit)))
            kept.append(parts[1])
            left[side].remove(bit)
        moved = yield sent
        values = [plus(own, other) for own, other in zip(kept, moved)]
    return values


def exchange_blocks(value, index):
    count = value.shape[0]
    bits, left, done = all_bits(count), all_bits(count), []
    shape = value.shape[1:]
    value = value.reshape((2,) * len(bits) + shape)
    for bit in bits:
        high = (index & bit) != 0
        sent, kept = halves(high, value, bit_axis(left, bit))
        left.remove(bit)
        (moved,) = yield [(sent, "dp", swap_pairs("dp", bit))]
        value = in_order(high, kept, moved, len(left) + bit_axis(done, bit))
        done.append(bit)
    return value.reshape((count,) + shape)


def plus(*values):
    return sum(value.astype(F32) for value in values)


def sum_all(value, axis):
    bit = 1
    while bit < lax.axis_size(axis):
        value = value + swap(value, axis, bit)
        bit *= 2
    return value


def gather_in_order(value, axis, index):
    bit = 1
    while bit < lax.axis_size(axis):
        other = swap(value, axis, bit)
        high = (index & bit) != 0
        value = jnp.concatenate(
            [jnp.where(high, other, value), jnp.where(high, value, other)], axis=0
        )
        bit *= 2
    return value


def rows_from_mp(value, axis=0):
    far = swap(value, "mp", 2)
    near = swap(value, "mp", 1)
    return jnp.concatenate([value, near, far, swap(far, "mp", 1)], axis=axis)


def slots_from_mp(value):
    far, near = yield [(value, "mp", swap_pairs("mp", bit)) for bit in (2, 1)]
    (last,) = yield [(far, "mp", swap_pairs("mp", 1))]
    return [value, near, far, last]


def sum_to_mp(value):
    count = value.shape[0] // 4
    blocks = [value[k * count : (k + 1) * count] for k in range(4)]
    far = blocks[2].astype(F32) + swap(blocks[3].astype(BF), "mp", 1).astype(F32)
    near = blocks[0].astype(F32) + swap(blocks[1].astype(BF), "mp", 1).astype(F32)
    return near + swap(far.astype(BF), "mp", 2).astype(F32)


def shifted(steps, keep=lambda i: True):
    count = lax.axis_size("dp")
    return [(i, i + steps) for i in range(count) if keep(i) and 0 <= i + steps < count]


def even(i):
    return i % 2 == 0


def odd(i):
    return i % 2 == 1


def out_pairs():
    return shifted(-2, even) + shifted(2, odd)


def back_pairs():
    return shifted(2, even) + shifted(-2, odd)


def send_sets(own, is_odd):
    beside, low, high = yield [
        (own, "dp", swap_pairs("dp", 1)),
        (own, "dp", shifted(2)),
        (own, "dp", shifted(-2)),
    ]
    across, third = yield [
        (jnp.where(is_odd, low, high), "dp", swap_pairs("dp", 1)),
        (beside, "dp", out_pairs()),
    ]
    (fourth,) = yield [(across, "dp", back_pairs())]
    return [own, beside, low, high, across, third, fourth]


def set_offsets(is_odd):
    return jnp.where(
        is_odd, jnp.asarray([0, -1, -2, 2, 1, -3, 3]), jnp.asarray([0, 1, -2, 2, -1, 3, -3])
    )


def return_sets(grads, is_odd):
    own, beside, low, high, across, third, fourth = grads
    (fourth,) = yield [(fourth, "dp", out_pairs())]
    across, third = yield [
        (plus(across, fourth).astype(BF), "dp", swap_pairs("dp", 1)),
        (third, "dp", back_pairs()),
    ]
    low = plus(low, jnp.where(is_odd, across, 0)).astype(BF)
    high = plus(high, jnp.where(is_odd, 0, across)).astype(BF)
    beside, low, high = yield [
        (plus(beside, third).astype(BF), "dp", swap_pairs("dp", 1)),
        (low, "dp", shifted(-2)),
        (high, "dp", shifted(2)),
    ]
    return plus(own, beside, low, high)


def norm_rows(values, weights):
    return values * lax.rsqrt(jnp.mean(values * values, axis=-1, keepdims=True) + EPS) * weights


def modulate(values, weights, scales):
    return norm_rows(values, weights) * (1.0 + scales)


def gated_add(branch, weights, gates, resid):
    return resid + jnp.tanh(gates) * norm_rows(branch, weights)


def swiglu(gate_pre, up_pre):
    return jax.nn.silu(gate_pre) * up_pre


def lanes(rows):
    return lax.broadcasted_iota(jnp.int32, (rows, PAIR), 1)


def head_sum(values):
    low = lanes(values.shape[0]) < HD
    first = jnp.sum(jnp.where(low, values, 0.0), axis=-1, keepdims=True)
    second = jnp.sum(jnp.where(low, 0.0, values), axis=-1, keepdims=True)
    return jnp.where(low, first, second)


def partner(values):
    quarter = HD // 4
    first = (lanes(values.shape[0]) % (2 * quarter)) < quarter
    return jnp.where(
        first, pltpu.roll(values, PAIR - quarter, 1), pltpu.roll(values, quarter, 1)
    )


def normed(values):
    return values * lax.rsqrt(head_sum(values * values) / HD + EPS)


def prep_kernel(pre_ref, gains_ref, cos_ref, sin_ref, out_ref):
    width = out_ref.shape[1]
    rows = pre_ref.shape[0]
    cos, sin = cos_ref[...], sin_ref[...]
    for part in range(2):
        for start in range(0, width, PAIR):
            here = pl.ds(part * width + start, PAIR)
            turned = normed(pre_ref[:, here]) * gains_ref[part : part + 1, pl.ds(start, PAIR)]
            if part == 0:
                turned = turned * cos + partner(turned) * sin
                out_ref[pl.ds(0, rows), pl.ds(start, PAIR)] = turned.astype(BF)
            else:
                turned = turned * cos + partner(turned) * sin
                out_ref[pl.ds(rows, rows), pl.ds(start, PAIR)] = turned.astype(BF)
    out_ref[pl.ds(2 * rows, rows), :] = pre_ref[:, pl.ds(2 * width, width)].astype(BF)


def near_prep_kernel(gains_ref, cos_ref, sin_ref, *refs):
    *pre_refs, out_ref = refs
    rows, width = pre_refs[0].shape[0], out_ref.shape[1]
    depth = rows * len(pre_refs)
    for slot, pre_ref in enumerate(pre_refs):
        there = pl.ds(slot * rows, rows)
        cos, sin = cos_ref[there, :], sin_ref[there, :]
        for start in range(0, width, PAIR):
            here = pl.ds(start, PAIR)
            turned = normed(pre_ref[:, here]) * gains_ref[1:2, here]
            turned = turned * cos + partner(turned) * sin
            out_ref[there, here] = turned.astype(BF)
        out_ref[pl.ds(depth + slot * rows, rows), :] = pre_ref[:, pl.ds(width, width)].astype(BF)


def text_prep_kernel(pre_ref, gains_ref, out_ref):
    rows, width = pre_ref.shape[0], out_ref.shape[1]
    for start in range(0, width, PAIR):
        here = pl.ds(start, PAIR)
        value = normed(pre_ref[:, here]) * gains_ref[2:3, here]
        out_ref[pl.ds(0, rows), here] = value.astype(BF)
    out_ref[pl.ds(rows, rows), :] = pre_ref[:, pl.ds(width, width)].astype(BF)


def norm_back(pre, gains, grad):
    ratio = lax.rsqrt(head_sum(pre * pre) / HD + EPS)
    scaled = grad * gains
    grad_pre = ratio * scaled - pre * (ratio * ratio * ratio) * (head_sum(pre * scaled) / HD)
    return grad_pre, jnp.sum(grad * pre * ratio, axis=0, keepdims=True)


def query_back_kernel(pre_ref, gains_ref, cos_ref, sin_ref, self_ref, text_ref, out_ref, head_ref):
    cos, sin = cos_ref[...], sin_ref[...]
    head_ref[...] = jnp.zeros_like(head_ref)
    for start in range(0, out_ref.shape[1], PAIR):
        here = pl.ds(start, PAIR)
        grad = self_ref[:, here] + text_ref[:, here]
        grad = grad * cos - partner(grad) * sin
        grad_pre, grad_gain = norm_back(pre_ref[:, here], gains_ref[0:1, here], grad)
        out_ref[:, here] = grad_pre.astype(BF)
        head_ref[0:1, here] = grad_gain


def key_back_kernel(pre_ref, gains_ref, cos_ref, sin_ref, set_ref, out_ref, head_ref):
    rows, width = pre_ref.shape[0], set_ref.shape[1]
    cos, sin = cos_ref[...], sin_ref[...]
    head_ref[...] = jnp.zeros_like(head_ref)
    for start in range(0, width, PAIR):
        here = pl.ds(start, PAIR)
        grad = set_ref[pl.ds(0, rows), here]
        grad = grad * cos - partner(grad) * sin
        grad_pre, grad_gain = norm_back(
            pre_ref[:, pl.ds(width + start, PAIR)], gains_ref[1:2, here], grad
        )
        out_ref[:, here] = grad_pre.astype(BF)
        head_ref[0:1, here] = grad_gain
    out_ref[:, pl.ds(width, width)] = set_ref[pl.ds(rows, rows), :].astype(BF)


def text_back_kernel(pre_ref, gains_ref, set_ref, out_ref, head_ref):
    rows, width = pre_ref.shape[0], set_ref.shape[1]
    head_ref[...] = jnp.zeros_like(head_ref)
    for start in range(0, width, PAIR):
        here = pl.ds(start, PAIR)
        grad_pre, grad_gain = norm_back(
            pre_ref[:, here], gains_ref[2:3, here], set_ref[pl.ds(0, rows), here]
        )
        out_ref[:, here] = grad_pre.astype(BF)
        head_ref[0:1, here] = grad_gain
    out_ref[:, pl.ds(width, width)] = set_ref[pl.ds(rows, rows), :].astype(BF)


def split_pair(values):
    low = lanes(values.shape[0]) < HD
    zero = jnp.zeros_like(values)
    return jnp.where(low, values, zero), jnp.where(low, zero, values)


def forward_sums(live_ref, query_ref, set_refs, bias_ref, total, weight):
    low = lanes(query_ref.shape[0]) < HD
    total[...] = jnp.zeros_like(total)
    weight[...] = jnp.zeros_like(weight)
    for index, source in enumerate(set_refs):

        @pl.when(live_ref[index] > 0)
        def _(index=index, source=source):
            depth = source.shape[0] // 2
            keys, values = source[pl.ds(0, depth), :], source[pl.ds(depth, depth), :]
            outs, sums = [], []
            for query in split_pair(query_ref[...] * jnp.asarray(SCALE, BF)):
                logits = mm(query, keys, NT)
                if bias_ref is not None:
                    logits = logits + bias_ref[index : index + 1, :]
                probs = jnp.exp(logits)
                sums.append(jnp.sum(probs, axis=-1, keepdims=True))
                outs.append(mm(probs.astype(BF), values, NN))
            total[...] += jnp.where(low, outs[0], outs[1])
            weight[...] += jnp.where(low, sums[0], sums[1])


def views(own_ref, near_refs):
    depth = own_ref.shape[0]
    return [own_ref] + [
        near_ref.at[pl.ds(start, depth), :]
        for near_ref in near_refs
        for start in range(0, near_ref.shape[0], depth)
    ]


def self_forward_kernel(live_ref, query_ref, own_ref, *refs):
    *near_refs, out_ref, log_ref, total, weight = refs
    set_refs = views(own_ref, near_refs)
    forward_sums(live_ref, query_ref, set_refs, None, total, weight)
    out_ref[...] = total[...] / weight[...]
    log_ref[...] = jnp.log(weight[...])


def text_forward_kernel(live_ref, gate_ref, query_ref, self_ref, bias_ref, *refs):
    *set_refs, attn_ref, out_ref, log_ref, total, weight = refs
    forward_sums(live_ref, query_ref, set_refs, bias_ref, total, weight)
    low = lanes(query_ref.shape[0]) < HD
    pair = pl.program_id(0)
    gate = jnp.where(low, gate_ref[2 * pair], gate_ref[2 * pair + 1])
    out = total[...] / weight[...]
    attn_ref[...] = (self_ref[...] + gate * out).astype(BF)
    out_ref[...] = out
    log_ref[...] = jnp.log(weight[...])


def backward_sums(live_ref, query_ref, grad_ref, log_ref, delta, bias_ref, gates, refs, total):
    count = len(refs) // 2
    low = lanes(query_ref.shape[0]) < HD
    logs_all, delta_all = jnp.transpose(log_ref[...]), jnp.transpose(delta)
    total[...] = jnp.zeros_like(total)
    for index, (source, out_ref) in enumerate(zip(refs[:count], refs[count:])):

        @pl.when(live_ref[index] > 0)
        def _(index=index, source=source, out_ref=out_ref):
            queries = split_pair(query_ref[...] * jnp.asarray(SCALE, BF))
            grads = split_pair(grad_ref[...])
            depth = source.shape[0] // 2
            keys, values = source[pl.ds(0, depth), :], source[pl.ds(depth, depth), :]
            grad_query, grad_key, grad_value = [], [], []
            for head in range(2):
                row = head * HD
                logits = mm(keys, queries[head], NT)
                if bias_ref is not None:
                    logits = logits + bias_ref[:, index : index + 1]
                probs = jnp.exp(logits - logs_all[row : row + 1, :])
                value_part = mm(probs.astype(BF), grads[head], NN)
                grad_probs = mm(values, grads[head], NT)
                if gates is not None:
                    value_part = value_part * gates[head]
                    grad_probs = grad_probs * gates[head]
                grad_logits = (probs * (grad_probs - delta_all[row : row + 1, :])).astype(BF)
                grad_value.append(value_part)
                grad_key.append(mm(grad_logits, queries[head], NN))
                grad_query.append(mm(grad_logits, keys, TN))
            total[...] += jnp.where(low, grad_query[0], grad_query[1])
            out_ref[pl.ds(0, depth), :] = (grad_key[0] + grad_key[1]).astype(BF)
            out_ref[pl.ds(depth, depth), :] = (grad_value[0] + grad_value[1]).astype(BF)

        @pl.when(live_ref[index] == 0)
        def _(out_ref=out_ref):
            out_ref[...] = jnp.zeros_like(out_ref)


def self_backward_kernel(
    live_ref, query_ref, grad_ref, out_ref, log_ref, own_ref, *refs
):
    near_refs, grad_refs = refs[:NEAR_PARTS], list(refs[NEAR_PARTS:-2])
    query_grad_ref, total = refs[-2:]
    set_refs = views(own_ref, near_refs) + grad_refs
    delta = head_sum(grad_ref[...].astype(F32) * out_ref[...])
    backward_sums(live_ref, query_ref, grad_ref, log_ref, delta, None, None, set_refs, total)
    query_grad_ref[...] = total[...] * SCALE


def text_backward_kernel(
    live_ref, gate_ref, query_ref, grad_ref, out_ref, log_ref, bias_ref, *refs
):
    *set_refs, query_grad_ref, gate_grad_ref, total = refs
    low = lanes(query_ref.shape[0]) < HD
    pair = pl.program_id(0)
    gates = (gate_ref[2 * pair], gate_ref[2 * pair + 1])
    dots = head_sum(grad_ref[...].astype(F32) * out_ref[...])
    gate_grad_ref[...] = jnp.broadcast_to(jnp.sum(dots, axis=0, keepdims=True), gate_grad_ref.shape)
    delta = jnp.where(low, gates[0], gates[1]) * dots
    backward_sums(live_ref, query_ref, grad_ref, log_ref, delta, bias_ref, gates, set_refs, total)
    query_grad_ref[...] = total[...] * SCALE


def params(limit=40):
    return pltpu.CompilerParams(vmem_limit_bytes=limit * 2**20)


def whole(kernel, outs, cost, *args):
    shapes = [jax.ShapeDtypeStruct(shape, dtype) for shape, dtype in outs]
    return pl.pallas_call(
        kernel,
        out_shape=shapes if len(shapes) > 1 else shapes[0],
        compiler_params=params(),
        cost_estimate=pl.CostEstimate(flops=cost, bytes_accessed=2 * cost // 10, transcendentals=0),
    )(*args)


def column(rows):
    return pl.BlockSpec((rows, PAIR), lambda pair: (0, pair))


def fixed(shape):
    return pl.BlockSpec(shape, lambda pair: (0, 0))


def prepare_near(pre, gains, cos, sin, sets):
    rows, width = pre[0].shape[0] // sets, gains.shape[1]
    depth = rows * len(pre)

    def block(count, columns):
        return pl.BlockSpec((count, columns), lambda k: (k, 0))

    return pl.pallas_call(
        near_prep_kernel,
        grid=(sets,),
        in_specs=[pl.BlockSpec(gains.shape, lambda k: (0, 0))]
        + [block(depth, PAIR)] * 2
        + [block(rows, 2 * width)] * len(pre),
        out_specs=block(2 * depth, width),
        out_shape=jax.ShapeDtypeStruct((sets * 2 * depth, width), BF),
        compiler_params=params(),
        cost_estimate=pl.CostEstimate(
            flops=40 * sets * depth * width,
            bytes_accessed=12 * sets * depth * width,
            transcendentals=0,
        ),
    )(gains, cos, sin, *pre)


def attend(kernel, scalars, columns, bias, sets, outs, passes, scratch, limit=56):
    rows, width = columns[0].shape
    keys = sets[0].shape[0] // 2
    smem = pl.BlockSpec(memory_space=pltpu.SMEM)
    return pl.pallas_call(
        kernel,
        grid=(width // PAIR,),
        in_specs=[smem] * len(scalars)
        + [column(value.shape[0]) for value in columns]
        + [fixed(value.shape) for value in bias]
        + [column(value.shape[0]) for value in sets],
        out_specs=[column(depth) for depth, _ in outs],
        out_shape=[jax.ShapeDtypeStruct((depth, width), dtype) for depth, dtype in outs],
        scratch_shapes=[pltpu.VMEM((rows, PAIR), F32)] * scratch,
        compiler_params=params(limit),
        cost_estimate=pl.CostEstimate(
            flops=passes * 16 * rows * keys * width,
            bytes_accessed=40 * rows * width,
            transcendentals=4 * rows * keys * width // HD,
        ),
    )(*scalars, *columns, *bias, *sets)


def local(
    tokens,
    caption,
    condition,
    cotangent,
    qkv_weight,
    proj_weight,
    text_weight,
    ffn_weight,
    down_weight,
    ada_weight,
    norm_gains,
    head_gains,
    ada_bias,
    cross_gate,
    group_map,
    grid_width,
    caption_len,
):
    dp_count = lax.axis_size("dp")
    mp_count = lax.axis_size("mp")
    dp_index = lax.axis_index("dp")
    mp_index = lax.axis_index("mp")
    row_count, width = tokens.shape
    seq_len = row_count * mp_count
    local_width = qkv_weight.shape[2]
    local_heads = local_width // HD
    text_len, text_dim = caption.shape[1:]
    units = ffn_weight.shape[2]
    shard = qkv_weight.shape[1]
    weight_scale = 1.0 / math.sqrt(seq_len * dp_count)
    is_odd = (dp_index % 2) == 1
    links = Links()

    qkv_shard = jnp.transpose(qkv_weight, (1, 0, 2)).reshape(shard, 3 * local_width)
    rest_shard = jnp.concatenate(
        [proj_weight.T, jnp.transpose(ffn_weight, (1, 0, 2)).reshape(shard, 2 * units), down_weight.T],
        axis=1,
    )
    qkv_full = lax.all_gather(qkv_shard, "dp", axis=0, tiled=True)
    rest = lax.all_gather(rest_shard, "dp", axis=0, tiled=True)
    cuts = (0, local_width, local_width + 2 * units, local_width + 3 * units)
    proj_full, ffn_full, down_full = [rest[:, low:high] for low, high in zip(cuts[:-1], cuts[1:])]

    text_shard = text_weight.shape[1]
    quarter_rows = text_len // mp_count
    my_rows = lax.dynamic_slice_in_dim(caption[0], mp_index * quarter_rows, quarter_rows, axis=0)
    text_matrix = jnp.transpose(text_weight, (1, 0, 2)).reshape(text_shard, 2 * local_width)
    my_rows = jnp.transpose(my_rows.reshape(quarter_rows, dp_count, text_shard), (1, 0, 2))

    def modulate_all():
        value = jax.nn.silu(condition).astype(BF)
        for bit in all_bits(dp_count):
            (other,) = yield [(value, "dp", swap_pairs("dp", bit))]
            value = in_order((dp_index & bit) != 0, value, other, 0).reshape(2 * bit, width)
        cond_mine = lax.dynamic_slice_in_dim(value, dp_index * shard, shard, axis=1)
        value = mm(cond_mine, ada_weight, NN)
        for bit in all_bits(dp_count):
            (other,) = yield [(value, "dp", swap_pairs("dp", bit))]
            value = value + other
        bias_part = lax.dynamic_slice_in_dim(ada_bias, mp_index * width, width)
        value = (value + bias_part[None, :])[None]
        for bit in all_bits(mp_count):
            (other,) = yield [(value, "mp", swap_pairs("mp", bit))]
            value = in_order((mp_index & bit) != 0, value, other, 0).reshape(2 * bit, dp_count, width)
        return cond_mine, value

    def caption_features():
        value = yield from exchange_blocks(my_rows, dp_index)
        far, near = yield [(value, "mp", swap_pairs("mp", bit)) for bit in (2, 1)]
        (last,) = yield [(far, "mp", swap_pairs("mp", 1))]
        return jnp.concatenate([value, near, far, last], axis=1)

    mod_chain, caption_chain = Chain(modulate_all()), Chain(caption_features())
    token_chain = Chain(send_sets(tokens, is_odd))
    links.finish(mod_chain, caption_chain, token_chain)
    cond_mine, modulation = mod_chain.result
    text_all = caption_chain.result.reshape(dp_count * text_len, text_shard)

    origins = dp_index + set_offsets(is_odd)
    chosen = jnp.arange(dp_count)[None, :] == origins[:, None]

    def looked_up(table):
        return jnp.sum(jnp.where(chosen, table[None, :], 0), axis=1)

    inside = (origins >= 0) & (origins < dp_count)
    first_slot = jnp.sum(jnp.where(jnp.arange(dp_count) == dp_index, group_map, 0))
    grid = jnp.sum(jnp.where(jnp.arange(dp_count) == dp_index, grid_width, 0))
    live = (inside & (looked_up(group_map) == first_slot)).astype(jnp.int32)
    lengths = looked_up(caption_len)

    near_scales = jnp.sum(
        jnp.where(chosen[1:, :, None], modulation[0][None], 0.0), axis=1
    )
    scale_attn, gate_attn, scale_ffn, gate_ffn = [
        lax.dynamic_index_in_dim(modulation, dp_index, 1, False)[k] for k in range(4)
    ]
    gains = [norm_gains[k] for k in range(4)]
    act_rows = tokens.astype(F32)
    first_in, first_pull = jax.vjp(modulate, act_rows, gains[0], scale_attn)
    near_tokens = jnp.stack(token_chain.result[1:]).astype(F32)
    near_in = modulate(near_tokens, gains[0], near_scales[:, None, :]).astype(BF)
    near_sets = near_in.shape[0]

    text_part = mm(text_all, text_matrix, NN).astype(BF)
    text_part = text_part.reshape(dp_count, text_len, 2 * local_width)
    text_sum = Chain(
        scatter_blocks([text_part[..., :local_width], text_part[..., local_width:]], dp_index)
    )
    first_chain = Chain(slots_from_mp(first_in.astype(BF)))
    near_chains = [
        Chain(slots_from_mp(near_in[k : k + 2].reshape(2 * row_count, width)))
        for k in range(0, near_sets, 2)
    ]
    links.stage(text_sum, first_chain, near_chains[0])
    links.stage(text_sum, first_chain, *near_chains[:2])
    first_low = jnp.concatenate(first_chain.result, axis=0)

    blocks = mp_index ^ jnp.arange(mp_count, dtype=jnp.int32)
    token_ids = (blocks[:, None] * row_count + jnp.arange(row_count, dtype=jnp.int32)).reshape(-1)
    text_ids = (blocks[:, None] * quarter_rows + jnp.arange(quarter_rows, dtype=jnp.int32)).reshape(-1)
    positions = ((origins - first_slot)[:, None] * seq_len + token_ids[None, :]).reshape(-1)
    quarter = HD // 4
    lane = jnp.arange(PAIR, dtype=jnp.int32)
    freqs = jnp.exp((lane % quarter).astype(F32) * (-math.log(10000.0) / quarter))
    place = jnp.where((lane % HD < HD // 2)[None, :], (positions // grid)[:, None], (positions % grid)[:, None])
    angles = place.astype(F32) * freqs[None, :]
    cos = jnp.cos(angles)
    sin = jnp.sin(angles) * jnp.where((lane % (2 * quarter)) < quarter, -1.0, 1.0)[None, :]
    local_gains = lax.dynamic_slice_in_dim(head_gains, mp_index * local_width, local_width, axis=1)
    tanh_gate = jnp.tanh(lax.dynamic_slice_in_dim(cross_gate, mp_index * local_heads, local_heads))

    bias = jnp.where(text_ids[None, :] < lengths[:, None], 0.0, NEG).astype(F32)
    bias = jnp.concatenate([bias, bias[:1]], axis=0)

    def project(tie):
        qkv_pre = mm(tie(first_low), qkv_full, NN)
        prepared = whole(
            prep_kernel,
            [((3 * seq_len, local_width), BF)],
            20 * seq_len * 3 * local_width,
            qkv_pre,
            local_gains,
            cos[:seq_len],
            sin[:seq_len],
        )
        return qkv_pre, prepared

    part_sets = near_sets // NEAR_PARTS
    part_rows = part_sets * seq_len

    def project_near(tie, k):
        pre = [mm(tie(slot), qkv_full[:, local_width:], NN) for slot in near_chains[k].result]
        there = slice(seq_len + k * part_rows, seq_len + (k + 1) * part_rows)
        return prepare_near(pre, local_gains, cos[there], sin[there], part_sets)

    (qkv_pre, prepared), near_first = links.stage(
        text_sum, *near_chains, work=lambda tie: (project(tie), project_near(tie, 0))
    )
    query = prepared[:seq_len]
    links.finish(text_sum)
    text_pre = jnp.concatenate(text_sum.result, axis=1)
    text_set = whole(
        text_prep_kernel,
        [((2 * text_len, local_width), BF)],
        20 * text_len * 2 * local_width,
        text_pre,
        local_gains,
    )
    text_sets_chain = Chain(send_sets(text_set, is_odd))
    near_second = links.stage(
        text_sets_chain, *near_chains, work=lambda tie: project_near(tie, 1)
    )
    links.finish(*near_chains)
    near_third = links.stage(text_sets_chain, work=lambda tie: project_near(tie, 2))
    self_sets = [prepared[seq_len:], near_first, near_second, near_third]

    def attend_self(tie):
        return attend(
            self_forward_kernel, [live], [tie(query)], [], self_sets, [(seq_len, F32)] * 2, 2, 2
        )

    out_self, log_self = links.stage(text_sets_chain, work=attend_self)
    text_sets = text_sets_chain.result

    def attend_text(tie):
        attn_low, out_text, log_text = attend(
            text_forward_kernel,
            [live, tanh_gate],
            [tie(query), out_self],
            [bias],
            text_sets,
            [(seq_len, BF), (seq_len, F32), (seq_len, F32)],
            2,
            2,
        )
        return attn_low, out_text, log_text

    attn_low, out_text, log_text = links.stage(work=attend_text)
    attn_rows = sum_to_mp(mm(attn_low, proj_full, NT))
    middle, middle_pull = jax.vjp(gated_add, attn_rows, gains[1], gate_attn, act_rows)
    second_in, second_pull = jax.vjp(modulate, middle, gains[2], scale_ffn)
    second_low = rows_from_mp(second_in.astype(BF))
    ffn_pre = mm(second_low, ffn_full, NN)
    hidden_f, swiglu_pull = jax.vjp(swiglu, ffn_pre[:, :units], ffn_pre[:, units:])
    hidden_low = hidden_f.astype(BF)
    ffn_rows = sum_to_mp(mm(hidden_low, down_full, NT))
    result, result_pull = jax.vjp(gated_add, ffn_rows, gains[3], gate_ffn, middle)


    grad_out = cotangent.astype(F32)
    grad_ffn_rows, grad_gain_four, grad_gate_ffn, grad_middle_a = result_pull(grad_out)
    grad_ffn_all = rows_from_mp(grad_ffn_rows.astype(BF))
    grad_hidden = mm(grad_ffn_all, down_full, NN)
    grad_gate_pre, grad_up_pre = swiglu_pull(grad_hidden)
    grad_pre_low = jnp.concatenate([grad_gate_pre, grad_up_pre], axis=1).astype(BF)
    second_part = mm(grad_pre_low, ffn_full, NT).astype(BF)

    def ffn_backward(tie):
        grad_second = sum_to_mp(second_part)
        terms = [mm(second_low, grad_pre_low, TN), mm(grad_ffn_all, hidden_low, TN)]
        return grad_second, jnp.concatenate([term.astype(BF) for term in terms], axis=1)

    grad_second, ffn_terms = links.stage(work=ffn_backward)
    ffn_sum = lax.psum_scatter(ffn_terms, "dp", scatter_dimension=0, tiled=True)
    grad_middle_b, grad_gain_three, grad_scale_ffn = second_pull(grad_second)
    grad_attn_rows, grad_gain_two, grad_gate_attn, grad_act_a = middle_pull(
        grad_middle_a + grad_middle_b
    )
    grad_attn_all = links.stage(
        work=lambda tie: rows_from_mp(tie(grad_attn_rows.astype(BF)))
    )

    def text_backward(tie):
        grad_attn_low = mm(tie(grad_attn_all), proj_full, NN).astype(BF)
        return grad_attn_low, attend(
            text_backward_kernel,
            [live, tanh_gate],
            [query, grad_attn_low, out_text, log_text],
            [bias.T],
            text_sets,
            [(2 * text_len, BF)] * len(text_sets) + [(seq_len, F32), (8, F32)],
            5,
            1,
        )

    def self_backward(tie):
        return attend(
            self_backward_kernel,
            [live],
            [query, tie(grad_attn_low), out_self, log_self],
            [],
            self_sets,
            [(2 * seq_len, BF)] * (near_sets + 1) + [(seq_len, F32)],
            5,
            1,
        )

    grad_attn_low, text_grads = links.stage(work=text_backward)
    gate_dots = text_grads[-1]
    text_return = Chain(return_sets(text_grads[: len(text_sets)], is_odd))
    self_grads = links.stage(text_return, work=self_backward)
    self_return = Chain(return_sets(self_grads[:-1], is_odd))

    def query_backward(tie):
        grad_query_low, head_query = whole(
            query_back_kernel,
            [((seq_len, local_width), BF), ((8, local_width), F32)],
            20 * seq_len * local_width,
            qkv_pre,
            local_gains,
            cos[:seq_len],
            sin[:seq_len],
            tie(self_grads[-1]),
            text_grads[-2],
        )
        return (
            grad_query_low,
            head_query,
            mm(first_low, grad_query_low, TN).astype(BF),
            mm(grad_attn_all, attn_low, TN).astype(BF),
        )

    grad_query_low, head_query, grad_query_weight, grad_proj = links.stage(
        text_return, self_return, work=query_backward
    )

    def blocks(value):
        return value.reshape(dp_count, shard, local_width)

    query_sum = Chain(scatter_blocks([blocks(grad_query_weight), blocks(grad_proj)], dp_index))
    links.stage(text_return, self_return, query_sum)
    own_text = text_return.result

    def text_rows_backward(tie):
        return whole(
            text_back_kernel,
            [((text_len, 2 * local_width), BF), ((8, local_width), F32)],
            20 * text_len * 2 * local_width,
            text_pre,
            local_gains,
            tie(own_text),
        )

    grad_text_low, head_text = text_rows_backward(lambda value: value)
    text_back = Chain(
        gather_blocks([grad_text_low[:, :local_width], grad_text_low[:, local_width:]], dp_index)
    )
    links.finish_only(self_return, (query_sum, text_back))
    own_self, ffn_sum = lax.optimization_barrier((self_return.result, ffn_sum))

    def key_backward(tie):
        grad_key_low, head_key = whole(
            key_back_kernel,
            [((seq_len, 2 * local_width), BF), ((8, local_width), F32)],
            20 * seq_len * 2 * local_width,
            qkv_pre,
            local_gains,
            cos[:seq_len],
            sin[:seq_len],
            tie(own_self),
        )
        first_part = mm(grad_query_low, qkv_full[:, :local_width], NT) + mm(
            grad_key_low, qkv_full[:, local_width:], NT
        )
        return head_key, mm(first_low, grad_key_low, TN).astype(BF), first_part.astype(BF)

    head_key, grad_key_weight, first_part = links.stage(query_sum, text_back, work=key_backward)
    key_sum = Chain(
        scatter_blocks(
            [blocks(grad_key_weight[:, :local_width]), blocks(grad_key_weight[:, local_width:])],
            dp_index,
        )
    )
    grad_first = links.stage(
        query_sum, text_back, key_sum, work=lambda tie: sum_to_mp(tie(first_part))
    )
    grad_act_b, grad_gain_one, grad_scale_attn = first_pull(grad_first)
    grad_tokens = grad_act_a + grad_act_b
    mod_grads = jnp.stack([grad_scale_attn, grad_gate_attn, grad_scale_ffn, grad_gate_ffn])
    links.finish(text_back)
    text_rows = jnp.concatenate(text_back.result, axis=1)

    def gather_mod_grads(tie):
        mod_sum = sum_all(tie(mod_grads), "mp")
        mine = jnp.arange(mp_count)[:, None] == mp_index
        grad_mod_low = jnp.sum(jnp.where(mine, mod_sum, 0.0), axis=0)[None].astype(BF)
        return grad_mod_low, gather_in_order(grad_mod_low, "dp", dp_index)

    def caption_rows(tie):
        part = mm(tie(text_rows), text_matrix, NT).astype(BF)
        part = part.reshape(dp_count, mp_count, quarter_rows, text_shard)
        part = jnp.transpose(part, (1, 0, 2, 3)).reshape(-1, text_shard)
        return sum_to_mp(part).astype(BF).reshape(dp_count, quarter_rows, text_shard)

    (grad_mod_low, grad_mod_all), caption_mine = links.stage(
        query_sum, key_sum, work=lambda tie: (gather_mod_grads(tie), caption_rows(tie))
    )
    caption_back = Chain(exchange_blocks(caption_mine, dp_index))

    row_grads = jnp.stack([grad_gain_one, grad_gain_two, grad_gain_three, grad_gain_four])
    grad_ada = mm(cond_mine, grad_mod_all, TN) * weight_scale
    cond_part = mm(grad_mod_all, ada_weight, NT)
    zeros = functools.partial(jnp.zeros, dtype=F32)
    cond_rows = lax.dynamic_update_slice_in_dim(
        zeros((dp_count, width)), cond_part, dp_index * shard, 1
    )
    head_local = jnp.concatenate([head_query[:1], head_key[:1], head_text[:1]], axis=0)
    head_rows = lax.dynamic_update_slice_in_dim(
        zeros((3, width)), head_local, mp_index * local_width, 1
    )
    bias_rows = jnp.where(
        jnp.arange(mp_count)[:, None] == mp_index, grad_mod_low.astype(F32), 0.0
    )
    gate_local = gate_dots[0].reshape(local_heads, HD)[:, 0] * (1.0 - tanh_gate * tanh_gate)
    gate_row = lax.dynamic_update_slice_in_dim(
        zeros((1, width)), gate_local[None], mp_index * local_heads, 1
    )
    small = jnp.concatenate([row_grads, head_rows, bias_rows, gate_row, cond_rows], axis=0)
    small = links.stage(
        query_sum, key_sum, caption_back, work=lambda tie: sum_all(sum_all(tie(small), "mp"), "dp")
    )
    links.finish(query_sum, key_sum, caption_back)
    columns = jnp.transpose(caption_back.result, (1, 0, 2)).reshape(quarter_rows, text_dim)
    block = text_dim // mp_count
    grad_caption = jnp.zeros((text_len, block), F32)
    for bit in range(mp_count):
        other = mp_index ^ bit
        piece = lax.dynamic_slice_in_dim(columns, other * block, block, axis=1)
        if bit:
            piece = swap(piece, "mp", bit)
        grad_caption = lax.dynamic_update_slice_in_dim(
            grad_caption, piece.astype(F32), other * quarter_rows, 0
        )
    grad_text = mm(text_all, text_rows, TN) * weight_scale
    ffn_sum = ffn_sum.astype(F32) * weight_scale
    query_sum, proj_sum = [value * weight_scale for value in query_sum.result]
    key_sum, value_sum = [value * weight_scale for value in key_sum.result]
    cond_width = width // mp_count
    cond_sum = lax.dynamic_slice(small[12:], (dp_index, mp_index * cond_width), (1, cond_width))
    cond_cols = lax.dynamic_slice_in_dim(condition, mp_index * cond_width, cond_width, axis=1)
    silu_vals, silu_pull = jax.vjp(jax.nn.silu, cond_cols)
    grad_condition = silu_pull(cond_sum)[0] * (1.0 / math.sqrt(seq_len))
    scaled = small[:12] * weight_scale

    def parted(values, parts):
        return jnp.transpose(values.reshape(values.shape[0], parts, -1), (1, 0, 2))

    return (
        result.astype(BF),
        grad_tokens,
        grad_caption[None],
        grad_condition,
        jnp.stack([query_sum, key_sum, value_sum]),
        proj_sum.T,
        parted(grad_text, 2),
        parted(ffn_sum[:, : 2 * units], 2),
        ffn_sum[:, 2 * units :].T,
        grad_ada,
        scaled[:4],
        scaled[4:7],
        scaled[7:11].reshape(-1),
        scaled[11, :HEADS],
    )


def solution(mesh):
    return jax.shard_map(
        local,
        mesh=mesh,
        in_specs=(
            P(("dp", "mp"), None),
            P("dp", None, None),
            P("dp", None),
            P(("dp", "mp"), None),
            P(None, "dp", "mp"),
            P("mp", "dp"),
            P(None, "dp", "mp"),
            P(None, "dp", "mp"),
            P("mp", "dp"),
            P("dp", "mp"),
            P(),
            P(),
            P(),
            P(),
            P(),
            P(),
            P(),
        ),
        out_specs=(
            P(("dp", "mp"), None),
            P(("dp", "mp"), None),
            P("dp", None, "mp"),
            P("dp", "mp"),
            P(None, "dp", "mp"),
            P("mp", "dp"),
            P(None, "dp", "mp"),
            P(None, "dp", "mp"),
            P("mp", "dp"),
            P("dp", "mp"),
            P(),
            P(),
            P(),
            P(),
        ),
        check_vma=False,
    )
```

```python
import functools
import math

import jax
import jax.numpy as jnp
from jax import lax
from jax.experimental import pallas as pl
from jax.experimental.pallas import tpu as pltpu
from jax.sharding import PartitionSpec as P

HEADS = 24
HD = 64
PAIR = 2 * HD
NEAR_PARTS = 3
EPS = 1e-06
NEG = -1e30
SCALE = HD ** (-0.5)
BF = jnp.bfloat16
F32 = jnp.float32
NN = (((1,), (0,)), ((), ()))
NT = (((1,), (1,)), ((), ()))
TN = (((0,), (0,)), ((), ()))


def mm(left, right, dims):
    return lax.dot_general(left, right, dims, preferred_element_type=F32)


def swap(value, axis, bit):
    count = lax.axis_size(axis)
    return lax.ppermute(value, axis, [(i, i ^ bit) for i in range(count)])


def all_bits(count):
    return [1 << k for k in range(count.bit_length() - 1)]


def after(value, *others):
    return lax.optimization_barrier((value,) + others)[0]


class Chain:
    def __init__(self, steps):
        self.steps, self.result = steps, None
        self.advance(None)

    def advance(self, arrived):
        try:
            self.wanted = self.steps.send(arrived)
        except StopIteration as end:
            self.wanted, self.result = None, end.value


class Links:
    def __init__(self):
        self.last = ()

    def stage(self, *chains, work=None):
        active = [chain for chain in chains if chain.wanted is not None]
        wanted = [item for chain in active for item in chain.wanted]
        values = [value for value, _, _ in wanted]
        if self.last and values:
            values = lax.optimization_barrier(tuple(values) + self.last)[: len(values)]
        moved = [
            lax.ppermute(value, axis, pairs) for value, (_, axis, pairs) in zip(values, wanted)
        ]
        made = work(lambda value: after(value, *self.last)) if work else ()
        moved, made = lax.optimization_barrier((moved, made))
        self.last = tuple(moved[:1]) or tuple(jax.tree.leaves(made)[:1])
        for chain in active:
            count = len(chain.wanted)
            chain.advance(moved[:count])
            moved = moved[count:]
        return made

    def finish_only(self, chain, others):
        while chain.wanted is not None:
            self.stage(chain, *others)

    def finish(self, *chains):
        while any(chain.wanted is not None for chain in chains):
            self.stage(*chains)


def swap_pairs(axis, bit):
    return [(i, i ^ bit) for i in range(lax.axis_size(axis))]


def crossed_bits():
    bits = all_bits(lax.axis_size("dp"))
    return bits, bits[1::-1] + bits[2:]


def bit_axis(bits, bit):
    return sum(other > bit for other in bits)


def in_order(high, own, other, axis):
    return jnp.stack([jnp.where(high, other, own), jnp.where(high, own, other)], axis=axis)


def halves(high, value, axis):
    zero, one = [lax.index_in_dim(value, k, axis, keepdims=False) for k in range(2)]
    return jnp.where(high, zero, one), jnp.where(high, one, zero)


def gather_blocks(pair, index):
    orders = [bits[::-1] for bits in crossed_bits()]
    values, done = list(pair), ([], [])
    for bits in zip(*orders):
        moved = yield [(value, "dp", swap_pairs("dp", bit)) for value, bit in zip(values, bits)]
        for side, bit in enumerate(bits):
            axis = bit_axis(done[side], bit)
            values[side] = in_order((index & bit) != 0, values[side], moved[side], axis)
            done[side].append(bit)
    return [value.reshape((-1,) + own.shape[1:]) for value, own in zip(values, pair)]


def scatter_blocks(pair, index):
    orders = crossed_bits()
    left = [list(bits) for bits in orders]
    values = [value.reshape((2,) * len(orders[0]) + value.shape[1:]) for value in pair]
    for bits in zip(*orders):
        sent, kept = [], []
        for side, bit in enumerate(bits):
            parts = halves((index & bit) != 0, values[side], bit_axis(left[side], bit))
            sent.append((parts[0].astype(BF), "dp", swap_pairs("dp", bit)))
            kept.append(parts[1])
            left[side].remove(bit)
        moved = yield sent
        values = [plus(own, other) for own, other in zip(kept, moved)]
    return values


def exchange_blocks(value, index):
    count = value.shape[0]
    bits, left, done = all_bits(count), all_bits(count), []
    shape = value.shape[1:]
    value = value.reshape((2,) * len(bits) + shape)
    for bit in bits:
        high = (index & bit) != 0
        sent, kept = halves(high, value, bit_axis(left, bit))
        left.remove(bit)
        (moved,) = yield [(sent, "dp", swap_pairs("dp", bit))]
        value = in_order(high, kept, moved, len(left) + bit_axis(done, bit))
        done.append(bit)
    return value.reshape((count,) + shape)


def plus(*values):
    return sum(value.astype(F32) for value in values)


def sum_all(value, axis):
    bit = 1
    while bit < lax.axis_size(axis):
        value = value + swap(value, axis, bit)
        bit *= 2
    return value


def gather_in_order(value, axis, index):
    bit = 1
    while bit < lax.axis_size(axis):
        other = swap(value, axis, bit)
        high = (index & bit) != 0
        value = jnp.concatenate(
            [jnp.where(high, other, value), jnp.where(high, value, other)], axis=0
        )
        bit *= 2
    return value


def chain_sum(value, axis):
    for bit in all_bits(lax.axis_size(axis)):
        (other,) = yield [(value, axis, swap_pairs(axis, bit))]
        value = value + other
    return value


def rows_from_mp(value, axis=0):
    far = swap(value, "mp", 2)
    near = swap(value, "mp", 1)
    return jnp.concatenate([value, near, far, swap(far, "mp", 1)], axis=axis)


def slots_from_mp(value):
    far, near = yield [(value, "mp", swap_pairs("mp", bit)) for bit in (2, 1)]
    (last,) = yield [(far, "mp", swap_pairs("mp", 1))]
    return [value, near, far, last]


def sum_to_mp(value):
    count = value.shape[0] // 4
    blocks = [value[k * count : (k + 1) * count] for k in range(4)]
    far = blocks[2].astype(F32) + swap(blocks[3].astype(BF), "mp", 1).astype(F32)
    near = blocks[0].astype(F32) + swap(blocks[1].astype(BF), "mp", 1).astype(F32)
    return near + swap(far.astype(BF), "mp", 2).astype(F32)


def shifted(steps, keep=lambda i: True):
    count = lax.axis_size("dp")
    return [(i, i + steps) for i in range(count) if keep(i) and 0 <= i + steps < count]


def even(i):
    return i % 2 == 0


def odd(i):
    return i % 2 == 1


def out_pairs():
    return shifted(-2, even) + shifted(2, odd)


def back_pairs():
    return shifted(2, even) + shifted(-2, odd)


def send_sets(own, is_odd):
    beside, low, high = yield [
        (own, "dp", swap_pairs("dp", 1)),
        (own, "dp", shifted(2)),
        (own, "dp", shifted(-2)),
    ]
    across, third = yield [
        (jnp.where(is_odd, low, high), "dp", swap_pairs("dp", 1)),
        (beside, "dp", out_pairs()),
    ]
    (fourth,) = yield [(across, "dp", back_pairs())]
    return [own, beside, low, high, across, third, fourth]


def set_offsets(is_odd):
    return jnp.where(
        is_odd, jnp.asarray([0, -1, -2, 2, 1, -3, 3]), jnp.asarray([0, 1, -2, 2, -1, 3, -3])
    )


def return_sets(grads, is_odd):
    own, beside, low, high, across, third, fourth = grads
    (fourth,) = yield [(fourth, "dp", out_pairs())]
    across, third = yield [
        (plus(across, fourth).astype(BF), "dp", swap_pairs("dp", 1)),
        (third, "dp", back_pairs()),
    ]
    low = plus(low, jnp.where(is_odd, across, 0)).astype(BF)
    high = plus(high, jnp.where(is_odd, 0, across)).astype(BF)
    beside, low, high = yield [
        (plus(beside, third).astype(BF), "dp", swap_pairs("dp", 1)),
        (low, "dp", shifted(-2)),
        (high, "dp", shifted(2)),
    ]
    return plus(own, beside, low, high)


def norm_rows(values, weights):
    return values * lax.rsqrt(jnp.mean(values * values, axis=-1, keepdims=True) + EPS) * weights


def modulate(values, weights, scales):
    return norm_rows(values, weights) * (1.0 + scales)


def gated_add(branch, weights, gates, resid):
    return resid + jnp.tanh(gates) * norm_rows(branch, weights)


def swiglu(gate_pre, up_pre):
    return jax.nn.silu(gate_pre) * up_pre


def lanes(rows):
    return lax.broadcasted_iota(jnp.int32, (rows, PAIR), 1)


def head_sum(values):
    low = lanes(values.shape[0]) < HD
    first = jnp.sum(jnp.where(low, values, 0.0), axis=-1, keepdims=True)
    second = jnp.sum(jnp.where(low, 0.0, values), axis=-1, keepdims=True)
    return jnp.where(low, first, second)


def partner(values):
    quarter = HD // 4
    first = (lanes(values.shape[0]) % (2 * quarter)) < quarter
    return jnp.where(
        first, pltpu.roll(values, PAIR - quarter, 1), pltpu.roll(values, quarter, 1)
    )


def normed(values):
    return values * lax.rsqrt(head_sum(values * values) / HD + EPS)


def prep_kernel(pre_ref, gains_ref, cos_ref, sin_ref, out_ref):
    width = out_ref.shape[1]
    rows = pre_ref.shape[0]
    cos, sin = cos_ref[...], sin_ref[...]
    for part in range(2):
        for start in range(0, width, PAIR):
            here = pl.ds(part * width + start, PAIR)
            turned = normed(pre_ref[:, here]) * gains_ref[part : part + 1, pl.ds(start, PAIR)]
            if part == 0:
                turned = turned * cos + partner(turned) * sin
                out_ref[pl.ds(0, rows), pl.ds(start, PAIR)] = turned.astype(BF)
            else:
                turned = turned * cos + partner(turned) * sin
                out_ref[pl.ds(rows, rows), pl.ds(start, PAIR)] = turned.astype(BF)
    out_ref[pl.ds(2 * rows, rows), :] = pre_ref[:, pl.ds(2 * width, width)].astype(BF)


def near_prep_kernel(gains_ref, cos_ref, sin_ref, *refs):
    *pre_refs, out_ref = refs
    rows, width = pre_refs[0].shape[0], out_ref.shape[1]
    depth = rows * len(pre_refs)
    for slot, pre_ref in enumerate(pre_refs):
        there = pl.ds(slot * rows, rows)
        cos, sin = cos_ref[there, :], sin_ref[there, :]
        for start in range(0, width, PAIR):
            here = pl.ds(start, PAIR)
            turned = normed(pre_ref[:, here]) * gains_ref[1:2, here]
            turned = turned * cos + partner(turned) * sin
            out_ref[there, here] = turned.astype(BF)
        out_ref[pl.ds(depth + slot * rows, rows), :] = pre_ref[:, pl.ds(width, width)].astype(BF)


def text_prep_kernel(pre_ref, gains_ref, out_ref):
    rows, width = pre_ref.shape[0], out_ref.shape[1]
    for start in range(0, width, PAIR):
        here = pl.ds(start, PAIR)
        value = normed(pre_ref[:, here]) * gains_ref[2:3, here]
        out_ref[pl.ds(0, rows), here] = value.astype(BF)
    out_ref[pl.ds(rows, rows), :] = pre_ref[:, pl.ds(width, width)].astype(BF)


def norm_back(pre, gains, grad):
    ratio = lax.rsqrt(head_sum(pre * pre) / HD + EPS)
    scaled = grad * gains
    grad_pre = ratio * scaled - pre * (ratio * ratio * ratio) * (head_sum(pre * scaled) / HD)
    return grad_pre, jnp.sum(grad * pre * ratio, axis=0, keepdims=True)


def query_back_kernel(pre_ref, gains_ref, cos_ref, sin_ref, self_ref, text_ref, out_ref, head_ref):
    cos, sin = cos_ref[...], sin_ref[...]
    head_ref[...] = jnp.zeros_like(head_ref)
    for start in range(0, out_ref.shape[1], PAIR):
        here = pl.ds(start, PAIR)
        grad = self_ref[:, here] + text_ref[:, here]
        grad = grad * cos - partner(grad) * sin
        grad_pre, grad_gain = norm_back(pre_ref[:, here], gains_ref[0:1, here], grad)
        out_ref[:, here] = grad_pre.astype(BF)
        head_ref[0:1, here] = grad_gain


def key_back_kernel(pre_ref, gains_ref, cos_ref, sin_ref, set_ref, out_ref, head_ref):
    rows, width = pre_ref.shape[0], set_ref.shape[1]
    cos, sin = cos_ref[...], sin_ref[...]
    head_ref[...] = jnp.zeros_like(head_ref)
    for start in range(0, width, PAIR):
        here = pl.ds(start, PAIR)
        grad = set_ref[pl.ds(0, rows), here]
        grad = grad * cos - partner(grad) * sin
        grad_pre, grad_gain = norm_back(
            pre_ref[:, pl.ds(width + start, PAIR)], gains_ref[1:2, here], grad
        )
        out_ref[:, here] = grad_pre.astype(BF)
        head_ref[0:1, here] = grad_gain
    out_ref[:, pl.ds(width, width)] = set_ref[pl.ds(rows, rows), :].astype(BF)


def text_back_kernel(pre_ref, gains_ref, set_ref, out_ref, head_ref):
    rows, width = pre_ref.shape[0], set_ref.shape[1]
    head_ref[...] = jnp.zeros_like(head_ref)
    for start in range(0, width, PAIR):
        here = pl.ds(start, PAIR)
        grad_pre, grad_gain = norm_back(
            pre_ref[:, here], gains_ref[2:3, here], set_ref[pl.ds(0, rows), here]
        )
        out_ref[:, here] = grad_pre.astype(BF)
        head_ref[0:1, here] = grad_gain
    out_ref[:, pl.ds(width, width)] = set_ref[pl.ds(rows, rows), :].astype(BF)


def split_pair(values):
    low = lanes(values.shape[0]) < HD
    zero = jnp.zeros_like(values)
    return jnp.where(low, values, zero), jnp.where(low, zero, values)


def forward_sums(live_ref, query_ref, set_refs, bias_ref, total, weight):
    low = lanes(query_ref.shape[0]) < HD
    total[...] = jnp.zeros_like(total)
    weight[...] = jnp.zeros_like(weight)
    for index, source in enumerate(set_refs):

        @pl.when(live_ref[index] > 0)
        def _(index=index, source=source):
            depth = source.shape[0] // 2
            keys, values = source[pl.ds(0, depth), :], source[pl.ds(depth, depth), :]
            outs, sums = [], []
            for query in split_pair(query_ref[...] * jnp.asarray(SCALE, BF)):
                logits = mm(query, keys, NT)
                if bias_ref is not None:
                    logits = logits + bias_ref[index : index + 1, :]
                probs = jnp.exp(logits)
                sums.append(jnp.sum(probs, axis=-1, keepdims=True))
                outs.append(mm(probs.astype(BF), values, NN))
            total[...] += jnp.where(low, outs[0], outs[1])
            weight[...] += jnp.where(low, sums[0], sums[1])


def views(own_ref, near_refs):
    depth = own_ref.shape[0]
    return [own_ref] + [
        near_ref.at[pl.ds(start, depth), :]
        for near_ref in near_refs
        for start in range(0, near_ref.shape[0], depth)
    ]


def self_forward_kernel(live_ref, query_ref, own_ref, *refs):
    *near_refs, out_ref, log_ref, total, weight = refs
    set_refs = views(own_ref, near_refs)
    forward_sums(live_ref, query_ref, set_refs, None, total, weight)
    out_ref[...] = total[...] / weight[...]
    log_ref[...] = jnp.log(weight[...])


def text_forward_kernel(live_ref, gate_ref, query_ref, self_ref, bias_ref, *refs):
    *set_refs, attn_ref, out_ref, log_ref, total, weight = refs
    forward_sums(live_ref, query_ref, set_refs, bias_ref, total, weight)
    low = lanes(query_ref.shape[0]) < HD
    pair = pl.program_id(0)
    gate = jnp.where(low, gate_ref[2 * pair], gate_ref[2 * pair + 1])
    out = total[...] / weight[...]
    attn_ref[...] = (self_ref[...] + gate * out).astype(BF)
    out_ref[...] = out
    log_ref[...] = jnp.log(weight[...])


def backward_sums(live_ref, query_ref, grad_ref, log_ref, delta, bias_ref, gates, refs, total):
    count = len(refs) // 2
    low = lanes(query_ref.shape[0]) < HD
    logs_all, delta_all = jnp.transpose(log_ref[...]), jnp.transpose(delta)
    total[...] = jnp.zeros_like(total)
    for index, (source, out_ref) in enumerate(zip(refs[:count], refs[count:])):

        @pl.when(live_ref[index] > 0)
        def _(index=index, source=source, out_ref=out_ref):
            queries = split_pair(query_ref[...] * jnp.asarray(SCALE, BF))
            grads = split_pair(grad_ref[...])
            depth = source.shape[0] // 2
            keys, values = source[pl.ds(0, depth), :], source[pl.ds(depth, depth), :]
            grad_query, grad_key, grad_value = [], [], []
            for head in range(2):
                row = head * HD
                logits = mm(keys, queries[head], NT)
                if bias_ref is not None:
                    logits = logits + bias_ref[:, index : index + 1]
                probs = jnp.exp(logits - logs_all[row : row + 1, :])
                value_part = mm(probs.astype(BF), grads[head], NN)
                grad_probs = mm(values, grads[head], NT)
                if gates is not None:
                    value_part = value_part * gates[head]
                    grad_probs = grad_probs * gates[head]
                grad_logits = (probs * (grad_probs - delta_all[row : row + 1, :])).astype(BF)
                grad_value.append(value_part)
                grad_key.append(mm(grad_logits, queries[head], NN))
                grad_query.append(mm(grad_logits, keys, TN))
            total[...] += jnp.where(low, grad_query[0], grad_query[1])
            out_ref[pl.ds(0, depth), :] = (grad_key[0] + grad_key[1]).astype(BF)
            out_ref[pl.ds(depth, depth), :] = (grad_value[0] + grad_value[1]).astype(BF)

        @pl.when(live_ref[index] == 0)
        def _(out_ref=out_ref):
            out_ref[...] = jnp.zeros_like(out_ref)


def self_backward_kernel(
    live_ref, query_ref, grad_ref, out_ref, log_ref, own_ref, *refs
):
    near_refs, grad_refs = refs[:NEAR_PARTS], list(refs[NEAR_PARTS:-2])
    query_grad_ref, total = refs[-2:]
    set_refs = views(own_ref, near_refs) + grad_refs
    delta = head_sum(grad_ref[...].astype(F32) * out_ref[...])
    backward_sums(live_ref, query_ref, grad_ref, log_ref, delta, None, None, set_refs, total)
    query_grad_ref[...] = total[...] * SCALE


def text_backward_kernel(
    live_ref, gate_ref, query_ref, grad_ref, out_ref, log_ref, bias_ref, *refs
):
    *set_refs, query_grad_ref, gate_grad_ref, total = refs
    low = lanes(query_ref.shape[0]) < HD
    pair = pl.program_id(0)
    gates = (gate_ref[2 * pair], gate_ref[2 * pair + 1])
    dots = head_sum(grad_ref[...].astype(F32) * out_ref[...])
    gate_grad_ref[...] = jnp.broadcast_to(jnp.sum(dots, axis=0, keepdims=True), gate_grad_ref.shape)
    delta = jnp.where(low, gates[0], gates[1]) * dots
    backward_sums(live_ref, query_ref, grad_ref, log_ref, delta, bias_ref, gates, set_refs, total)
    query_grad_ref[...] = total[...] * SCALE


def params(limit=40):
    return pltpu.CompilerParams(vmem_limit_bytes=limit * 2**20)


def whole(kernel, outs, cost, *args):
    shapes = [jax.ShapeDtypeStruct(shape, dtype) for shape, dtype in outs]
    return pl.pallas_call(
        kernel,
        out_shape=shapes if len(shapes) > 1 else shapes[0],
        compiler_params=params(),
        cost_estimate=pl.CostEstimate(flops=cost, bytes_accessed=2 * cost // 10, transcendentals=0),
    )(*args)


def column(rows):
    return pl.BlockSpec((rows, PAIR), lambda pair: (0, pair))


def fixed(shape):
    return pl.BlockSpec(shape, lambda pair: (0, 0))


def prepare_near(pre, gains, cos, sin, sets):
    rows, width = pre[0].shape[0] // sets, gains.shape[1]
    depth = rows * len(pre)

    def block(count, columns):
        return pl.BlockSpec((count, columns), lambda k: (k, 0))

    return pl.pallas_call(
        near_prep_kernel,
        grid=(sets,),
        in_specs=[pl.BlockSpec(gains.shape, lambda k: (0, 0))]
        + [block(depth, PAIR)] * 2
        + [block(rows, 2 * width)] * len(pre),
        out_specs=block(2 * depth, width),
        out_shape=jax.ShapeDtypeStruct((sets * 2 * depth, width), BF),
        compiler_params=params(),
        cost_estimate=pl.CostEstimate(
            flops=40 * sets * depth * width,
            bytes_accessed=12 * sets * depth * width,
            transcendentals=0,
        ),
    )(gains, cos, sin, *pre)


def attend(kernel, scalars, columns, bias, sets, outs, passes, scratch, limit=56):
    rows, width = columns[0].shape
    keys = sets[0].shape[0] // 2
    smem = pl.BlockSpec(memory_space=pltpu.SMEM)
    return pl.pallas_call(
        kernel,
        grid=(width // PAIR,),
        in_specs=[smem] * len(scalars)
        + [column(value.shape[0]) for value in columns]
        + [fixed(value.shape) for value in bias]
        + [column(value.shape[0]) for value in sets],
        out_specs=[column(depth) for depth, _ in outs],
        out_shape=[jax.ShapeDtypeStruct((depth, width), dtype) for depth, dtype in outs],
        scratch_shapes=[pltpu.VMEM((rows, PAIR), F32)] * scratch,
        compiler_params=params(limit),
        cost_estimate=pl.CostEstimate(
            flops=passes * 16 * rows * keys * width,
            bytes_accessed=40 * rows * width,
            transcendentals=4 * rows * keys * width // HD,
        ),
    )(*scalars, *columns, *bias, *sets)


def local(
    tokens,
    caption,
    condition,
    cotangent,
    qkv_weight,
    proj_weight,
    text_weight,
    ffn_weight,
    down_weight,
    ada_weight,
    norm_gains,
    head_gains,
    ada_bias,
    cross_gate,
    group_map,
    grid_width,
    caption_len,
):
    dp_count = lax.axis_size("dp")
    mp_count = lax.axis_size("mp")
    dp_index = lax.axis_index("dp")
    mp_index = lax.axis_index("mp")
    row_count, width = tokens.shape
    seq_len = row_count * mp_count
    local_width = qkv_weight.shape[2]
    local_heads = local_width // HD
    text_len, text_dim = caption.shape[1:]
    units = ffn_weight.shape[2]
    shard = qkv_weight.shape[1]
    weight_scale = 1.0 / math.sqrt(seq_len * dp_count)
    is_odd = (dp_index % 2) == 1
    links = Links()

    qkv_shard = jnp.transpose(qkv_weight, (1, 0, 2)).reshape(shard, 3 * local_width)
    rest_shard = jnp.concatenate(
        [proj_weight.T, jnp.transpose(ffn_weight, (1, 0, 2)).reshape(shard, 2 * units), down_weight.T],
        axis=1,
    )
    qkv_full = lax.all_gather(qkv_shard, "dp", axis=0, tiled=True)
    rest = lax.all_gather(rest_shard, "dp", axis=0, tiled=True)
    cuts = (0, local_width, local_width + 2 * units, local_width + 3 * units)
    proj_full, ffn_full, down_full = [rest[:, low:high] for low, high in zip(cuts[:-1], cuts[1:])]

    text_shard = text_weight.shape[1]
    quarter_rows = text_len // mp_count
    my_rows = lax.dynamic_slice_in_dim(caption[0], mp_index * quarter_rows, quarter_rows, axis=0)
    text_matrix = jnp.transpose(text_weight, (1, 0, 2)).reshape(text_shard, 2 * local_width)
    my_rows = jnp.transpose(my_rows.reshape(quarter_rows, dp_count, text_shard), (1, 0, 2))

    def modulate_all():
        value = jax.nn.silu(condition).astype(BF)
        for bit in all_bits(dp_count):
            (other,) = yield [(value, "dp", swap_pairs("dp", bit))]
            value = in_order((dp_index & bit) != 0, value, other, 0).reshape(2 * bit, width)
        cond_mine = lax.dynamic_slice_in_dim(value, dp_index * shard, shard, axis=1)
        value = mm(cond_mine, ada_weight, NN)
        for bit in all_bits(dp_count):
            (other,) = yield [(value, "dp", swap_pairs("dp", bit))]
            value = value + other
        bias_part = lax.dynamic_slice_in_dim(ada_bias, mp_index * width, width)
        value = (value + bias_part[None, :])[None]
        for bit in all_bits(mp_count):
            (other,) = yield [(value, "mp", swap_pairs("mp", bit))]
            value = in_order((mp_index & bit) != 0, value, other, 0).reshape(2 * bit, dp_count, width)
        return cond_mine, value

    def caption_features():
        value = yield from exchange_blocks(my_rows, dp_index)
        far, near = yield [(value, "mp", swap_pairs("mp", bit)) for bit in (2, 1)]
        (last,) = yield [(far, "mp", swap_pairs("mp", 1))]
        return jnp.concatenate([value, near, far, last], axis=1)

    mod_chain, caption_chain = Chain(modulate_all()), Chain(caption_features())
    token_chain = Chain(send_sets(tokens, is_odd))
    links.finish(mod_chain, caption_chain, token_chain)
    cond_mine, modulation = mod_chain.result
    text_all = caption_chain.result.reshape(dp_count * text_len, text_shard)

    origins = dp_index + set_offsets(is_odd)
    chosen = jnp.arange(dp_count)[None, :] == origins[:, None]

    def looked_up(table):
        return jnp.sum(jnp.where(chosen, table[None, :], 0), axis=1)

    inside = (origins >= 0) & (origins < dp_count)
    first_slot = jnp.sum(jnp.where(jnp.arange(dp_count) == dp_index, group_map, 0))
    grid = jnp.sum(jnp.where(jnp.arange(dp_count) == dp_index, grid_width, 0))
    live = (inside & (looked_up(group_map) == first_slot)).astype(jnp.int32)
    lengths = looked_up(caption_len)

    near_scales = jnp.sum(
        jnp.where(chosen[1:, :, None], modulation[0][None], 0.0), axis=1
    )
    scale_attn, gate_attn, scale_ffn, gate_ffn = [
        lax.dynamic_index_in_dim(modulation, dp_index, 1, False)[k] for k in range(4)
    ]
    gains = [norm_gains[k] for k in range(4)]
    act_rows = tokens.astype(F32)
    first_in, first_pull = jax.vjp(modulate, act_rows, gains[0], scale_attn)
    near_tokens = jnp.stack(token_chain.result[1:]).astype(F32)
    near_in = modulate(near_tokens, gains[0], near_scales[:, None, :]).astype(BF)
    near_sets = near_in.shape[0]

    text_part = mm(text_all, text_matrix, NN).astype(BF)
    text_part = text_part.reshape(dp_count, text_len, 2 * local_width)
    text_sum = Chain(
        scatter_blocks([text_part[..., :local_width], text_part[..., local_width:]], dp_index)
    )
    first_chain = Chain(slots_from_mp(first_in.astype(BF)))
    near_chains = [
        Chain(slots_from_mp(near_in[k : k + 2].reshape(2 * row_count, width)))
        for k in range(0, near_sets, 2)
    ]
    links.stage(text_sum, first_chain, near_chains[0])
    links.stage(text_sum, first_chain, *near_chains[:2])
    first_low = jnp.concatenate(first_chain.result, axis=0)

    blocks = mp_index ^ jnp.arange(mp_count, dtype=jnp.int32)
    token_ids = (blocks[:, None] * row_count + jnp.arange(row_count, dtype=jnp.int32)).reshape(-1)
    text_ids = (blocks[:, None] * quarter_rows + jnp.arange(quarter_rows, dtype=jnp.int32)).reshape(-1)
    positions = ((origins - first_slot)[:, None] * seq_len + token_ids[None, :]).reshape(-1)
    quarter = HD // 4
    lane = jnp.arange(PAIR, dtype=jnp.int32)
    freqs = jnp.exp((lane % quarter).astype(F32) * (-math.log(10000.0) / quarter))
    place = jnp.where((lane % HD < HD // 2)[None, :], (positions // grid)[:, None], (positions % grid)[:, None])
    angles = place.astype(F32) * freqs[None, :]
    cos = jnp.cos(angles)
    sin = jnp.sin(angles) * jnp.where((lane % (2 * quarter)) < quarter, -1.0, 1.0)[None, :]
    local_gains = lax.dynamic_slice_in_dim(head_gains, mp_index * local_width, local_width, axis=1)
    tanh_gate = jnp.tanh(lax.dynamic_slice_in_dim(cross_gate, mp_index * local_heads, local_heads))

    bias = jnp.where(text_ids[None, :] < lengths[:, None], 0.0, NEG).astype(F32)
    bias = jnp.concatenate([bias, bias[:1]], axis=0)

    def project(tie):
        qkv_pre = mm(tie(first_low), qkv_full, NN)
        prepared = whole(
            prep_kernel,
            [((3 * seq_len, local_width), BF)],
            20 * seq_len * 3 * local_width,
            qkv_pre,
            local_gains,
            cos[:seq_len],
            sin[:seq_len],
        )
        return qkv_pre, prepared

    part_sets = near_sets // NEAR_PARTS
    part_rows = part_sets * seq_len

    def project_near(tie, k):
        pre = [mm(tie(slot), qkv_full[:, local_width:], NN) for slot in near_chains[k].result]
        there = slice(seq_len + k * part_rows, seq_len + (k + 1) * part_rows)
        return prepare_near(pre, local_gains, cos[there], sin[there], part_sets)

    (qkv_pre, prepared), near_first = links.stage(
        text_sum, *near_chains, work=lambda tie: (project(tie), project_near(tie, 0))
    )
    query = prepared[:seq_len]
    links.finish(text_sum)
    text_pre = jnp.concatenate(text_sum.result, axis=1)
    text_set = whole(
        text_prep_kernel,
        [((2 * text_len, local_width), BF)],
        20 * text_len * 2 * local_width,
        text_pre,
        local_gains,
    )
    text_sets_chain = Chain(send_sets(text_set, is_odd))
    near_second = links.stage(
        text_sets_chain, *near_chains, work=lambda tie: project_near(tie, 1)
    )
    links.finish(*near_chains)
    near_third = links.stage(text_sets_chain, work=lambda tie: project_near(tie, 2))
    self_sets = [prepared[seq_len:], near_first, near_second, near_third]

    def attend_self(tie):
        return attend(
            self_forward_kernel, [live], [tie(query)], [], self_sets, [(seq_len, F32)] * 2, 2, 2
        )

    out_self, log_self = links.stage(text_sets_chain, work=attend_self)
    text_sets = text_sets_chain.result

    def attend_text(tie):
        attn_low, out_text, log_text = attend(
            text_forward_kernel,
            [live, tanh_gate],
            [tie(query), out_self],
            [bias],
            text_sets,
            [(seq_len, BF), (seq_len, F32), (seq_len, F32)],
            2,
            2,
        )
        return attn_low, out_text, log_text

    attn_low, out_text, log_text = links.stage(work=attend_text)
    attn_rows = sum_to_mp(mm(attn_low, proj_full, NT))
    middle, middle_pull = jax.vjp(gated_add, attn_rows, gains[1], gate_attn, act_rows)
    second_in, second_pull = jax.vjp(modulate, middle, gains[2], scale_ffn)
    second_low = rows_from_mp(second_in.astype(BF))
    ffn_pre = mm(second_low, ffn_full, NN)
    hidden_f, swiglu_pull = jax.vjp(swiglu, ffn_pre[:, :units], ffn_pre[:, units:])
    hidden_low = hidden_f.astype(BF)
    ffn_rows = sum_to_mp(mm(hidden_low, down_full, NT))
    result, result_pull = jax.vjp(gated_add, ffn_rows, gains[3], gate_ffn, middle)


    grad_out = cotangent.astype(F32)
    grad_ffn_rows, grad_gain_four, grad_gate_ffn, grad_middle_a = result_pull(grad_out)
    grad_ffn_all = rows_from_mp(grad_ffn_rows.astype(BF))
    grad_hidden = mm(grad_ffn_all, down_full, NN)
    grad_gate_pre, grad_up_pre = swiglu_pull(grad_hidden)
    grad_pre_low = jnp.concatenate([grad_gate_pre, grad_up_pre], axis=1).astype(BF)
    second_part = mm(grad_pre_low, ffn_full, NT).astype(BF)

    def ffn_backward(tie):
        grad_second = sum_to_mp(second_part)
        terms = [mm(second_low, grad_pre_low, TN), mm(grad_ffn_all, hidden_low, TN)]
        return grad_second, jnp.concatenate([term.astype(BF) for term in terms], axis=1)

    grad_second, ffn_terms = links.stage(work=ffn_backward)
    ffn_sum = lax.psum_scatter(ffn_terms, "dp", scatter_dimension=0, tiled=True)
    grad_middle_b, grad_gain_three, grad_scale_ffn = second_pull(grad_second)
    grad_attn_rows, grad_gain_two, grad_gate_attn, grad_act_a = middle_pull(
        grad_middle_a + grad_middle_b
    )
    grad_attn_all = links.stage(
        work=lambda tie: rows_from_mp(tie(grad_attn_rows.astype(BF)))
    )

    def text_backward(tie):
        grad_attn_low = mm(tie(grad_attn_all), proj_full, NN).astype(BF)
        return grad_attn_low, attend(
            text_backward_kernel,
            [live, tanh_gate],
            [query, grad_attn_low, out_text, log_text],
            [bias.T],
            text_sets,
            [(2 * text_len, BF)] * len(text_sets) + [(seq_len, F32), (8, F32)],
            5,
            1,
        )

    def self_backward(tie):
        return attend(
            self_backward_kernel,
            [live],
            [query, tie(grad_attn_low), out_self, log_self],
            [],
            self_sets,
            [(2 * seq_len, BF)] * (near_sets + 1) + [(seq_len, F32)],
            5,
            1,
        )

    grad_attn_low, text_grads = links.stage(work=text_backward)
    gate_dots = text_grads[-1]
    text_return = Chain(return_sets(text_grads[: len(text_sets)], is_odd))
    self_grads = links.stage(text_return, work=self_backward)
    self_return = Chain(return_sets(self_grads[:-1], is_odd))

    def query_backward(tie):
        grad_query_low, head_query = whole(
            query_back_kernel,
            [((seq_len, local_width), BF), ((8, local_width), F32)],
            20 * seq_len * local_width,
            qkv_pre,
            local_gains,
            cos[:seq_len],
            sin[:seq_len],
            tie(self_grads[-1]),
            text_grads[-2],
        )
        return (
            grad_query_low,
            head_query,
            mm(first_low, grad_query_low, TN).astype(BF),
            mm(grad_attn_all, attn_low, TN).astype(BF),
        )

    grad_query_low, head_query, grad_query_weight, grad_proj = links.stage(
        text_return, self_return, work=query_backward
    )

    links.stage(text_return, self_return)
    own_text = text_return.result

    def text_rows_backward(tie):
        return whole(
            text_back_kernel,
            [((text_len, 2 * local_width), BF), ((8, local_width), F32)],
            20 * text_len * 2 * local_width,
            text_pre,
            local_gains,
            tie(own_text),
        )

    grad_text_low, head_text = text_rows_backward(lambda value: value)
    text_back = Chain(
        gather_blocks([grad_text_low[:, :local_width], grad_text_low[:, local_width:]], dp_index)
    )
    links.finish_only(self_return, (text_back,))
    own_self, ffn_sum = lax.optimization_barrier((self_return.result, ffn_sum))

    def key_backward(tie):
        grad_key_low, head_key = whole(
            key_back_kernel,
            [((seq_len, 2 * local_width), BF), ((8, local_width), F32)],
            20 * seq_len * 2 * local_width,
            qkv_pre,
            local_gains,
            cos[:seq_len],
            sin[:seq_len],
            tie(own_self),
        )
        first_part = mm(grad_query_low, qkv_full[:, :local_width], NT) + mm(
            grad_key_low, qkv_full[:, local_width:], NT
        )
        return grad_key_low, head_key, first_part.astype(BF)

    def blocks(value):
        return value.reshape(dp_count, shard, local_width)

    def sum_rows(tie):
        first_blocks = [first_part[k * row_count : (k + 1) * row_count] for k in range(mp_count)]
        moved = swap(first_blocks[3], "mp", 1)
        far_rows = plus(first_blocks[2], moved).astype(BF)
        grad_first = plus(first_blocks[0], swap(first_blocks[1], "mp", 1), swap(far_rows, "mp", 2))
        grad_keys = mm(first_low, after(grad_key_low, far_rows), TN).astype(BF)
        terms = [
            grad_query_weight,
            grad_keys[:, :local_width],
            grad_keys[:, local_width:],
            grad_proj,
        ]
        terms = jnp.stack([blocks(term) for term in terms], axis=1)
        attn_terms.append(terms.reshape(-1, shard, local_width))
        return grad_first

    grad_key_low, head_key, first_part = links.stage(text_back, work=key_backward)
    attn_terms = []
    grad_first = links.stage(text_back, work=sum_rows)
    attn_sum = lax.psum_scatter(attn_terms[0], "dp", scatter_dimension=0, tiled=True)
    grad_act_b, grad_gain_one, grad_scale_attn = first_pull(grad_first)
    grad_tokens = grad_act_a + grad_act_b
    mod_grads = jnp.stack([grad_scale_attn, grad_gate_attn, grad_scale_ffn, grad_gate_ffn])
    links.finish(text_back)
    text_rows = jnp.concatenate(text_back.result, axis=1)

    def gather_mod_grads(tie):
        mod_sum = sum_all(tie(mod_grads), "mp")
        mine = jnp.arange(mp_count)[:, None] == mp_index
        grad_mod_low = jnp.sum(jnp.where(mine, mod_sum, 0.0), axis=0)[None].astype(BF)
        return grad_mod_low, gather_in_order(grad_mod_low, "dp", dp_index)

    caption_part = mm(text_rows, text_matrix, NT).astype(BF)
    caption_part = caption_part.reshape(dp_count, mp_count, quarter_rows, text_shard)
    caption_part = jnp.transpose(caption_part, (1, 0, 2, 3)).reshape(-1, text_shard)
    (grad_mod_low, grad_mod_all), caption_mine = links.stage(
        work=lambda tie: (gather_mod_grads(tie), sum_to_mp(caption_part).astype(BF))
    )

    row_grads = jnp.stack([grad_gain_one, grad_gain_two, grad_gain_three, grad_gain_four])
    grad_ada = mm(cond_mine, grad_mod_all, TN) * weight_scale
    cond_part = mm(grad_mod_all, ada_weight, NT)
    zeros = functools.partial(jnp.zeros, dtype=F32)
    cond_rows = lax.dynamic_update_slice_in_dim(
        zeros((dp_count, width)), cond_part, dp_index * shard, 1
    )
    head_local = jnp.concatenate([head_query[:1], head_key[:1], head_text[:1]], axis=0)
    head_rows = lax.dynamic_update_slice_in_dim(
        zeros((3, width)), head_local, mp_index * local_width, 1
    )
    bias_rows = jnp.where(
        jnp.arange(mp_count)[:, None] == mp_index, grad_mod_low.astype(F32), 0.0
    )
    gate_local = gate_dots[0].reshape(local_heads, HD)[:, 0] * (1.0 - tanh_gate * tanh_gate)
    gate_row = lax.dynamic_update_slice_in_dim(
        zeros((1, width)), gate_local[None], mp_index * local_heads, 1
    )
    parts = [row_grads, head_rows, bias_rows, gate_row, cond_rows]
    count = sum(part.shape[0] for part in parts)
    small, start = 0.0, 0
    for part in parts:
        end = start + part.shape[0]
        small = small + jnp.pad(part, ((start, count - end), (0, 0)))
        start = end
    block = text_dim // mp_count

    def sum_small():
        value = yield from chain_sum(small, "mp")
        return (yield from chain_sum(value, "dp"))

    def send_captions():
        columns = yield from exchange_blocks(
            caption_mine.reshape(dp_count, quarter_rows, text_shard), dp_index
        )
        columns = jnp.transpose(columns, (1, 0, 2)).reshape(quarter_rows, text_dim)
        pieces = [
            lax.dynamic_slice_in_dim(columns, (mp_index ^ k) * block, block, axis=1)
            for k in range(mp_count)
        ]
        moved = yield [(pieces[k], "mp", swap_pairs("mp", k)) for k in range(1, mp_count)]
        return [pieces[0]] + list(moved)

    small_chain, caption_back = Chain(sum_small()), Chain(send_captions())
    links.finish(small_chain, caption_back)
    small = small_chain.result
    grad_caption = jnp.zeros((text_len, block), F32)
    for k, piece in enumerate(caption_back.result):
        grad_caption = lax.dynamic_update_slice_in_dim(
            grad_caption, piece.astype(F32), (mp_index ^ k) * quarter_rows, 0
        )
    grad_text = mm(text_all, text_rows, TN) * weight_scale
    ffn_sum = ffn_sum.astype(F32) * weight_scale
    attn_sum = attn_sum.astype(F32) * weight_scale
    cond_width = width // mp_count
    cond_sum = lax.dynamic_slice(small[12:], (dp_index, mp_index * cond_width), (1, cond_width))
    cond_cols = lax.dynamic_slice_in_dim(condition, mp_index * cond_width, cond_width, axis=1)
    silu_vals, silu_pull = jax.vjp(jax.nn.silu, cond_cols)
    grad_condition = silu_pull(cond_sum)[0] * (1.0 / math.sqrt(seq_len))
    scaled = small[:12] * weight_scale

    def parted(values, parts):
        return jnp.transpose(values.reshape(values.shape[0], parts, -1), (1, 0, 2))

    return (
        result.astype(BF),
        grad_tokens,
        grad_caption[None],
        grad_condition,
        attn_sum[:3],
        attn_sum[3].T,
        parted(grad_text, 2),
        parted(ffn_sum[:, : 2 * units], 2),
        ffn_sum[:, 2 * units :].T,
        grad_ada,
        scaled[:4],
        scaled[4:7],
        scaled[7:11].reshape(-1),
        scaled[11, :HEADS],
    )


def solution(mesh):
    return jax.shard_map(
        local,
        mesh=mesh,
        in_specs=(
            P(("dp", "mp"), None),
            P("dp", None, None),
            P("dp", None),
            P(("dp", "mp"), None),
            P(None, "dp", "mp"),
            P("mp", "dp"),
            P(None, "dp", "mp"),
            P(None, "dp", "mp"),
            P("mp", "dp"),
            P("dp", "mp"),
            P(),
            P(),
            P(),
            P(),
            P(),
            P(),
            P(),
        ),
        out_specs=(
            P(("dp", "mp"), None),
            P(("dp", "mp"), None),
            P("dp", None, "mp"),
            P("dp", "mp"),
            P(None, "dp", "mp"),
            P("mp", "dp"),
            P(None, "dp", "mp"),
            P(None, "dp", "mp"),
            P("mp", "dp"),
            P("dp", "mp"),
            P(),
            P(),
            P(),
            P(),
        ),
        check_vma=False,
    )
```

```python
import functools
import math

import jax
import jax.numpy as jnp
from jax import lax
from jax.experimental import pallas as pl
from jax.experimental.pallas import tpu as pltpu
from jax.sharding import PartitionSpec as P

HEADS = 24
HD = 64
PAIR = 2 * HD
NEAR_PARTS = 3
EPS = 1e-06
NEG = -1e30
SCALE = HD ** (-0.5)
BF = jnp.bfloat16
F32 = jnp.float32
NN = (((1,), (0,)), ((), ()))
NT = (((1,), (1,)), ((), ()))
TN = (((0,), (0,)), ((), ()))


def mm(left, right, dims):
    return lax.dot_general(left, right, dims, preferred_element_type=F32)


def swap(value, axis, bit):
    count = lax.axis_size(axis)
    return lax.ppermute(value, axis, [(i, i ^ bit) for i in range(count)])


def all_bits(count):
    return [1 << k for k in range(count.bit_length() - 1)]


def after(value, *others):
    return lax.optimization_barrier((value,) + others)[0]


class Chain:
    def __init__(self, steps):
        self.steps, self.result = steps, None
        self.advance(None)

    def advance(self, arrived):
        try:
            self.wanted = self.steps.send(arrived)
        except StopIteration as end:
            self.wanted, self.result = None, end.value


class Links:
    def __init__(self):
        self.last = ()

    def stage(self, *chains, work=None):
        active = [chain for chain in chains if chain.wanted is not None]
        wanted = [item for chain in active for item in chain.wanted]
        values = [value for value, _, _ in wanted]
        if self.last and values:
            values = lax.optimization_barrier(tuple(values) + self.last)[: len(values)]
        moved = [
            lax.ppermute(value, axis, pairs) for value, (_, axis, pairs) in zip(values, wanted)
        ]
        made = work(lambda value: after(value, *self.last)) if work else ()
        moved, made = lax.optimization_barrier((moved, made))
        self.last = tuple(moved[:1]) or tuple(jax.tree.leaves(made)[:1])
        for chain in active:
            count = len(chain.wanted)
            chain.advance(moved[:count])
            moved = moved[count:]
        return made

    def finish_only(self, chain, others):
        while chain.wanted is not None:
            self.stage(chain, *others)

    def finish(self, *chains):
        while any(chain.wanted is not None for chain in chains):
            self.stage(*chains)


def swap_pairs(axis, bit):
    return [(i, i ^ bit) for i in range(lax.axis_size(axis))]


def crossed_bits():
    bits = all_bits(lax.axis_size("dp"))
    return bits, bits[1::-1] + bits[2:]


def bit_axis(bits, bit):
    return sum(other > bit for other in bits)


def in_order(high, own, other, axis):
    return jnp.stack([jnp.where(high, other, own), jnp.where(high, own, other)], axis=axis)


def halves(high, value, axis):
    zero, one = [lax.index_in_dim(value, k, axis, keepdims=False) for k in range(2)]
    return jnp.where(high, zero, one), jnp.where(high, one, zero)


def gather_blocks(pair, index):
    orders = [bits[::-1] for bits in crossed_bits()]
    values, done = list(pair), ([], [])
    for bits in zip(*orders):
        moved = yield [(value, "dp", swap_pairs("dp", bit)) for value, bit in zip(values, bits)]
        for side, bit in enumerate(bits):
            axis = bit_axis(done[side], bit)
            values[side] = in_order((index & bit) != 0, values[side], moved[side], axis)
            done[side].append(bit)
    return [value.reshape((-1,) + own.shape[1:]) for value, own in zip(values, pair)]


def scatter_blocks(pair, index):
    orders = crossed_bits()
    left = [list(bits) for bits in orders]
    values = [value.reshape((2,) * len(orders[0]) + value.shape[1:]) for value in pair]
    for bits in zip(*orders):
        sent, kept = [], []
        for side, bit in enumerate(bits):
            parts = halves((index & bit) != 0, values[side], bit_axis(left[side], bit))
            sent.append((parts[0].astype(BF), "dp", swap_pairs("dp", bit)))
            kept.append(parts[1])
            left[side].remove(bit)
        moved = yield sent
        values = [plus(own, other) for own, other in zip(kept, moved)]
    return values


def exchange_blocks(value, index):
    count = value.shape[0]
    bits, left, done = all_bits(count), all_bits(count), []
    shape = value.shape[1:]
    value = value.reshape((2,) * len(bits) + shape)
    for bit in bits:
        high = (index & bit) != 0
        sent, kept = halves(high, value, bit_axis(left, bit))
        left.remove(bit)
        (moved,) = yield [(sent, "dp", swap_pairs("dp", bit))]
        value = in_order(high, kept, moved, len(left) + bit_axis(done, bit))
        done.append(bit)
    return value.reshape((count,) + shape)


def plus(*values):
    return sum(value.astype(F32) for value in values)


def sum_all(value, axis):
    bit = 1
    while bit < lax.axis_size(axis):
        value = value + swap(value, axis, bit)
        bit *= 2
    return value


def gather_in_order(value, axis, index):
    bit = 1
    while bit < lax.axis_size(axis):
        other = swap(value, axis, bit)
        high = (index & bit) != 0
        value = jnp.concatenate(
            [jnp.where(high, other, value), jnp.where(high, value, other)], axis=0
        )
        bit *= 2
    return value


def chain_sum(value, axis):
    for bit in all_bits(lax.axis_size(axis)):
        (other,) = yield [(value, axis, swap_pairs(axis, bit))]
        value = value + other
    return value


def rows_from_mp(value, axis=0):
    far = swap(value, "mp", 2)
    near = swap(value, "mp", 1)
    return jnp.concatenate([value, near, far, swap(far, "mp", 1)], axis=axis)


def slots_from_mp(value):
    far, near = yield [(value, "mp", swap_pairs("mp", bit)) for bit in (2, 1)]
    (last,) = yield [(far, "mp", swap_pairs("mp", 1))]
    return [value, near, far, last]


def sum_to_mp(value):
    count = value.shape[0] // 4
    blocks = [value[k * count : (k + 1) * count] for k in range(4)]
    far = blocks[2].astype(F32) + swap(blocks[3].astype(BF), "mp", 1).astype(F32)
    near = blocks[0].astype(F32) + swap(blocks[1].astype(BF), "mp", 1).astype(F32)
    return near + swap(far.astype(BF), "mp", 2).astype(F32)


def shifted(steps, keep=lambda i: True):
    count = lax.axis_size("dp")
    return [(i, i + steps) for i in range(count) if keep(i) and 0 <= i + steps < count]


def even(i):
    return i % 2 == 0


def odd(i):
    return i % 2 == 1


def out_pairs():
    return shifted(-2, even) + shifted(2, odd)


def back_pairs():
    return shifted(2, even) + shifted(-2, odd)


def send_sets(own, is_odd):
    beside, low, high = yield [
        (own, "dp", swap_pairs("dp", 1)),
        (own, "dp", shifted(2)),
        (own, "dp", shifted(-2)),
    ]
    across, third = yield [
        (jnp.where(is_odd, low, high), "dp", swap_pairs("dp", 1)),
        (beside, "dp", out_pairs()),
    ]
    (fourth,) = yield [(across, "dp", back_pairs())]
    return [own, beside, low, high, across, third, fourth]


def set_offsets(is_odd):
    return jnp.where(
        is_odd, jnp.asarray([0, -1, -2, 2, 1, -3, 3]), jnp.asarray([0, 1, -2, 2, -1, 3, -3])
    )


def return_sets(grads, is_odd):
    own, beside, low, high, across, third, fourth = grads
    (fourth,) = yield [(fourth, "dp", out_pairs())]
    across, third = yield [
        (plus(across, fourth).astype(BF), "dp", swap_pairs("dp", 1)),
        (third, "dp", back_pairs()),
    ]
    low = plus(low, jnp.where(is_odd, across, 0)).astype(BF)
    high = plus(high, jnp.where(is_odd, 0, across)).astype(BF)
    beside, low, high = yield [
        (plus(beside, third).astype(BF), "dp", swap_pairs("dp", 1)),
        (low, "dp", shifted(-2)),
        (high, "dp", shifted(2)),
    ]
    return plus(own, beside, low, high)


def norm_rows(values, weights):
    return values * lax.rsqrt(jnp.mean(values * values, axis=-1, keepdims=True) + EPS) * weights


def modulate(values, weights, scales):
    return norm_rows(values, weights) * (1.0 + scales)


def gated_add(branch, weights, gates, resid):
    return resid + jnp.tanh(gates) * norm_rows(branch, weights)


def swiglu(gate_pre, up_pre):
    return jax.nn.silu(gate_pre) * up_pre


def lanes(rows):
    return lax.broadcasted_iota(jnp.int32, (rows, PAIR), 1)


def head_sum(values):
    low = lanes(values.shape[0]) < HD
    first = jnp.sum(jnp.where(low, values, 0.0), axis=-1, keepdims=True)
    second = jnp.sum(jnp.where(low, 0.0, values), axis=-1, keepdims=True)
    return jnp.where(low, first, second)


def partner(values):
    quarter = HD // 4
    first = (lanes(values.shape[0]) % (2 * quarter)) < quarter
    return jnp.where(
        first, pltpu.roll(values, PAIR - quarter, 1), pltpu.roll(values, quarter, 1)
    )


def normed(values):
    return values * lax.rsqrt(head_sum(values * values) / HD + EPS)


def prep_kernel(pre_ref, gains_ref, cos_ref, sin_ref, out_ref):
    width = out_ref.shape[1]
    rows = pre_ref.shape[0]
    cos, sin = cos_ref[...], sin_ref[...]
    for part in range(2):
        for start in range(0, width, PAIR):
            here = pl.ds(part * width + start, PAIR)
            turned = normed(pre_ref[:, here]) * gains_ref[part : part + 1, pl.ds(start, PAIR)]
            if part == 0:
                turned = turned * cos + partner(turned) * sin
                out_ref[pl.ds(0, rows), pl.ds(start, PAIR)] = turned.astype(BF)
            else:
                turned = turned * cos + partner(turned) * sin
                out_ref[pl.ds(rows, rows), pl.ds(start, PAIR)] = turned.astype(BF)
    out_ref[pl.ds(2 * rows, rows), :] = pre_ref[:, pl.ds(2 * width, width)].astype(BF)


def near_prep_kernel(gains_ref, cos_ref, sin_ref, *refs):
    *pre_refs, out_ref = refs
    rows, width = pre_refs[0].shape[0], out_ref.shape[1]
    depth = rows * len(pre_refs)
    for slot, pre_ref in enumerate(pre_refs):
        there = pl.ds(slot * rows, rows)
        cos, sin = cos_ref[there, :], sin_ref[there, :]
        for start in range(0, width, PAIR):
            here = pl.ds(start, PAIR)
            turned = normed(pre_ref[:, here]) * gains_ref[1:2, here]
            turned = turned * cos + partner(turned) * sin
            out_ref[there, here] = turned.astype(BF)
        out_ref[pl.ds(depth + slot * rows, rows), :] = pre_ref[:, pl.ds(width, width)].astype(BF)


def text_prep_kernel(pre_ref, gains_ref, out_ref):
    rows, width = pre_ref.shape[0], out_ref.shape[1]
    for start in range(0, width, PAIR):
        here = pl.ds(start, PAIR)
        value = normed(pre_ref[:, here]) * gains_ref[2:3, here]
        out_ref[pl.ds(0, rows), here] = value.astype(BF)
    out_ref[pl.ds(rows, rows), :] = pre_ref[:, pl.ds(width, width)].astype(BF)


def norm_back(pre, gains, grad):
    ratio = lax.rsqrt(head_sum(pre * pre) / HD + EPS)
    scaled = grad * gains
    grad_pre = ratio * scaled - pre * (ratio * ratio * ratio) * (head_sum(pre * scaled) / HD)
    return grad_pre, jnp.sum(grad * pre * ratio, axis=0, keepdims=True)


def query_back_kernel(pre_ref, gains_ref, cos_ref, sin_ref, self_ref, text_ref, out_ref, head_ref):
    cos, sin = cos_ref[...], sin_ref[...]
    head_ref[...] = jnp.zeros_like(head_ref)
    for start in range(0, out_ref.shape[1], PAIR):
        here = pl.ds(start, PAIR)
        grad = self_ref[:, here] + text_ref[:, here]
        grad = grad * cos - partner(grad) * sin
        grad_pre, grad_gain = norm_back(pre_ref[:, here], gains_ref[0:1, here], grad)
        out_ref[:, here] = grad_pre.astype(BF)
        head_ref[0:1, here] = grad_gain


def key_back_kernel(pre_ref, gains_ref, cos_ref, sin_ref, set_ref, out_ref, head_ref):
    rows, width = pre_ref.shape[0], set_ref.shape[1]
    cos, sin = cos_ref[...], sin_ref[...]
    head_ref[...] = jnp.zeros_like(head_ref)
    for start in range(0, width, PAIR):
        here = pl.ds(start, PAIR)
        grad = set_ref[pl.ds(0, rows), here]
        grad = grad * cos - partner(grad) * sin
        grad_pre, grad_gain = norm_back(
            pre_ref[:, pl.ds(width + start, PAIR)], gains_ref[1:2, here], grad
        )
        out_ref[:, here] = grad_pre.astype(BF)
        head_ref[0:1, here] = grad_gain
    out_ref[:, pl.ds(width, width)] = set_ref[pl.ds(rows, rows), :].astype(BF)


def text_back_kernel(pre_ref, gains_ref, set_ref, out_ref, head_ref):
    rows, width = pre_ref.shape[0], set_ref.shape[1]
    head_ref[...] = jnp.zeros_like(head_ref)
    for start in range(0, width, PAIR):
        here = pl.ds(start, PAIR)
        grad_pre, grad_gain = norm_back(
            pre_ref[:, here], gains_ref[2:3, here], set_ref[pl.ds(0, rows), here]
        )
        out_ref[:, here] = grad_pre.astype(BF)
        head_ref[0:1, here] = grad_gain
    out_ref[:, pl.ds(width, width)] = set_ref[pl.ds(rows, rows), :].astype(BF)


def split_pair(values):
    low = lanes(values.shape[0]) < HD
    zero = jnp.zeros_like(values)
    return jnp.where(low, values, zero), jnp.where(low, zero, values)


def forward_sums(live_ref, query_ref, set_refs, bias_ref, total, weight):
    low = lanes(query_ref.shape[0]) < HD
    total[...] = jnp.zeros_like(total)
    weight[...] = jnp.zeros_like(weight)
    for index, source in enumerate(set_refs):

        @pl.when(live_ref[index] > 0)
        def _(index=index, source=source):
            depth = source.shape[0] // 2
            keys, values = source[pl.ds(0, depth), :], source[pl.ds(depth, depth), :]
            outs, sums = [], []
            for query in split_pair(query_ref[...] * jnp.asarray(SCALE, BF)):
                logits = mm(query, keys, NT)
                if bias_ref is not None:
                    logits = logits + bias_ref[index : index + 1, :]
                probs = jnp.exp(logits)
                sums.append(jnp.sum(probs, axis=-1, keepdims=True))
                outs.append(mm(probs.astype(BF), values, NN))
            total[...] += jnp.where(low, outs[0], outs[1])
            weight[...] += jnp.where(low, sums[0], sums[1])


def views(own_ref, near_refs):
    depth = own_ref.shape[0]
    return [own_ref] + [
        near_ref.at[pl.ds(start, depth), :]
        for near_ref in near_refs
        for start in range(0, near_ref.shape[0], depth)
    ]


def self_forward_kernel(live_ref, query_ref, own_ref, *refs):
    *near_refs, out_ref, log_ref, total, weight = refs
    set_refs = views(own_ref, near_refs)
    forward_sums(live_ref, query_ref, set_refs, None, total, weight)
    out_ref[...] = total[...] / weight[...]
    log_ref[...] = jnp.log(weight[...])


def text_forward_kernel(live_ref, gate_ref, query_ref, self_ref, bias_ref, *refs):
    *set_refs, attn_ref, out_ref, log_ref, total, weight = refs
    forward_sums(live_ref, query_ref, set_refs, bias_ref, total, weight)
    low = lanes(query_ref.shape[0]) < HD
    pair = pl.program_id(0)
    gate = jnp.where(low, gate_ref[2 * pair], gate_ref[2 * pair + 1])
    out = total[...] / weight[...]
    attn_ref[...] = (self_ref[...] + gate * out).astype(BF)
    out_ref[...] = out
    log_ref[...] = jnp.log(weight[...])


def backward_sums(live_ref, query_ref, grad_ref, log_ref, delta, bias_ref, gates, refs, total):
    count = len(refs) // 2
    low = lanes(query_ref.shape[0]) < HD
    logs_all, delta_all = jnp.transpose(log_ref[...]), jnp.transpose(delta)
    total[...] = jnp.zeros_like(total)
    for index, (source, out_ref) in enumerate(zip(refs[:count], refs[count:])):

        @pl.when(live_ref[index] > 0)
        def _(index=index, source=source, out_ref=out_ref):
            queries = split_pair(query_ref[...] * jnp.asarray(SCALE, BF))
            grads = split_pair(grad_ref[...])
            depth = source.shape[0] // 2
            keys, values = source[pl.ds(0, depth), :], source[pl.ds(depth, depth), :]
            grad_query, grad_key, grad_value = [], [], []
            for head in range(2):
                row = head * HD
                logits = mm(keys, queries[head], NT)
                if bias_ref is not None:
                    logits = logits + bias_ref[:, index : index + 1]
                probs = jnp.exp(logits - logs_all[row : row + 1, :])
                value_part = mm(probs.astype(BF), grads[head], NN)
                grad_probs = mm(values, grads[head], NT)
                if gates is not None:
                    value_part = value_part * gates[head]
                    grad_probs = grad_probs * gates[head]
                grad_logits = (probs * (grad_probs - delta_all[row : row + 1, :])).astype(BF)
                grad_value.append(value_part)
                grad_key.append(mm(grad_logits, queries[head], NN))
                grad_query.append(mm(grad_logits, keys, TN))
            total[...] += jnp.where(low, grad_query[0], grad_query[1])
            out_ref[pl.ds(0, depth), :] = (grad_key[0] + grad_key[1]).astype(BF)
            out_ref[pl.ds(depth, depth), :] = (grad_value[0] + grad_value[1]).astype(BF)

        @pl.when(live_ref[index] == 0)
        def _(out_ref=out_ref):
            out_ref[...] = jnp.zeros_like(out_ref)


def self_backward_kernel(
    live_ref, query_ref, grad_ref, out_ref, log_ref, own_ref, *refs
):
    near_refs, grad_refs = refs[:NEAR_PARTS], list(refs[NEAR_PARTS:-2])
    query_grad_ref, total = refs[-2:]
    set_refs = views(own_ref, near_refs) + grad_refs
    delta = head_sum(grad_ref[...].astype(F32) * out_ref[...])
    backward_sums(live_ref, query_ref, grad_ref, log_ref, delta, None, None, set_refs, total)
    query_grad_ref[...] = total[...] * SCALE


def text_backward_kernel(
    live_ref, gate_ref, query_ref, grad_ref, out_ref, log_ref, bias_ref, *refs
):
    *set_refs, query_grad_ref, gate_grad_ref, total = refs
    low = lanes(query_ref.shape[0]) < HD
    pair = pl.program_id(0)
    gates = (gate_ref[2 * pair], gate_ref[2 * pair + 1])
    dots = head_sum(grad_ref[...].astype(F32) * out_ref[...])
    gate_grad_ref[...] = jnp.broadcast_to(jnp.sum(dots, axis=0, keepdims=True), gate_grad_ref.shape)
    delta = jnp.where(low, gates[0], gates[1]) * dots
    backward_sums(live_ref, query_ref, grad_ref, log_ref, delta, bias_ref, gates, set_refs, total)
    query_grad_ref[...] = total[...] * SCALE


def params(limit=40):
    return pltpu.CompilerParams(vmem_limit_bytes=limit * 2**20)


def whole(kernel, outs, cost, *args):
    shapes = [jax.ShapeDtypeStruct(shape, dtype) for shape, dtype in outs]
    return pl.pallas_call(
        kernel,
        out_shape=shapes if len(shapes) > 1 else shapes[0],
        compiler_params=params(),
        cost_estimate=pl.CostEstimate(flops=cost, bytes_accessed=2 * cost // 10, transcendentals=0),
    )(*args)


def column(rows):
    return pl.BlockSpec((rows, PAIR), lambda pair: (0, pair))


def fixed(shape):
    return pl.BlockSpec(shape, lambda pair: (0, 0))


def prepare_near(pre, gains, cos, sin, sets):
    rows, width = pre[0].shape[0] // sets, gains.shape[1]
    depth = rows * len(pre)

    def block(count, columns):
        return pl.BlockSpec((count, columns), lambda k: (k, 0))

    return pl.pallas_call(
        near_prep_kernel,
        grid=(sets,),
        in_specs=[pl.BlockSpec(gains.shape, lambda k: (0, 0))]
        + [block(depth, PAIR)] * 2
        + [block(rows, 2 * width)] * len(pre),
        out_specs=block(2 * depth, width),
        out_shape=jax.ShapeDtypeStruct((sets * 2 * depth, width), BF),
        compiler_params=params(),
        cost_estimate=pl.CostEstimate(
            flops=40 * sets * depth * width,
            bytes_accessed=12 * sets * depth * width,
            transcendentals=0,
        ),
    )(gains, cos, sin, *pre)


def attend(kernel, scalars, columns, bias, sets, outs, passes, scratch, limit=56):
    rows, width = columns[0].shape
    keys = sets[0].shape[0] // 2
    smem = pl.BlockSpec(memory_space=pltpu.SMEM)
    return pl.pallas_call(
        kernel,
        grid=(width // PAIR,),
        in_specs=[smem] * len(scalars)
        + [column(value.shape[0]) for value in columns]
        + [fixed(value.shape) for value in bias]
        + [column(value.shape[0]) for value in sets],
        out_specs=[column(depth) for depth, _ in outs],
        out_shape=[jax.ShapeDtypeStruct((depth, width), dtype) for depth, dtype in outs],
        scratch_shapes=[pltpu.VMEM((rows, PAIR), F32)] * scratch,
        compiler_params=params(limit),
        cost_estimate=pl.CostEstimate(
            flops=passes * 16 * rows * keys * width,
            bytes_accessed=40 * rows * width,
            transcendentals=4 * rows * keys * width // HD,
        ),
    )(*scalars, *columns, *bias, *sets)


def local(
    tokens,
    caption,
    condition,
    cotangent,
    qkv_weight,
    proj_weight,
    text_weight,
    ffn_weight,
    down_weight,
    ada_weight,
    norm_gains,
    head_gains,
    ada_bias,
    cross_gate,
    group_map,
    grid_width,
    caption_len,
):
    dp_count = lax.axis_size("dp")
    mp_count = lax.axis_size("mp")
    dp_index = lax.axis_index("dp")
    mp_index = lax.axis_index("mp")
    row_count, width = tokens.shape
    seq_len = row_count * mp_count
    local_width = qkv_weight.shape[2]
    local_heads = local_width // HD
    text_len, text_dim = caption.shape[1:]
    units = ffn_weight.shape[2]
    shard = qkv_weight.shape[1]
    weight_scale = 1.0 / math.sqrt(seq_len * dp_count)
    is_odd = (dp_index % 2) == 1
    links = Links()

    qkv_shard = jnp.transpose(qkv_weight, (1, 0, 2)).reshape(shard, 3 * local_width)
    rest_shard = jnp.concatenate(
        [proj_weight.T, jnp.transpose(ffn_weight, (1, 0, 2)).reshape(shard, 2 * units), down_weight.T],
        axis=1,
    )
    qkv_full = lax.all_gather(qkv_shard, "dp", axis=0, tiled=True)
    rest = lax.all_gather(rest_shard, "dp", axis=0, tiled=True)
    cuts = (0, local_width, local_width + 2 * units, local_width + 3 * units)
    proj_full, ffn_full, down_full = [rest[:, low:high] for low, high in zip(cuts[:-1], cuts[1:])]

    text_shard = text_weight.shape[1]
    quarter_rows = text_len // mp_count
    my_rows = lax.dynamic_slice_in_dim(caption[0], mp_index * quarter_rows, quarter_rows, axis=0)
    text_matrix = jnp.transpose(text_weight, (1, 0, 2)).reshape(text_shard, 2 * local_width)
    my_rows = jnp.transpose(my_rows.reshape(quarter_rows, dp_count, text_shard), (1, 0, 2))

    def modulate_all():
        value = jax.nn.silu(condition).astype(BF)
        for bit in all_bits(dp_count):
            (other,) = yield [(value, "dp", swap_pairs("dp", bit))]
            value = in_order((dp_index & bit) != 0, value, other, 0).reshape(2 * bit, width)
        cond_mine = lax.dynamic_slice_in_dim(value, dp_index * shard, shard, axis=1)
        value = mm(cond_mine, ada_weight, NN)
        for bit in all_bits(dp_count):
            (other,) = yield [(value, "dp", swap_pairs("dp", bit))]
            value = value + other
        bias_part = lax.dynamic_slice_in_dim(ada_bias, mp_index * width, width)
        value = (value + bias_part[None, :])[None]
        for bit in all_bits(mp_count):
            (other,) = yield [(value, "mp", swap_pairs("mp", bit))]
            value = in_order((mp_index & bit) != 0, value, other, 0).reshape(2 * bit, dp_count, width)
        return cond_mine, value

    def caption_features():
        value = yield from exchange_blocks(my_rows, dp_index)
        far, near = yield [(value, "mp", swap_pairs("mp", bit)) for bit in (2, 1)]
        (last,) = yield [(far, "mp", swap_pairs("mp", 1))]
        return jnp.concatenate([value, near, far, last], axis=1)

    mod_chain, caption_chain = Chain(modulate_all()), Chain(caption_features())
    token_chain = Chain(send_sets(tokens, is_odd))
    links.finish(mod_chain, caption_chain, token_chain)
    cond_mine, modulation = mod_chain.result
    text_all = caption_chain.result.reshape(dp_count * text_len, text_shard)

    origins = dp_index + set_offsets(is_odd)
    chosen = jnp.arange(dp_count)[None, :] == origins[:, None]

    def looked_up(table):
        return jnp.sum(jnp.where(chosen, table[None, :], 0), axis=1)

    inside = (origins >= 0) & (origins < dp_count)
    first_slot = jnp.sum(jnp.where(jnp.arange(dp_count) == dp_index, group_map, 0))
    grid = jnp.sum(jnp.where(jnp.arange(dp_count) == dp_index, grid_width, 0))
    live = (inside & (looked_up(group_map) == first_slot)).astype(jnp.int32)
    lengths = looked_up(caption_len)

    near_scales = jnp.sum(
        jnp.where(chosen[1:, :, None], modulation[0][None], 0.0), axis=1
    )
    scale_attn, gate_attn, scale_ffn, gate_ffn = [
        lax.dynamic_index_in_dim(modulation, dp_index, 1, False)[k] for k in range(4)
    ]
    gains = [norm_gains[k] for k in range(4)]
    act_rows = tokens.astype(F32)
    first_in, first_pull = jax.vjp(modulate, act_rows, gains[0], scale_attn)
    near_tokens = jnp.stack(token_chain.result[1:]).astype(F32)
    near_in = modulate(near_tokens, gains[0], near_scales[:, None, :]).astype(BF)
    near_sets = near_in.shape[0]

    text_part = mm(text_all, text_matrix, NN).astype(BF)
    text_part = text_part.reshape(dp_count, text_len, 2 * local_width)
    text_sum = Chain(
        scatter_blocks([text_part[..., :local_width], text_part[..., local_width:]], dp_index)
    )
    first_chain = Chain(slots_from_mp(first_in.astype(BF)))
    near_chains = [
        Chain(slots_from_mp(near_in[k : k + 2].reshape(2 * row_count, width)))
        for k in range(0, near_sets, 2)
    ]
    links.stage(text_sum, first_chain, near_chains[0])
    links.stage(text_sum, first_chain, *near_chains[:2])
    first_low = jnp.concatenate(first_chain.result, axis=0)

    blocks = mp_index ^ jnp.arange(mp_count, dtype=jnp.int32)
    token_ids = (blocks[:, None] * row_count + jnp.arange(row_count, dtype=jnp.int32)).reshape(-1)
    text_ids = (blocks[:, None] * quarter_rows + jnp.arange(quarter_rows, dtype=jnp.int32)).reshape(-1)
    positions = ((origins - first_slot)[:, None] * seq_len + token_ids[None, :]).reshape(-1)
    quarter = HD // 4
    lane = jnp.arange(PAIR, dtype=jnp.int32)
    freqs = jnp.exp((lane % quarter).astype(F32) * (-math.log(10000.0) / quarter))
    place = jnp.where((lane % HD < HD // 2)[None, :], (positions // grid)[:, None], (positions % grid)[:, None])
    angles = place.astype(F32) * freqs[None, :]
    cos = jnp.cos(angles)
    sin = jnp.sin(angles) * jnp.where((lane % (2 * quarter)) < quarter, -1.0, 1.0)[None, :]
    local_gains = lax.dynamic_slice_in_dim(head_gains, mp_index * local_width, local_width, axis=1)
    tanh_gate = jnp.tanh(lax.dynamic_slice_in_dim(cross_gate, mp_index * local_heads, local_heads))

    bias = jnp.where(text_ids[None, :] < lengths[:, None], 0.0, NEG).astype(F32)
    bias = jnp.concatenate([bias, bias[:1]], axis=0)

    def project(tie):
        qkv_pre = mm(tie(first_low), qkv_full, NN)
        prepared = whole(
            prep_kernel,
            [((3 * seq_len, local_width), BF)],
            20 * seq_len * 3 * local_width,
            qkv_pre,
            local_gains,
            cos[:seq_len],
            sin[:seq_len],
        )
        return qkv_pre, prepared

    part_sets = near_sets // NEAR_PARTS
    part_rows = part_sets * seq_len

    def project_near(tie, k):
        pre = [mm(tie(slot), qkv_full[:, local_width:], NN) for slot in near_chains[k].result]
        there = slice(seq_len + k * part_rows, seq_len + (k + 1) * part_rows)
        return prepare_near(pre, local_gains, cos[there], sin[there], part_sets)

    (qkv_pre, prepared), near_first = links.stage(
        text_sum, *near_chains, work=lambda tie: (project(tie), project_near(tie, 0))
    )
    query = prepared[:seq_len]
    links.finish(text_sum)
    text_pre = jnp.concatenate(text_sum.result, axis=1)
    text_set = whole(
        text_prep_kernel,
        [((2 * text_len, local_width), BF)],
        20 * text_len * 2 * local_width,
        text_pre,
        local_gains,
    )
    text_sets_chain = Chain(send_sets(text_set, is_odd))
    near_second = links.stage(
        text_sets_chain, *near_chains, work=lambda tie: project_near(tie, 1)
    )
    links.finish(*near_chains)
    near_third = links.stage(text_sets_chain, work=lambda tie: project_near(tie, 2))
    self_sets = [prepared[seq_len:], near_first, near_second, near_third]

    def attend_self(tie):
        return attend(
            self_forward_kernel, [live], [tie(query)], [], self_sets, [(seq_len, F32)] * 2, 2, 2
        )

    out_self, log_self = links.stage(text_sets_chain, work=attend_self)
    text_sets = text_sets_chain.result

    def attend_text(tie):
        attn_low, out_text, log_text = attend(
            text_forward_kernel,
            [live, tanh_gate],
            [tie(query), out_self],
            [bias],
            text_sets,
            [(seq_len, BF), (seq_len, F32), (seq_len, F32)],
            2,
            2,
        )
        return attn_low, out_text, log_text

    attn_low, out_text, log_text = links.stage(work=attend_text)
    attn_rows = sum_to_mp(mm(attn_low, proj_full, NT))
    middle, middle_pull = jax.vjp(gated_add, attn_rows, gains[1], gate_attn, act_rows)
    second_in, second_pull = jax.vjp(modulate, middle, gains[2], scale_ffn)
    second_low = rows_from_mp(second_in.astype(BF))
    ffn_pre = mm(second_low, ffn_full, NN)
    hidden_f, swiglu_pull = jax.vjp(swiglu, ffn_pre[:, :units], ffn_pre[:, units:])
    hidden_low = hidden_f.astype(BF)
    ffn_rows = sum_to_mp(mm(hidden_low, down_full, NT))
    result, result_pull = jax.vjp(gated_add, ffn_rows, gains[3], gate_ffn, middle)


    grad_out = cotangent.astype(F32)
    grad_ffn_rows, grad_gain_four, grad_gate_ffn, grad_middle_a = result_pull(grad_out)
    grad_ffn_all = rows_from_mp(grad_ffn_rows.astype(BF))
    grad_hidden = mm(grad_ffn_all, down_full, NN)
    grad_gate_pre, grad_up_pre = swiglu_pull(grad_hidden)
    grad_pre_low = jnp.concatenate([grad_gate_pre, grad_up_pre], axis=1).astype(BF)
    second_part = mm(grad_pre_low, ffn_full, NT).astype(BF)

    def ffn_backward(tie):
        grad_second = sum_to_mp(second_part)
        terms = [mm(second_low, grad_pre_low, TN), mm(grad_ffn_all, hidden_low, TN)]
        return grad_second, jnp.concatenate([term.astype(BF) for term in terms], axis=1)

    grad_second, ffn_terms = links.stage(work=ffn_backward)
    ffn_sum = lax.psum_scatter(ffn_terms, "dp", scatter_dimension=0, tiled=True)
    grad_middle_b, grad_gain_three, grad_scale_ffn = second_pull(grad_second)
    grad_attn_rows, grad_gain_two, grad_gate_attn, grad_act_a = middle_pull(
        grad_middle_a + grad_middle_b
    )
    grad_attn_all = links.stage(
        work=lambda tie: rows_from_mp(tie(grad_attn_rows.astype(BF)))
    )

    def self_backward(tie):
        grad_attn_low = mm(tie(grad_attn_all), proj_full, NN).astype(BF)
        return grad_attn_low, attend(
            self_backward_kernel,
            [live],
            [query, grad_attn_low, out_self, log_self],
            [],
            self_sets,
            [(2 * seq_len, BF)] * (near_sets + 1) + [(seq_len, F32)],
            5,
            1,
        )

    def text_backward(tie):
        return attend(
            text_backward_kernel,
            [live, tanh_gate],
            [query, tie(grad_attn_low), out_text, log_text],
            [bias.T],
            text_sets,
            [(2 * text_len, BF)] * len(text_sets) + [(seq_len, F32), (8, F32)],
            5,
            1,
        )

    grad_attn_low, self_grads = links.stage(work=self_backward)
    self_return = Chain(return_sets(self_grads[:-1], is_odd))
    text_grads = links.stage(self_return, work=text_backward)
    gate_dots = text_grads[-1]
    text_return = Chain(return_sets(text_grads[: len(text_sets)], is_odd))

    def query_backward(tie):
        grad_query_low, head_query = whole(
            query_back_kernel,
            [((seq_len, local_width), BF), ((8, local_width), F32)],
            20 * seq_len * local_width,
            qkv_pre,
            local_gains,
            cos[:seq_len],
            sin[:seq_len],
            tie(self_grads[-1]),
            text_grads[-2],
        )
        return (
            grad_query_low,
            head_query,
            mm(first_low, grad_query_low, TN).astype(BF),
            mm(grad_attn_all, attn_low, TN).astype(BF),
        )

    grad_query_low, head_query, grad_query_weight, grad_proj = links.stage(
        text_return, self_return, work=query_backward
    )

    links.stage(text_return, self_return)
    own_self = self_return.result

    def key_backward(tie):
        grad_key_low, head_key = whole(
            key_back_kernel,
            [((seq_len, 2 * local_width), BF), ((8, local_width), F32)],
            20 * seq_len * 2 * local_width,
            qkv_pre,
            local_gains,
            cos[:seq_len],
            sin[:seq_len],
            tie(own_self),
        )
        first_part = mm(grad_query_low, qkv_full[:, :local_width], NT) + mm(
            grad_key_low, qkv_full[:, local_width:], NT
        )
        return grad_key_low, head_key, first_part.astype(BF)

    def blocks(value):
        return value.reshape(dp_count, shard, local_width)

    def sum_rows(tie):
        first_blocks = [first_part[k * row_count : (k + 1) * row_count] for k in range(mp_count)]
        moved = swap(first_blocks[3], "mp", 1)
        far_rows = plus(first_blocks[2], moved).astype(BF)
        grad_first = plus(first_blocks[0], swap(first_blocks[1], "mp", 1), swap(far_rows, "mp", 2))
        grad_keys = mm(first_low, after(grad_key_low, far_rows), TN).astype(BF)
        terms = [
            grad_query_weight,
            grad_keys[:, :local_width],
            grad_keys[:, local_width:],
            grad_proj,
        ]
        terms = jnp.stack([blocks(term) for term in terms], axis=1)
        attn_terms.append(terms.reshape(-1, shard, local_width))
        return grad_first

    grad_key_low, head_key, first_part = links.stage(text_return, work=key_backward)
    grad_text_low, head_text = whole(
        text_back_kernel,
        [((text_len, 2 * local_width), BF), ((8, local_width), F32)],
        20 * text_len * 2 * local_width,
        text_pre,
        local_gains,
        text_return.result,
    )
    text_back = Chain(
        gather_blocks([grad_text_low[:, :local_width], grad_text_low[:, local_width:]], dp_index)
    )
    attn_terms = []
    grad_first = links.stage(text_back, work=sum_rows)
    attn_sum = lax.psum_scatter(attn_terms[0], "dp", scatter_dimension=0, tiled=True)
    grad_act_b, grad_gain_one, grad_scale_attn = first_pull(grad_first)
    grad_tokens = grad_act_a + grad_act_b
    mod_grads = jnp.stack([grad_scale_attn, grad_gate_attn, grad_scale_ffn, grad_gate_ffn])
    def gather_mod_grads(tie):
        mod_sum = sum_all(tie(mod_grads), "mp")
        mine = jnp.arange(mp_count)[:, None] == mp_index
        grad_mod_low = jnp.sum(jnp.where(mine, mod_sum, 0.0), axis=0)[None].astype(BF)
        return grad_mod_low, gather_in_order(grad_mod_low, "dp", dp_index)

    grad_mod_low, grad_mod_all = links.stage(text_back, work=gather_mod_grads)

    row_grads = jnp.stack([grad_gain_one, grad_gain_two, grad_gain_three, grad_gain_four])
    grad_ada = mm(cond_mine, grad_mod_all, TN) * weight_scale
    cond_part = mm(grad_mod_all, ada_weight, NT)
    zeros = functools.partial(jnp.zeros, dtype=F32)
    cond_rows = lax.dynamic_update_slice_in_dim(
        zeros((dp_count, width)), cond_part, dp_index * shard, 1
    )
    head_local = jnp.concatenate([head_query[:1], head_key[:1], head_text[:1]], axis=0)
    head_rows = lax.dynamic_update_slice_in_dim(
        zeros((3, width)), head_local, mp_index * local_width, 1
    )
    bias_rows = jnp.where(
        jnp.arange(mp_count)[:, None] == mp_index, grad_mod_low.astype(F32), 0.0
    )
    gate_local = gate_dots[0].reshape(local_heads, HD)[:, 0] * (1.0 - tanh_gate * tanh_gate)
    gate_row = lax.dynamic_update_slice_in_dim(
        zeros((1, width)), gate_local[None], mp_index * local_heads, 1
    )
    parts = [row_grads, head_rows, bias_rows, gate_row, cond_rows]
    count = sum(part.shape[0] for part in parts)
    small, start = 0.0, 0
    for part in parts:
        end = start + part.shape[0]
        small = small + jnp.pad(part, ((start, count - end), (0, 0)))
        start = end
    block = text_dim // mp_count

    def sum_small():
        value = yield from chain_sum(small, "mp")
        return (yield from chain_sum(value, "dp"))

    def send_captions():
        columns = yield from exchange_blocks(
            caption_mine.reshape(dp_count, quarter_rows, text_shard), dp_index
        )
        columns = jnp.transpose(columns, (1, 0, 2)).reshape(quarter_rows, text_dim)
        pieces = [
            lax.dynamic_slice_in_dim(columns, (mp_index ^ k) * block, block, axis=1)
            for k in range(mp_count)
        ]
        moved = yield [(pieces[k], "mp", swap_pairs("mp", k)) for k in range(1, mp_count)]
        return [pieces[0]] + list(moved)

    small_chain = Chain(sum_small())
    links.stage(small_chain, text_back)
    links.finish(text_back)
    text_rows, ffn_sum = lax.optimization_barrier(
        (jnp.concatenate(text_back.result, axis=1), ffn_sum)
    )
    caption_part = mm(text_rows, text_matrix, NT).astype(BF)
    caption_part = caption_part.reshape(dp_count, mp_count, quarter_rows, text_shard)
    caption_part = jnp.transpose(caption_part, (1, 0, 2, 3)).reshape(-1, text_shard)
    caption_mine = links.stage(
        small_chain, work=lambda tie: sum_to_mp(caption_part).astype(BF)
    )
    caption_back = Chain(send_captions())
    links.finish(small_chain, caption_back)
    small = small_chain.result
    grad_caption = jnp.zeros((text_len, block), F32)
    for k, piece in enumerate(caption_back.result):
        grad_caption = lax.dynamic_update_slice_in_dim(
            grad_caption, piece.astype(F32), (mp_index ^ k) * quarter_rows, 0
        )
    grad_text = mm(text_all, text_rows, TN) * weight_scale
    ffn_sum = ffn_sum.astype(F32) * weight_scale
    attn_sum = attn_sum.astype(F32) * weight_scale
    cond_width = width // mp_count
    cond_sum = lax.dynamic_slice(small[12:], (dp_index, mp_index * cond_width), (1, cond_width))
    cond_cols = lax.dynamic_slice_in_dim(condition, mp_index * cond_width, cond_width, axis=1)
    silu_vals, silu_pull = jax.vjp(jax.nn.silu, cond_cols)
    grad_condition = silu_pull(cond_sum)[0] * (1.0 / math.sqrt(seq_len))
    scaled = small[:12] * weight_scale

    def parted(values, parts):
        return jnp.transpose(values.reshape(values.shape[0], parts, -1), (1, 0, 2))

    return (
        result.astype(BF),
        grad_tokens,
        grad_caption[None],
        grad_condition,
        attn_sum[:3],
        attn_sum[3].T,
        parted(grad_text, 2),
        parted(ffn_sum[:, : 2 * units], 2),
        ffn_sum[:, 2 * units :].T,
        grad_ada,
        scaled[:4],
        scaled[4:7],
        scaled[7:11].reshape(-1),
        scaled[11, :HEADS],
    )


def solution(mesh):
    return jax.shard_map(
        local,
        mesh=mesh,
        in_specs=(
            P(("dp", "mp"), None),
            P("dp", None, None),
            P("dp", None),
            P(("dp", "mp"), None),
            P(None, "dp", "mp"),
            P("mp", "dp"),
            P(None, "dp", "mp"),
            P(None, "dp", "mp"),
            P("mp", "dp"),
            P("dp", "mp"),
            P(),
            P(),
            P(),
            P(),
            P(),
            P(),
            P(),
        ),
        out_specs=(
            P(("dp", "mp"), None),
            P(("dp", "mp"), None),
            P("dp", None, "mp"),
            P("dp", "mp"),
            P(None, "dp", "mp"),
            P("mp", "dp"),
            P(None, "dp", "mp"),
            P(None, "dp", "mp"),
            P("mp", "dp"),
            P("dp", "mp"),
            P(),
            P(),
            P(),
            P(),
        ),
        check_vma=False,
    )
```

```python
import functools
import math

import jax
import jax.numpy as jnp
from jax import lax
from jax.experimental import pallas as pl
from jax.experimental.pallas import tpu as pltpu
from jax.sharding import PartitionSpec as P

HEADS = 24
HD = 64
PAIR = 2 * HD
NEAR_PARTS = 3
EPS = 1e-06
NEG = -1e30
SCALE = HD ** (-0.5)
BF = jnp.bfloat16
F32 = jnp.float32
NN = (((1,), (0,)), ((), ()))
NT = (((1,), (1,)), ((), ()))
TN = (((0,), (0,)), ((), ()))


def mm(left, right, dims):
    return lax.dot_general(left, right, dims, preferred_element_type=F32)


def swap(value, axis, bit):
    count = lax.axis_size(axis)
    return lax.ppermute(value, axis, [(i, i ^ bit) for i in range(count)])


def all_bits(count):
    return [1 << k for k in range(count.bit_length() - 1)]


def after(value, *others):
    return lax.optimization_barrier((value,) + others)[0]


class Chain:
    def __init__(self, steps):
        self.steps, self.result = steps, None
        self.advance(None)

    def advance(self, arrived):
        try:
            self.wanted = self.steps.send(arrived)
        except StopIteration as end:
            self.wanted, self.result = None, end.value


class Links:
    def __init__(self):
        self.last = ()

    def stage(self, *chains, work=None):
        active = [chain for chain in chains if chain.wanted is not None]
        wanted = [item for chain in active for item in chain.wanted]
        values = [value for value, _, _ in wanted]
        if self.last and values:
            values = lax.optimization_barrier(tuple(values) + self.last)[: len(values)]
        moved = [
            lax.ppermute(value, axis, pairs) for value, (_, axis, pairs) in zip(values, wanted)
        ]
        made = work(lambda value: after(value, *self.last)) if work else ()
        moved, made = lax.optimization_barrier((moved, made))
        self.last = tuple(moved[:1]) or tuple(jax.tree.leaves(made)[:1])
        for chain in active:
            count = len(chain.wanted)
            chain.advance(moved[:count])
            moved = moved[count:]
        return made

    def finish_only(self, chain, others):
        while chain.wanted is not None:
            self.stage(chain, *others)

    def finish(self, *chains):
        while any(chain.wanted is not None for chain in chains):
            self.stage(*chains)


def swap_pairs(axis, bit):
    return [(i, i ^ bit) for i in range(lax.axis_size(axis))]


def crossed_bits():
    bits = all_bits(lax.axis_size("dp"))
    return bits, bits[1::-1] + bits[2:]


def bit_axis(bits, bit):
    return sum(other > bit for other in bits)


def in_order(high, own, other, axis):
    return jnp.stack([jnp.where(high, other, own), jnp.where(high, own, other)], axis=axis)


def halves(high, value, axis):
    zero, one = [lax.index_in_dim(value, k, axis, keepdims=False) for k in range(2)]
    return jnp.where(high, zero, one), jnp.where(high, one, zero)


def gather_blocks(pair, index):
    orders = [bits[::-1] for bits in crossed_bits()]
    values, done = list(pair), ([], [])
    for bits in zip(*orders):
        moved = yield [(value, "dp", swap_pairs("dp", bit)) for value, bit in zip(values, bits)]
        for side, bit in enumerate(bits):
            axis = bit_axis(done[side], bit)
            values[side] = in_order((index & bit) != 0, values[side], moved[side], axis)
            done[side].append(bit)
    return [value.reshape((-1,) + own.shape[1:]) for value, own in zip(values, pair)]


def scatter_blocks(pair, index):
    orders = crossed_bits()
    left = [list(bits) for bits in orders]
    values = [value.reshape((2,) * len(orders[0]) + value.shape[1:]) for value in pair]
    for bits in zip(*orders):
        sent, kept = [], []
        for side, bit in enumerate(bits):
            parts = halves((index & bit) != 0, values[side], bit_axis(left[side], bit))
            sent.append((parts[0].astype(BF), "dp", swap_pairs("dp", bit)))
            kept.append(parts[1])
            left[side].remove(bit)
        moved = yield sent
        values = [plus(own, other) for own, other in zip(kept, moved)]
    return values


def exchange_blocks(value, index):
    count = value.shape[0]
    bits, left, done = all_bits(count), all_bits(count), []
    shape = value.shape[1:]
    value = value.reshape((2,) * len(bits) + shape)
    for bit in bits:
        high = (index & bit) != 0
        sent, kept = halves(high, value, bit_axis(left, bit))
        left.remove(bit)
        (moved,) = yield [(sent, "dp", swap_pairs("dp", bit))]
        value = in_order(high, kept, moved, len(left) + bit_axis(done, bit))
        done.append(bit)
    return value.reshape((count,) + shape)


def plus(*values):
    return sum(value.astype(F32) for value in values)


def sum_all(value, axis):
    bit = 1
    while bit < lax.axis_size(axis):
        value = value + swap(value, axis, bit)
        bit *= 2
    return value


def gather_in_order(value, axis, index):
    bit = 1
    while bit < lax.axis_size(axis):
        other = swap(value, axis, bit)
        high = (index & bit) != 0
        value = jnp.concatenate(
            [jnp.where(high, other, value), jnp.where(high, value, other)], axis=0
        )
        bit *= 2
    return value


def to_partners(value, axis):
    return [(value, axis, swap_pairs(axis, k)) for k in range(1, lax.axis_size(axis))]


def placed(own, moved, index):
    count = len(moved) + 1
    result = jnp.broadcast_to(own[None], (count,) + own.shape)
    place = jnp.arange(count).reshape((count,) + (1,) * own.ndim)
    for k, value in enumerate(moved):
        result = jnp.where(place == (index ^ (k + 1)), value[None], result)
    return result


def tree_sum(values):
    values = list(values)
    while len(values) > 1:
        values = [one + two for one, two in zip(values[::2], values[1::2])]
    return values[0]


def chain_sum(value, axis):
    for bit in all_bits(lax.axis_size(axis)):
        (other,) = yield [(value, axis, swap_pairs(axis, bit))]
        value = value + other
    return value


def rows_from_mp(value, axis=0):
    far = swap(value, "mp", 2)
    near = swap(value, "mp", 1)
    return jnp.concatenate([value, near, far, swap(far, "mp", 1)], axis=axis)


def slots_from_mp(value):
    far, near = yield [(value, "mp", swap_pairs("mp", bit)) for bit in (2, 1)]
    (last,) = yield [(far, "mp", swap_pairs("mp", 1))]
    return [value, near, far, last]


def sum_to_mp(value):
    count = value.shape[0] // 4
    blocks = [value[k * count : (k + 1) * count] for k in range(4)]
    far = blocks[2].astype(F32) + swap(blocks[3].astype(BF), "mp", 1).astype(F32)
    near = blocks[0].astype(F32) + swap(blocks[1].astype(BF), "mp", 1).astype(F32)
    return near + swap(far.astype(BF), "mp", 2).astype(F32)


def shifted(steps, keep=lambda i: True):
    count = lax.axis_size("dp")
    return [(i, i + steps) for i in range(count) if keep(i) and 0 <= i + steps < count]


def even(i):
    return i % 2 == 0


def odd(i):
    return i % 2 == 1


def out_pairs():
    return shifted(-2, even) + shifted(2, odd)


def back_pairs():
    return shifted(2, even) + shifted(-2, odd)


def send_sets(own, is_odd):
    beside, low, high = yield [
        (own, "dp", swap_pairs("dp", 1)),
        (own, "dp", shifted(2)),
        (own, "dp", shifted(-2)),
    ]
    across, third = yield [
        (jnp.where(is_odd, low, high), "dp", swap_pairs("dp", 1)),
        (beside, "dp", out_pairs()),
    ]
    (fourth,) = yield [(across, "dp", back_pairs())]
    return [own, beside, low, high, across, third, fourth]


def set_offsets(is_odd):
    return jnp.where(
        is_odd, jnp.asarray([0, -1, -2, 2, 1, -3, 3]), jnp.asarray([0, 1, -2, 2, -1, 3, -3])
    )


def return_sets(grads, is_odd):
    own, beside, low, high, across, third, fourth = grads
    (fourth,) = yield [(fourth, "dp", out_pairs())]
    across, third = yield [
        (plus(across, fourth).astype(BF), "dp", swap_pairs("dp", 1)),
        (third, "dp", back_pairs()),
    ]
    low = plus(low, jnp.where(is_odd, across, 0)).astype(BF)
    high = plus(high, jnp.where(is_odd, 0, across)).astype(BF)
    beside, low, high = yield [
        (plus(beside, third).astype(BF), "dp", swap_pairs("dp", 1)),
        (low, "dp", shifted(-2)),
        (high, "dp", shifted(2)),
    ]
    return plus(own, beside, low, high)


def norm_rows(values, weights):
    return values * lax.rsqrt(jnp.mean(values * values, axis=-1, keepdims=True) + EPS) * weights


def modulate(values, weights, scales):
    return norm_rows(values, weights) * (1.0 + scales)


def gated_add(branch, weights, gates, resid):
    return resid + jnp.tanh(gates) * norm_rows(branch, weights)


def swiglu(gate_pre, up_pre):
    return jax.nn.silu(gate_pre) * up_pre


def lanes(rows):
    return lax.broadcasted_iota(jnp.int32, (rows, PAIR), 1)


def head_sum(values):
    low = lanes(values.shape[0]) < HD
    first = jnp.sum(jnp.where(low, values, 0.0), axis=-1, keepdims=True)
    second = jnp.sum(jnp.where(low, 0.0, values), axis=-1, keepdims=True)
    return jnp.where(low, first, second)


def partner(values):
    quarter = HD // 4
    first = (lanes(values.shape[0]) % (2 * quarter)) < quarter
    return jnp.where(
        first, pltpu.roll(values, PAIR - quarter, 1), pltpu.roll(values, quarter, 1)
    )


def normed(values):
    return values * lax.rsqrt(head_sum(values * values) / HD + EPS)


def prep_kernel(pre_ref, gains_ref, cos_ref, sin_ref, out_ref):
    width = out_ref.shape[1]
    rows = pre_ref.shape[0]
    cos, sin = cos_ref[...], sin_ref[...]
    for part in range(2):
        for start in range(0, width, PAIR):
            here = pl.ds(part * width + start, PAIR)
            turned = normed(pre_ref[:, here]) * gains_ref[part : part + 1, pl.ds(start, PAIR)]
            if part == 0:
                turned = turned * cos + partner(turned) * sin
                out_ref[pl.ds(0, rows), pl.ds(start, PAIR)] = turned.astype(BF)
            else:
                turned = turned * cos + partner(turned) * sin
                out_ref[pl.ds(rows, rows), pl.ds(start, PAIR)] = turned.astype(BF)
    out_ref[pl.ds(2 * rows, rows), :] = pre_ref[:, pl.ds(2 * width, width)].astype(BF)


def near_prep_kernel(gains_ref, cos_ref, sin_ref, *refs):
    *pre_refs, out_ref = refs
    rows, width = pre_refs[0].shape[0], out_ref.shape[1]
    depth = rows * len(pre_refs)
    for slot, pre_ref in enumerate(pre_refs):
        there = pl.ds(slot * rows, rows)
        cos, sin = cos_ref[there, :], sin_ref[there, :]
        for start in range(0, width, PAIR):
            here = pl.ds(start, PAIR)
            turned = normed(pre_ref[:, here]) * gains_ref[1:2, here]
            turned = turned * cos + partner(turned) * sin
            out_ref[there, here] = turned.astype(BF)
        out_ref[pl.ds(depth + slot * rows, rows), :] = pre_ref[:, pl.ds(width, width)].astype(BF)


def text_prep_kernel(pre_ref, gains_ref, out_ref):
    rows, width = pre_ref.shape[0], out_ref.shape[1]
    for start in range(0, width, PAIR):
        here = pl.ds(start, PAIR)
        value = normed(pre_ref[:, here]) * gains_ref[2:3, here]
        out_ref[pl.ds(0, rows), here] = value.astype(BF)
    out_ref[pl.ds(rows, rows), :] = pre_ref[:, pl.ds(width, width)].astype(BF)


def norm_back(pre, gains, grad):
    ratio = lax.rsqrt(head_sum(pre * pre) / HD + EPS)
    scaled = grad * gains
    grad_pre = ratio * scaled - pre * (ratio * ratio * ratio) * (head_sum(pre * scaled) / HD)
    return grad_pre, jnp.sum(grad * pre * ratio, axis=0, keepdims=True)


def query_back_kernel(pre_ref, gains_ref, cos_ref, sin_ref, self_ref, text_ref, out_ref, head_ref):
    cos, sin = cos_ref[...], sin_ref[...]
    head_ref[...] = jnp.zeros_like(head_ref)
    for start in range(0, out_ref.shape[1], PAIR):
        here = pl.ds(start, PAIR)
        grad = self_ref[:, here] + text_ref[:, here]
        grad = grad * cos - partner(grad) * sin
        grad_pre, grad_gain = norm_back(pre_ref[:, here], gains_ref[0:1, here], grad)
        out_ref[:, here] = grad_pre.astype(BF)
        head_ref[0:1, here] = grad_gain


def key_back_kernel(pre_ref, gains_ref, cos_ref, sin_ref, set_ref, out_ref, head_ref):
    rows, width = pre_ref.shape[0], set_ref.shape[1]
    cos, sin = cos_ref[...], sin_ref[...]
    head_ref[...] = jnp.zeros_like(head_ref)
    for start in range(0, width, PAIR):
        here = pl.ds(start, PAIR)
        grad = set_ref[pl.ds(0, rows), here]
        grad = grad * cos - partner(grad) * sin
        grad_pre, grad_gain = norm_back(
            pre_ref[:, pl.ds(width + start, PAIR)], gains_ref[1:2, here], grad
        )
        out_ref[:, here] = grad_pre.astype(BF)
        head_ref[0:1, here] = grad_gain
    out_ref[:, pl.ds(width, width)] = set_ref[pl.ds(rows, rows), :].astype(BF)


def text_back_kernel(pre_ref, gains_ref, set_ref, out_ref, head_ref):
    rows, width = pre_ref.shape[0], set_ref.shape[1]
    head_ref[...] = jnp.zeros_like(head_ref)
    for start in range(0, width, PAIR):
        here = pl.ds(start, PAIR)
        grad_pre, grad_gain = norm_back(
            pre_ref[:, here], gains_ref[2:3, here], set_ref[pl.ds(0, rows), here]
        )
        out_ref[:, here] = grad_pre.astype(BF)
        head_ref[0:1, here] = grad_gain
    out_ref[:, pl.ds(width, width)] = set_ref[pl.ds(rows, rows), :].astype(BF)


def split_pair(values):
    low = lanes(values.shape[0]) < HD
    zero = jnp.zeros_like(values)
    return jnp.where(low, values, zero), jnp.where(low, zero, values)


def forward_sums(live_ref, query_ref, set_refs, bias_ref, total, weight):
    low = lanes(query_ref.shape[0]) < HD
    total[...] = jnp.zeros_like(total)
    weight[...] = jnp.zeros_like(weight)
    for index, source in enumerate(set_refs):

        @pl.when(live_ref[index] > 0)
        def _(index=index, source=source):
            depth = source.shape[0] // 2
            keys, values = source[pl.ds(0, depth), :], source[pl.ds(depth, depth), :]
            outs, sums = [], []
            for query in split_pair(query_ref[...] * jnp.asarray(SCALE, BF)):
                logits = mm(query, keys, NT)
                if bias_ref is not None:
                    logits = logits + bias_ref[index : index + 1, :]
                probs = jnp.exp(logits)
                sums.append(jnp.sum(probs, axis=-1, keepdims=True))
                outs.append(mm(probs.astype(BF), values, NN))
            total[...] += jnp.where(low, outs[0], outs[1])
            weight[...] += jnp.where(low, sums[0], sums[1])


def views(own_ref, near_refs):
    depth = own_ref.shape[0]
    return [own_ref] + [
        near_ref.at[pl.ds(start, depth), :]
        for near_ref in near_refs
        for start in range(0, near_ref.shape[0], depth)
    ]


def self_forward_kernel(live_ref, query_ref, own_ref, *refs):
    *near_refs, out_ref, log_ref, total, weight = refs
    set_refs = views(own_ref, near_refs)
    forward_sums(live_ref, query_ref, set_refs, None, total, weight)
    out_ref[...] = total[...] / weight[...]
    log_ref[...] = jnp.log(weight[...])


def text_forward_kernel(live_ref, gate_ref, query_ref, self_ref, bias_ref, *refs):
    *set_refs, attn_ref, out_ref, log_ref, total, weight = refs
    forward_sums(live_ref, query_ref, set_refs, bias_ref, total, weight)
    low = lanes(query_ref.shape[0]) < HD
    pair = pl.program_id(0)
    gate = jnp.where(low, gate_ref[2 * pair], gate_ref[2 * pair + 1])
    out = total[...] / weight[...]
    attn_ref[...] = (self_ref[...] + gate * out).astype(BF)
    out_ref[...] = out
    log_ref[...] = jnp.log(weight[...])


def backward_sums(live_ref, query_ref, grad_ref, log_ref, delta, bias_ref, gates, refs, total):
    count = len(refs) // 2
    low = lanes(query_ref.shape[0]) < HD
    logs_all, delta_all = jnp.transpose(log_ref[...]), jnp.transpose(delta)
    total[...] = jnp.zeros_like(total)
    for index, (source, out_ref) in enumerate(zip(refs[:count], refs[count:])):

        @pl.when(live_ref[index] > 0)
        def _(index=index, source=source, out_ref=out_ref):
            queries = split_pair(query_ref[...] * jnp.asarray(SCALE, BF))
            grads = split_pair(grad_ref[...])
            depth = source.shape[0] // 2
            keys, values = source[pl.ds(0, depth), :], source[pl.ds(depth, depth), :]
            grad_query, grad_key, grad_value = [], [], []
            for head in range(2):
                row = head * HD
                logits = mm(keys, queries[head], NT)
                if bias_ref is not None:
                    logits = logits + bias_ref[:, index : index + 1]
                probs = jnp.exp(logits - logs_all[row : row + 1, :])
                value_part = mm(probs.astype(BF), grads[head], NN)
                grad_probs = mm(values, grads[head], NT)
                if gates is not None:
                    value_part = value_part * gates[head]
                    grad_probs = grad_probs * gates[head]
                grad_logits = (probs * (grad_probs - delta_all[row : row + 1, :])).astype(BF)
                grad_value.append(value_part)
                grad_key.append(mm(grad_logits, queries[head], NN))
                grad_query.append(mm(grad_logits, keys, TN))
            total[...] += jnp.where(low, grad_query[0], grad_query[1])
            out_ref[pl.ds(0, depth), :] = (grad_key[0] + grad_key[1]).astype(BF)
            out_ref[pl.ds(depth, depth), :] = (grad_value[0] + grad_value[1]).astype(BF)

        @pl.when(live_ref[index] == 0)
        def _(out_ref=out_ref):
            out_ref[...] = jnp.zeros_like(out_ref)


def self_backward_kernel(
    live_ref, query_ref, grad_ref, out_ref, log_ref, own_ref, *refs
):
    near_refs, grad_refs = refs[:NEAR_PARTS], list(refs[NEAR_PARTS:-2])
    query_grad_ref, total = refs[-2:]
    set_refs = views(own_ref, near_refs) + grad_refs
    delta = head_sum(grad_ref[...].astype(F32) * out_ref[...])
    backward_sums(live_ref, query_ref, grad_ref, log_ref, delta, None, None, set_refs, total)
    query_grad_ref[...] = total[...] * SCALE


def text_backward_kernel(
    live_ref, gate_ref, query_ref, grad_ref, out_ref, log_ref, bias_ref, *refs
):
    *set_refs, query_grad_ref, gate_grad_ref, total = refs
    low = lanes(query_ref.shape[0]) < HD
    pair = pl.program_id(0)
    gates = (gate_ref[2 * pair], gate_ref[2 * pair + 1])
    dots = head_sum(grad_ref[...].astype(F32) * out_ref[...])
    gate_grad_ref[...] = jnp.broadcast_to(jnp.sum(dots, axis=0, keepdims=True), gate_grad_ref.shape)
    delta = jnp.where(low, gates[0], gates[1]) * dots
    backward_sums(live_ref, query_ref, grad_ref, log_ref, delta, bias_ref, gates, set_refs, total)
    query_grad_ref[...] = total[...] * SCALE


def params(limit=40):
    return pltpu.CompilerParams(vmem_limit_bytes=limit * 2**20)


def whole(kernel, outs, cost, *args):
    shapes = [jax.ShapeDtypeStruct(shape, dtype) for shape, dtype in outs]
    return pl.pallas_call(
        kernel,
        out_shape=shapes if len(shapes) > 1 else shapes[0],
        compiler_params=params(),
        cost_estimate=pl.CostEstimate(flops=cost, bytes_accessed=2 * cost // 10, transcendentals=0),
    )(*args)


def column(rows):
    return pl.BlockSpec((rows, PAIR), lambda pair: (0, pair))


def fixed(shape):
    return pl.BlockSpec(shape, lambda pair: (0, 0))


def prepare_near(pre, gains, cos, sin, sets):
    rows, width = pre[0].shape[0] // sets, gains.shape[1]
    depth = rows * len(pre)

    def block(count, columns):
        return pl.BlockSpec((count, columns), lambda k: (k, 0))

    return pl.pallas_call(
        near_prep_kernel,
        grid=(sets,),
        in_specs=[pl.BlockSpec(gains.shape, lambda k: (0, 0))]
        + [block(depth, PAIR)] * 2
        + [block(rows, 2 * width)] * len(pre),
        out_specs=block(2 * depth, width),
        out_shape=jax.ShapeDtypeStruct((sets * 2 * depth, width), BF),
        compiler_params=params(),
        cost_estimate=pl.CostEstimate(
            flops=40 * sets * depth * width,
            bytes_accessed=12 * sets * depth * width,
            transcendentals=0,
        ),
    )(gains, cos, sin, *pre)


def attend(kernel, scalars, columns, bias, sets, outs, passes, scratch, limit=56):
    rows, width = columns[0].shape
    keys = sets[0].shape[0] // 2
    smem = pl.BlockSpec(memory_space=pltpu.SMEM)
    return pl.pallas_call(
        kernel,
        grid=(width // PAIR,),
        in_specs=[smem] * len(scalars)
        + [column(value.shape[0]) for value in columns]
        + [fixed(value.shape) for value in bias]
        + [column(value.shape[0]) for value in sets],
        out_specs=[column(depth) for depth, _ in outs],
        out_shape=[jax.ShapeDtypeStruct((depth, width), dtype) for depth, dtype in outs],
        scratch_shapes=[pltpu.VMEM((rows, PAIR), F32)] * scratch,
        compiler_params=params(limit),
        cost_estimate=pl.CostEstimate(
            flops=passes * 16 * rows * keys * width,
            bytes_accessed=40 * rows * width,
            transcendentals=4 * rows * keys * width // HD,
        ),
    )(*scalars, *columns, *bias, *sets)


def local(
    tokens,
    caption,
    condition,
    cotangent,
    qkv_weight,
    proj_weight,
    text_weight,
    ffn_weight,
    down_weight,
    ada_weight,
    norm_gains,
    head_gains,
    ada_bias,
    cross_gate,
    group_map,
    grid_width,
    caption_len,
):
    dp_count = lax.axis_size("dp")
    mp_count = lax.axis_size("mp")
    dp_index = lax.axis_index("dp")
    mp_index = lax.axis_index("mp")
    row_count, width = tokens.shape
    seq_len = row_count * mp_count
    local_width = qkv_weight.shape[2]
    local_heads = local_width // HD
    text_len, text_dim = caption.shape[1:]
    units = ffn_weight.shape[2]
    shard = qkv_weight.shape[1]
    weight_scale = 1.0 / math.sqrt(seq_len * dp_count)
    is_odd = (dp_index % 2) == 1
    links = Links()

    qkv_shard = jnp.transpose(qkv_weight, (1, 0, 2)).reshape(shard, 3 * local_width)
    rest_shard = jnp.concatenate(
        [proj_weight.T, jnp.transpose(ffn_weight, (1, 0, 2)).reshape(shard, 2 * units), down_weight.T],
        axis=1,
    )
    qkv_full = lax.all_gather(qkv_shard, "dp", axis=0, tiled=True)
    rest = lax.all_gather(rest_shard, "dp", axis=0, tiled=True)
    cuts = (0, local_width, local_width + 2 * units, local_width + 3 * units)
    proj_full, ffn_full, down_full = [rest[:, low:high] for low, high in zip(cuts[:-1], cuts[1:])]

    text_shard = text_weight.shape[1]
    quarter_rows = text_len // mp_count
    my_rows = lax.dynamic_slice_in_dim(caption[0], mp_index * quarter_rows, quarter_rows, axis=0)
    text_matrix = jnp.transpose(text_weight, (1, 0, 2)).reshape(text_shard, 2 * local_width)
    my_rows = jnp.transpose(my_rows.reshape(quarter_rows, dp_count, text_shard), (1, 0, 2))

    def modulate_all():
        value = jax.nn.silu(condition).astype(BF)
        moved = yield to_partners(value, "dp")
        value = placed(value, moved, dp_index).reshape(dp_count, width)
        cond_mine = lax.dynamic_slice_in_dim(value, dp_index * shard, shard, axis=1)
        value = mm(cond_mine, ada_weight, NN)
        for bit in all_bits(dp_count):
            (other,) = yield [(value, "dp", swap_pairs("dp", bit))]
            value = value + other
        bias_part = lax.dynamic_slice_in_dim(ada_bias, mp_index * width, width)
        value = value + bias_part[None, :]
        moved = yield to_partners(value, "mp")
        value = placed(value, moved, mp_index)
        return cond_mine, value

    def caption_features():
        value = yield from exchange_blocks(my_rows, dp_index)
        far, near = yield [(value, "mp", swap_pairs("mp", bit)) for bit in (2, 1)]
        (last,) = yield [(far, "mp", swap_pairs("mp", 1))]
        return jnp.concatenate([value, near, far, last], axis=1)

    mod_chain, caption_chain = Chain(modulate_all()), Chain(caption_features())
    token_chain = Chain(send_sets(tokens, is_odd))
    links.finish(mod_chain, caption_chain, token_chain)
    cond_mine, modulation = mod_chain.result
    text_all = caption_chain.result.reshape(dp_count * text_len, text_shard)

    origins = dp_index + set_offsets(is_odd)
    chosen = jnp.arange(dp_count)[None, :] == origins[:, None]

    def looked_up(table):
        return jnp.sum(jnp.where(chosen, table[None, :], 0), axis=1)

    inside = (origins >= 0) & (origins < dp_count)
    first_slot = jnp.sum(jnp.where(jnp.arange(dp_count) == dp_index, group_map, 0))
    grid = jnp.sum(jnp.where(jnp.arange(dp_count) == dp_index, grid_width, 0))
    live = (inside & (looked_up(group_map) == first_slot)).astype(jnp.int32)
    lengths = looked_up(caption_len)

    near_scales = jnp.sum(
        jnp.where(chosen[1:, :, None], modulation[0][None], 0.0), axis=1
    )
    scale_attn, gate_attn, scale_ffn, gate_ffn = [
        lax.dynamic_index_in_dim(modulation, dp_index, 1, False)[k] for k in range(4)
    ]
    gains = [norm_gains[k] for k in range(4)]
    act_rows = tokens.astype(F32)
    first_in, first_pull = jax.vjp(modulate, act_rows, gains[0], scale_attn)
    near_tokens = jnp.stack(token_chain.result[1:]).astype(F32)
    near_in = modulate(near_tokens, gains[0], near_scales[:, None, :]).astype(BF)
    near_sets = near_in.shape[0]

    text_part = mm(text_all, text_matrix, NN).astype(BF)
    text_part = text_part.reshape(dp_count, text_len, 2 * local_width)
    text_sum = Chain(
        scatter_blocks([text_part[..., :local_width], text_part[..., local_width:]], dp_index)
    )
    first_chain = Chain(slots_from_mp(first_in.astype(BF)))
    near_chains = [
        Chain(slots_from_mp(near_in[k : k + 2].reshape(2 * row_count, width)))
        for k in range(0, near_sets, 2)
    ]
    links.stage(text_sum, first_chain, near_chains[0])
    links.stage(text_sum, first_chain, *near_chains[:2])
    first_low = jnp.concatenate(first_chain.result, axis=0)

    blocks = mp_index ^ jnp.arange(mp_count, dtype=jnp.int32)
    token_ids = (blocks[:, None] * row_count + jnp.arange(row_count, dtype=jnp.int32)).reshape(-1)
    text_ids = (blocks[:, None] * quarter_rows + jnp.arange(quarter_rows, dtype=jnp.int32)).reshape(-1)
    positions = ((origins - first_slot)[:, None] * seq_len + token_ids[None, :]).reshape(-1)
    quarter = HD // 4
    lane = jnp.arange(PAIR, dtype=jnp.int32)
    freqs = jnp.exp((lane % quarter).astype(F32) * (-math.log(10000.0) / quarter))
    place = jnp.where((lane % HD < HD // 2)[None, :], (positions // grid)[:, None], (positions % grid)[:, None])
    angles = place.astype(F32) * freqs[None, :]
    cos = jnp.cos(angles)
    sin = jnp.sin(angles) * jnp.where((lane % (2 * quarter)) < quarter, -1.0, 1.0)[None, :]
    local_gains = lax.dynamic_slice_in_dim(head_gains, mp_index * local_width, local_width, axis=1)
    tanh_gate = jnp.tanh(lax.dynamic_slice_in_dim(cross_gate, mp_index * local_heads, local_heads))

    bias = jnp.where(text_ids[None, :] < lengths[:, None], 0.0, NEG).astype(F32)
    bias = jnp.concatenate([bias, bias[:1]], axis=0)

    def project(tie):
        qkv_pre = mm(tie(first_low), qkv_full, NN)
        prepared = whole(
            prep_kernel,
            [((3 * seq_len, local_width), BF)],
            20 * seq_len * 3 * local_width,
            qkv_pre,
            local_gains,
            cos[:seq_len],
            sin[:seq_len],
        )
        return qkv_pre, prepared

    part_sets = near_sets // NEAR_PARTS
    part_rows = part_sets * seq_len

    def project_near(tie, k):
        pre = [mm(tie(slot), qkv_full[:, local_width:], NN) for slot in near_chains[k].result]
        there = slice(seq_len + k * part_rows, seq_len + (k + 1) * part_rows)
        return prepare_near(pre, local_gains, cos[there], sin[there], part_sets)

    (qkv_pre, prepared), near_first = links.stage(
        text_sum, *near_chains, work=lambda tie: (project(tie), project_near(tie, 0))
    )
    query = prepared[:seq_len]
    links.finish(text_sum)
    text_pre = jnp.concatenate(text_sum.result, axis=1)
    text_set = whole(
        text_prep_kernel,
        [((2 * text_len, local_width), BF)],
        20 * text_len * 2 * local_width,
        text_pre,
        local_gains,
    )
    text_sets_chain = Chain(send_sets(text_set, is_odd))
    near_second = links.stage(
        text_sets_chain, *near_chains, work=lambda tie: project_near(tie, 1)
    )
    links.finish(*near_chains)
    near_third = links.stage(text_sets_chain, work=lambda tie: project_near(tie, 2))
    self_sets = [prepared[seq_len:], near_first, near_second, near_third]

    def attend_self(tie):
        return attend(
            self_forward_kernel, [live], [tie(query)], [], self_sets, [(seq_len, F32)] * 2, 2, 2
        )

    out_self, log_self = links.stage(text_sets_chain, work=attend_self)
    text_sets = text_sets_chain.result

    def attend_text(tie):
        attn_low, out_text, log_text = attend(
            text_forward_kernel,
            [live, tanh_gate],
            [tie(query), out_self],
            [bias],
            text_sets,
            [(seq_len, BF), (seq_len, F32), (seq_len, F32)],
            2,
            2,
        )
        return attn_low, out_text, log_text

    attn_low, out_text, log_text = links.stage(work=attend_text)
    attn_rows = sum_to_mp(mm(attn_low, proj_full, NT))
    middle, middle_pull = jax.vjp(gated_add, attn_rows, gains[1], gate_attn, act_rows)
    second_in, second_pull = jax.vjp(modulate, middle, gains[2], scale_ffn)
    second_low = rows_from_mp(second_in.astype(BF))
    ffn_pre = mm(second_low, ffn_full, NN)
    hidden_f, swiglu_pull = jax.vjp(swiglu, ffn_pre[:, :units], ffn_pre[:, units:])
    hidden_low = hidden_f.astype(BF)
    ffn_rows = sum_to_mp(mm(hidden_low, down_full, NT))
    result, result_pull = jax.vjp(gated_add, ffn_rows, gains[3], gate_ffn, middle)


    grad_out = cotangent.astype(F32)
    grad_ffn_rows, grad_gain_four, grad_gate_ffn, grad_middle_a = result_pull(grad_out)
    grad_ffn_all = rows_from_mp(grad_ffn_rows.astype(BF))
    grad_hidden = mm(grad_ffn_all, down_full, NN)
    grad_gate_pre, grad_up_pre = swiglu_pull(grad_hidden)
    grad_pre_low = jnp.concatenate([grad_gate_pre, grad_up_pre], axis=1).astype(BF)
    second_part = mm(grad_pre_low, ffn_full, NT).astype(BF)

    def ffn_backward(tie):
        grad_second = sum_to_mp(second_part)
        terms = [mm(second_low, grad_pre_low, TN), mm(grad_ffn_all, hidden_low, TN)]
        return grad_second, jnp.concatenate([term.astype(BF) for term in terms], axis=1)

    grad_second, ffn_terms = links.stage(work=ffn_backward)
    ffn_sum = lax.psum_scatter(ffn_terms, "dp", scatter_dimension=0, tiled=True)
    grad_middle_b, grad_gain_three, grad_scale_ffn = second_pull(grad_second)
    grad_attn_rows, grad_gain_two, grad_gate_attn, grad_act_a = middle_pull(
        grad_middle_a + grad_middle_b
    )
    grad_attn_all = links.stage(
        work=lambda tie: rows_from_mp(tie(grad_attn_rows.astype(BF)))
    )

    def text_backward(tie):
        grad_attn_low = mm(tie(grad_attn_all), proj_full, NN).astype(BF)
        return grad_attn_low, attend(
            text_backward_kernel,
            [live, tanh_gate],
            [query, grad_attn_low, out_text, log_text],
            [bias.T],
            text_sets,
            [(2 * text_len, BF)] * len(text_sets) + [(seq_len, F32), (8, F32)],
            5,
            1,
        )

    def self_backward(tie):
        return attend(
            self_backward_kernel,
            [live],
            [query, tie(grad_attn_low), out_self, log_self],
            [],
            self_sets,
            [(2 * seq_len, BF)] * (near_sets + 1) + [(seq_len, F32)],
            5,
            1,
        )

    grad_attn_low, text_grads = links.stage(work=text_backward)
    gate_dots = text_grads[-1]
    text_return = Chain(return_sets(text_grads[: len(text_sets)], is_odd))
    self_grads = links.stage(text_return, work=self_backward)
    self_return = Chain(return_sets(self_grads[:-1], is_odd))

    def query_backward(tie):
        grad_query_low, head_query = whole(
            query_back_kernel,
            [((seq_len, local_width), BF), ((8, local_width), F32)],
            20 * seq_len * local_width,
            qkv_pre,
            local_gains,
            cos[:seq_len],
            sin[:seq_len],
            tie(self_grads[-1]),
            text_grads[-2],
        )
        return (
            grad_query_low,
            head_query,
            mm(first_low, grad_query_low, TN).astype(BF),
            mm(grad_attn_all, attn_low, TN).astype(BF),
        )

    grad_query_low, head_query, grad_query_weight, grad_proj = links.stage(
        text_return, self_return, work=query_backward
    )

    links.stage(text_return, self_return)
    own_text = text_return.result

    def text_rows_backward(tie):
        return whole(
            text_back_kernel,
            [((text_len, 2 * local_width), BF), ((8, local_width), F32)],
            20 * text_len * 2 * local_width,
            text_pre,
            local_gains,
            tie(own_text),
        )

    grad_text_low, head_text = text_rows_backward(lambda value: value)
    text_back = Chain(
        gather_blocks([grad_text_low[:, :local_width], grad_text_low[:, local_width:]], dp_index)
    )
    links.finish_only(self_return, (text_back,))
    own_self, ffn_sum = lax.optimization_barrier((self_return.result, ffn_sum))

    def key_backward(tie):
        grad_key_low, head_key = whole(
            key_back_kernel,
            [((seq_len, 2 * local_width), BF), ((8, local_width), F32)],
            20 * seq_len * 2 * local_width,
            qkv_pre,
            local_gains,
            cos[:seq_len],
            sin[:seq_len],
            tie(own_self),
        )
        first_part = mm(grad_query_low, qkv_full[:, :local_width], NT) + mm(
            grad_key_low, qkv_full[:, local_width:], NT
        )
        return grad_key_low, head_key, first_part.astype(BF)

    def blocks(value):
        return value.reshape(dp_count, shard, local_width)

    def sum_rows(tie):
        first_blocks = [first_part[k * row_count : (k + 1) * row_count] for k in range(mp_count)]
        moved = swap(first_blocks[3], "mp", 1)
        far_rows = plus(first_blocks[2], moved).astype(BF)
        grad_first = plus(first_blocks[0], swap(first_blocks[1], "mp", 1), swap(far_rows, "mp", 2))
        grad_keys = mm(first_low, after(grad_key_low, far_rows), TN).astype(BF)
        terms = [
            grad_query_weight,
            grad_keys[:, :local_width],
            grad_keys[:, local_width:],
            grad_proj,
        ]
        terms = jnp.stack([blocks(term) for term in terms], axis=1)
        attn_terms.append(terms.reshape(-1, shard, local_width))
        return grad_first

    grad_key_low, head_key, first_part = links.stage(text_back, work=key_backward)
    attn_terms = []
    grad_first = links.stage(text_back, work=sum_rows)
    attn_sum = lax.psum_scatter(attn_terms[0], "dp", scatter_dimension=0, tiled=True)
    grad_act_b, grad_gain_one, grad_scale_attn = first_pull(grad_first)
    grad_tokens = grad_act_a + grad_act_b
    mod_grads = jnp.stack([grad_scale_attn, grad_gate_attn, grad_scale_ffn, grad_gate_ffn])
    links.finish(text_back)
    text_rows = jnp.concatenate(text_back.result, axis=1)

    def gather_mod_grads(tie):
        own = tie(mod_grads)
        mod_sum = tree_sum([own] + [swap(own, "mp", k) for k in range(1, mp_count)])
        mine = jnp.arange(mp_count)[:, None] == mp_index
        grad_mod_low = jnp.sum(jnp.where(mine, mod_sum, 0.0), axis=0)[None].astype(BF)
        return grad_mod_low, gather_in_order(grad_mod_low, "dp", dp_index)

    caption_part = mm(text_rows, text_matrix, NT).astype(BF)
    caption_part = caption_part.reshape(dp_count, mp_count, quarter_rows, text_shard)
    caption_part = jnp.transpose(caption_part, (1, 0, 2, 3)).reshape(-1, text_shard)
    (grad_mod_low, grad_mod_all), caption_mine = links.stage(
        work=lambda tie: (gather_mod_grads(tie), sum_to_mp(caption_part).astype(BF))
    )

    row_grads = jnp.stack([grad_gain_one, grad_gain_two, grad_gain_three, grad_gain_four])
    grad_ada = mm(cond_mine, grad_mod_all, TN) * weight_scale
    cond_part = mm(grad_mod_all, ada_weight, NT)
    zeros = functools.partial(jnp.zeros, dtype=F32)
    cond_rows = lax.dynamic_update_slice_in_dim(
        zeros((dp_count, width)), cond_part, dp_index * shard, 1
    )
    head_local = jnp.concatenate([head_query[:1], head_key[:1], head_text[:1]], axis=0)
    head_rows = lax.dynamic_update_slice_in_dim(
        zeros((3, width)), head_local, mp_index * local_width, 1
    )
    bias_rows = jnp.where(
        jnp.arange(mp_count)[:, None] == mp_index, grad_mod_low.astype(F32), 0.0
    )
    gate_local = gate_dots[0].reshape(local_heads, HD)[:, 0] * (1.0 - tanh_gate * tanh_gate)
    gate_row = lax.dynamic_update_slice_in_dim(
        zeros((1, width)), gate_local[None], mp_index * local_heads, 1
    )
    parts = [row_grads, head_rows, bias_rows, gate_row, cond_rows]
    count = sum(part.shape[0] for part in parts)
    small, start = 0.0, 0
    for part in parts:
        end = start + part.shape[0]
        small = small + jnp.pad(part, ((start, count - end), (0, 0)))
        start = end
    block = text_dim // mp_count

    def sum_small():
        moved = yield to_partners(small, "mp")
        return (yield from chain_sum(tree_sum([small] + list(moved)), "dp"))

    def send_captions():
        columns = yield from exchange_blocks(
            caption_mine.reshape(dp_count, quarter_rows, text_shard), dp_index
        )
        columns = jnp.transpose(columns, (1, 0, 2)).reshape(quarter_rows, text_dim)
        pieces = [
            lax.dynamic_slice_in_dim(columns, (mp_index ^ k) * block, block, axis=1)
            for k in range(mp_count)
        ]
        moved = yield [(pieces[k], "mp", swap_pairs("mp", k)) for k in range(1, mp_count)]
        return [pieces[0]] + list(moved)

    small_chain, caption_back = Chain(sum_small()), Chain(send_captions())
    links.finish(small_chain, caption_back)
    small = small_chain.result
    grad_caption = jnp.zeros((text_len, block), F32)
    for k, piece in enumerate(caption_back.result):
        grad_caption = lax.dynamic_update_slice_in_dim(
            grad_caption, piece.astype(F32), (mp_index ^ k) * quarter_rows, 0
        )
    grad_text = mm(text_all, text_rows, TN) * weight_scale
    ffn_sum = ffn_sum.astype(F32) * weight_scale
    attn_sum = attn_sum.astype(F32) * weight_scale
    cond_width = width // mp_count
    cond_sum = lax.dynamic_slice(small[12:], (dp_index, mp_index * cond_width), (1, cond_width))
    cond_cols = lax.dynamic_slice_in_dim(condition, mp_index * cond_width, cond_width, axis=1)
    silu_vals, silu_pull = jax.vjp(jax.nn.silu, cond_cols)
    grad_condition = silu_pull(cond_sum)[0] * (1.0 / math.sqrt(seq_len))
    scaled = small[:12] * weight_scale

    def parted(values, parts):
        return jnp.transpose(values.reshape(values.shape[0], parts, -1), (1, 0, 2))

    return (
        result.astype(BF),
        grad_tokens,
        grad_caption[None],
        grad_condition,
        attn_sum[:3],
        attn_sum[3].T,
        parted(grad_text, 2),
        parted(ffn_sum[:, : 2 * units], 2),
        ffn_sum[:, 2 * units :].T,
        grad_ada,
        scaled[:4],
        scaled[4:7],
        scaled[7:11].reshape(-1),
        scaled[11, :HEADS],
    )


def solution(mesh):
    return jax.shard_map(
        local,
        mesh=mesh,
        in_specs=(
            P(("dp", "mp"), None),
            P("dp", None, None),
            P("dp", None),
            P(("dp", "mp"), None),
            P(None, "dp", "mp"),
            P("mp", "dp"),
            P(None, "dp", "mp"),
            P(None, "dp", "mp"),
            P("mp", "dp"),
            P("dp", "mp"),
            P(),
            P(),
            P(),
            P(),
            P(),
            P(),
            P(),
        ),
        out_specs=(
            P(("dp", "mp"), None),
            P(("dp", "mp"), None),
            P("dp", None, "mp"),
            P("dp", "mp"),
            P(None, "dp", "mp"),
            P("mp", "dp"),
            P(None, "dp", "mp"),
            P(None, "dp", "mp"),
            P("mp", "dp"),
            P("dp", "mp"),
            P(),
            P(),
            P(),
            P(),
        ),
        check_vma=False,
    )
```

```python
import functools
import math

import jax
import jax.numpy as jnp
from jax import lax
from jax.experimental import pallas as pl
from jax.experimental.pallas import tpu as pltpu
from jax.sharding import PartitionSpec as P

HEADS = 24
HD = 64
PAIR = 2 * HD
NEAR_PARTS = 3
EPS = 1e-06
NEG = -1e30
SCALE = HD ** (-0.5)
BF = jnp.bfloat16
F32 = jnp.float32
NN = (((1,), (0,)), ((), ()))
NT = (((1,), (1,)), ((), ()))
TN = (((0,), (0,)), ((), ()))


def mm(left, right, dims):
    return lax.dot_general(left, right, dims, preferred_element_type=F32)


def swap(value, axis, bit):
    count = lax.axis_size(axis)
    return lax.ppermute(value, axis, [(i, i ^ bit) for i in range(count)])


def all_bits(count):
    return [1 << k for k in range(count.bit_length() - 1)]


def after(value, *others):
    return lax.optimization_barrier((value,) + others)[0]


class Chain:
    def __init__(self, steps):
        self.steps, self.result = steps, None
        self.advance(None)

    def advance(self, arrived):
        try:
            self.wanted = self.steps.send(arrived)
        except StopIteration as end:
            self.wanted, self.result = None, end.value


class Links:
    def __init__(self):
        self.last = ()

    def stage(self, *chains, work=None):
        active = [chain for chain in chains if chain.wanted is not None]
        wanted = [item for chain in active for item in chain.wanted]
        values = [value for value, _, _ in wanted]
        if self.last and values:
            values = lax.optimization_barrier(tuple(values) + self.last)[: len(values)]
        moved = [
            lax.ppermute(value, axis, pairs) for value, (_, axis, pairs) in zip(values, wanted)
        ]
        made = work(lambda value: after(value, *self.last)) if work else ()
        moved, made = lax.optimization_barrier((moved, made))
        self.last = tuple(moved[:1]) or tuple(jax.tree.leaves(made)[:1])
        for chain in active:
            count = len(chain.wanted)
            chain.advance(moved[:count])
            moved = moved[count:]
        return made

    def finish_only(self, chain, others):
        while chain.wanted is not None:
            self.stage(chain, *others)

    def finish(self, *chains):
        while any(chain.wanted is not None for chain in chains):
            self.stage(*chains)


def swap_pairs(axis, bit):
    return [(i, i ^ bit) for i in range(lax.axis_size(axis))]


def crossed_bits():
    bits = all_bits(lax.axis_size("dp"))
    return bits, bits[1::-1] + bits[2:]


def bit_axis(bits, bit):
    return sum(other > bit for other in bits)


def in_order(high, own, other, axis):
    return jnp.stack([jnp.where(high, other, own), jnp.where(high, own, other)], axis=axis)


def halves(high, value, axis):
    zero, one = [lax.index_in_dim(value, k, axis, keepdims=False) for k in range(2)]
    return jnp.where(high, zero, one), jnp.where(high, one, zero)


def gather_blocks(pair, index):
    orders = [bits[::-1] for bits in crossed_bits()]
    values, done = list(pair), ([], [])
    for bits in zip(*orders):
        moved = yield [(value, "dp", swap_pairs("dp", bit)) for value, bit in zip(values, bits)]
        for side, bit in enumerate(bits):
            axis = bit_axis(done[side], bit)
            values[side] = in_order((index & bit) != 0, values[side], moved[side], axis)
            done[side].append(bit)
    return [value.reshape((-1,) + own.shape[1:]) for value, own in zip(values, pair)]


def scatter_blocks(pair, index):
    orders = crossed_bits()
    left = [list(bits) for bits in orders]
    values = [value.reshape((2,) * len(orders[0]) + value.shape[1:]) for value in pair]
    for bits in zip(*orders):
        sent, kept = [], []
        for side, bit in enumerate(bits):
            parts = halves((index & bit) != 0, values[side], bit_axis(left[side], bit))
            sent.append((parts[0].astype(BF), "dp", swap_pairs("dp", bit)))
            kept.append(parts[1])
            left[side].remove(bit)
        moved = yield sent
        values = [plus(own, other) for own, other in zip(kept, moved)]
    return values


def exchange_blocks(value, index):
    count = value.shape[0]
    bits, left, done = all_bits(count), all_bits(count), []
    shape = value.shape[1:]
    value = value.reshape((2,) * len(bits) + shape)
    for bit in bits:
        high = (index & bit) != 0
        sent, kept = halves(high, value, bit_axis(left, bit))
        left.remove(bit)
        (moved,) = yield [(sent, "dp", swap_pairs("dp", bit))]
        value = in_order(high, kept, moved, len(left) + bit_axis(done, bit))
        done.append(bit)
    return value.reshape((count,) + shape)


def plus(*values):
    return sum(value.astype(F32) for value in values)


def sum_all(value, axis):
    bit = 1
    while bit < lax.axis_size(axis):
        value = value + swap(value, axis, bit)
        bit *= 2
    return value


def gather_in_order(value, axis, index):
    bit = 1
    while bit < lax.axis_size(axis):
        other = swap(value, axis, bit)
        high = (index & bit) != 0
        value = jnp.concatenate(
            [jnp.where(high, other, value), jnp.where(high, value, other)], axis=0
        )
        bit *= 2
    return value


def chain_sum(value, axis):
    for bit in all_bits(lax.axis_size(axis)):
        (other,) = yield [(value, axis, swap_pairs(axis, bit))]
        value = value + other
    return value


def rows_from_mp(value, axis=0):
    far = swap(value, "mp", 2)
    near = swap(value, "mp", 1)
    return jnp.concatenate([value, near, far, swap(far, "mp", 1)], axis=axis)


def slots_from_mp(value):
    far, near = yield [(value, "mp", swap_pairs("mp", bit)) for bit in (2, 1)]
    (last,) = yield [(far, "mp", swap_pairs("mp", 1))]
    return [value, near, far, last]


def sum_to_mp(value):
    count = value.shape[0] // 4
    blocks = [value[k * count : (k + 1) * count] for k in range(4)]
    far = blocks[2].astype(F32) + swap(blocks[3].astype(BF), "mp", 1).astype(F32)
    near = blocks[0].astype(F32) + swap(blocks[1].astype(BF), "mp", 1).astype(F32)
    return near + swap(far.astype(BF), "mp", 2).astype(F32)


def shifted(steps, keep=lambda i: True):
    count = lax.axis_size("dp")
    return [(i, i + steps) for i in range(count) if keep(i) and 0 <= i + steps < count]


def even(i):
    return i % 2 == 0


def odd(i):
    return i % 2 == 1


def out_pairs():
    return shifted(-2, even) + shifted(2, odd)


def back_pairs():
    return shifted(2, even) + shifted(-2, odd)


def send_sets(own, is_odd):
    beside, low, high = yield [
        (own, "dp", swap_pairs("dp", 1)),
        (own, "dp", shifted(2)),
        (own, "dp", shifted(-2)),
    ]
    across, third = yield [
        (jnp.where(is_odd, low, high), "dp", swap_pairs("dp", 1)),
        (beside, "dp", out_pairs()),
    ]
    (fourth,) = yield [(across, "dp", back_pairs())]
    return [own, beside, low, high, across, third, fourth]


def set_offsets(is_odd):
    return jnp.where(
        is_odd, jnp.asarray([0, -1, -2, 2, 1, -3, 3]), jnp.asarray([0, 1, -2, 2, -1, 3, -3])
    )


def return_sets(grads, is_odd):
    own, beside, low, high, across, third, fourth = grads
    (fourth,) = yield [(fourth, "dp", out_pairs())]
    across, third = yield [
        (plus(across, fourth).astype(BF), "dp", swap_pairs("dp", 1)),
        (third, "dp", back_pairs()),
    ]
    low = plus(low, jnp.where(is_odd, across, 0)).astype(BF)
    high = plus(high, jnp.where(is_odd, 0, across)).astype(BF)
    beside, low, high = yield [
        (plus(beside, third).astype(BF), "dp", swap_pairs("dp", 1)),
        (low, "dp", shifted(-2)),
        (high, "dp", shifted(2)),
    ]
    return [own, beside, low, high]


def norm_rows(values, weights):
    return values * lax.rsqrt(jnp.mean(values * values, axis=-1, keepdims=True) + EPS) * weights


def modulate(values, weights, scales):
    return norm_rows(values, weights) * (1.0 + scales)


def gated_add(branch, weights, gates, resid):
    return resid + jnp.tanh(gates) * norm_rows(branch, weights)


def swiglu(gate_pre, up_pre):
    return jax.nn.silu(gate_pre) * up_pre


def lanes(rows):
    return lax.broadcasted_iota(jnp.int32, (rows, PAIR), 1)


def head_sum(values):
    low = lanes(values.shape[0]) < HD
    first = jnp.sum(jnp.where(low, values, 0.0), axis=-1, keepdims=True)
    second = jnp.sum(jnp.where(low, 0.0, values), axis=-1, keepdims=True)
    return jnp.where(low, first, second)


def partner(values):
    quarter = HD // 4
    first = (lanes(values.shape[0]) % (2 * quarter)) < quarter
    return jnp.where(
        first, pltpu.roll(values, PAIR - quarter, 1), pltpu.roll(values, quarter, 1)
    )


def normed(values):
    return values * lax.rsqrt(head_sum(values * values) / HD + EPS)


def prep_kernel(pre_ref, gains_ref, cos_ref, sin_ref, out_ref):
    width = out_ref.shape[1]
    rows = pre_ref.shape[0]
    cos, sin = cos_ref[...], sin_ref[...]
    for part in range(2):
        for start in range(0, width, PAIR):
            here = pl.ds(part * width + start, PAIR)
            turned = normed(pre_ref[:, here]) * gains_ref[part : part + 1, pl.ds(start, PAIR)]
            if part == 0:
                turned = turned * cos + partner(turned) * sin
                out_ref[pl.ds(0, rows), pl.ds(start, PAIR)] = turned.astype(BF)
            else:
                turned = turned * cos + partner(turned) * sin
                out_ref[pl.ds(rows, rows), pl.ds(start, PAIR)] = turned.astype(BF)
    out_ref[pl.ds(2 * rows, rows), :] = pre_ref[:, pl.ds(2 * width, width)].astype(BF)


def near_prep_kernel(gains_ref, cos_ref, sin_ref, *refs):
    *pre_refs, out_ref = refs
    rows, width = pre_refs[0].shape[0], out_ref.shape[1]
    depth = rows * len(pre_refs)
    for slot, pre_ref in enumerate(pre_refs):
        there = pl.ds(slot * rows, rows)
        cos, sin = cos_ref[there, :], sin_ref[there, :]
        for start in range(0, width, PAIR):
            here = pl.ds(start, PAIR)
            turned = normed(pre_ref[:, here]) * gains_ref[1:2, here]
            turned = turned * cos + partner(turned) * sin
            out_ref[there, here] = turned.astype(BF)
        out_ref[pl.ds(depth + slot * rows, rows), :] = pre_ref[:, pl.ds(width, width)].astype(BF)


def text_prep_kernel(pre_ref, gains_ref, out_ref):
    rows, width = pre_ref.shape[0], out_ref.shape[1]
    for start in range(0, width, PAIR):
        here = pl.ds(start, PAIR)
        value = normed(pre_ref[:, here]) * gains_ref[2:3, here]
        out_ref[pl.ds(0, rows), here] = value.astype(BF)
    out_ref[pl.ds(rows, rows), :] = pre_ref[:, pl.ds(width, width)].astype(BF)


def norm_back(pre, gains, grad):
    ratio = lax.rsqrt(head_sum(pre * pre) / HD + EPS)
    scaled = grad * gains
    grad_pre = ratio * scaled - pre * (ratio * ratio * ratio) * (head_sum(pre * scaled) / HD)
    return grad_pre, jnp.sum(grad * pre * ratio, axis=0, keepdims=True)


def query_back_kernel(pre_ref, gains_ref, cos_ref, sin_ref, self_ref, text_ref, out_ref, head_ref):
    cos, sin = cos_ref[...], sin_ref[...]
    head_ref[...] = jnp.zeros_like(head_ref)
    for start in range(0, out_ref.shape[1], PAIR):
        here = pl.ds(start, PAIR)
        grad = self_ref[:, here] + text_ref[:, here]
        grad = grad * cos - partner(grad) * sin
        grad_pre, grad_gain = norm_back(pre_ref[:, here], gains_ref[0:1, here], grad)
        out_ref[:, here] = grad_pre.astype(BF)
        head_ref[0:1, here] = grad_gain


def summed(refs, rows, columns):
    return sum(ref[rows, columns].astype(F32) for ref in refs)


def key_back_kernel(pre_ref, gains_ref, cos_ref, sin_ref, *refs):
    *set_refs, out_ref, head_ref = refs
    rows, width = pre_ref.shape[0], set_refs[0].shape[1]
    cos, sin = cos_ref[...], sin_ref[...]
    head_ref[...] = jnp.zeros_like(head_ref)
    for start in range(0, width, PAIR):
        here = pl.ds(start, PAIR)
        grad = summed(set_refs, pl.ds(0, rows), here)
        grad = grad * cos - partner(grad) * sin
        grad_pre, grad_gain = norm_back(
            pre_ref[:, pl.ds(width + start, PAIR)], gains_ref[1:2, here], grad
        )
        out_ref[:, here] = grad_pre.astype(BF)
        head_ref[0:1, here] = grad_gain
        out_ref[:, pl.ds(width + start, PAIR)] = summed(set_refs, pl.ds(rows, rows), here).astype(BF)


def text_back_kernel(pre_ref, gains_ref, *refs):
    *set_refs, out_ref, head_ref = refs
    rows, width = pre_ref.shape[0], set_refs[0].shape[1]
    head_ref[...] = jnp.zeros_like(head_ref)
    for start in range(0, width, PAIR):
        here = pl.ds(start, PAIR)
        grad_pre, grad_gain = norm_back(
            pre_ref[:, here], gains_ref[2:3, here], summed(set_refs, pl.ds(0, rows), here)
        )
        out_ref[:, here] = grad_pre.astype(BF)
        head_ref[0:1, here] = grad_gain
        out_ref[:, pl.ds(width + start, PAIR)] = summed(set_refs, pl.ds(rows, rows), here).astype(BF)


def split_pair(values):
    low = lanes(values.shape[0]) < HD
    zero = jnp.zeros_like(values)
    return jnp.where(low, values, zero), jnp.where(low, zero, values)


def forward_sums(live_ref, query_ref, set_refs, bias_ref, total, weight):
    low = lanes(query_ref.shape[0]) < HD
    total[...] = jnp.zeros_like(total)
    weight[...] = jnp.zeros_like(weight)
    for index, source in enumerate(set_refs):

        @pl.when(live_ref[index] > 0)
        def _(index=index, source=source):
            depth = source.shape[0] // 2
            keys, values = source[pl.ds(0, depth), :], source[pl.ds(depth, depth), :]
            outs, sums = [], []
            for query in split_pair(query_ref[...] * jnp.asarray(SCALE, BF)):
                logits = mm(query, keys, NT)
                if bias_ref is not None:
                    logits = logits + bias_ref[index : index + 1, :]
                probs = jnp.exp(logits)
                sums.append(jnp.sum(probs, axis=-1, keepdims=True))
                outs.append(mm(probs.astype(BF), values, NN))
            total[...] += jnp.where(low, outs[0], outs[1])
            weight[...] += jnp.where(low, sums[0], sums[1])


def views(own_ref, near_refs):
    depth = own_ref.shape[0]
    return [own_ref] + [
        near_ref.at[pl.ds(start, depth), :]
        for near_ref in near_refs
        for start in range(0, near_ref.shape[0], depth)
    ]


def self_forward_kernel(live_ref, query_ref, own_ref, *refs):
    *near_refs, out_ref, log_ref, total, weight = refs
    set_refs = views(own_ref, near_refs)
    forward_sums(live_ref, query_ref, set_refs, None, total, weight)
    out_ref[...] = total[...] / weight[...]
    log_ref[...] = jnp.log(weight[...])


def text_forward_kernel(live_ref, gate_ref, query_ref, self_ref, bias_ref, *refs):
    *set_refs, attn_ref, out_ref, log_ref, total, weight = refs
    forward_sums(live_ref, query_ref, set_refs, bias_ref, total, weight)
    low = lanes(query_ref.shape[0]) < HD
    pair = pl.program_id(0)
    gate = jnp.where(low, gate_ref[2 * pair], gate_ref[2 * pair + 1])
    out = total[...] / weight[...]
    attn_ref[...] = (self_ref[...] + gate * out).astype(BF)
    out_ref[...] = out
    log_ref[...] = jnp.log(weight[...])


def backward_sums(live_ref, query_ref, grad_ref, log_ref, delta, bias_ref, gates, refs, total):
    count = len(refs) // 2
    low = lanes(query_ref.shape[0]) < HD
    logs_all, delta_all = jnp.transpose(log_ref[...]), jnp.transpose(delta)
    total[...] = jnp.zeros_like(total)
    for index, (source, out_ref) in enumerate(zip(refs[:count], refs[count:])):

        @pl.when(live_ref[index] > 0)
        def _(index=index, source=source, out_ref=out_ref):
            queries = split_pair(query_ref[...] * jnp.asarray(SCALE, BF))
            grads = split_pair(grad_ref[...])
            depth = source.shape[0] // 2
            keys, values = source[pl.ds(0, depth), :], source[pl.ds(depth, depth), :]
            grad_query, grad_key, grad_value = [], [], []
            for head in range(2):
                row = head * HD
                logits = mm(keys, queries[head], NT)
                if bias_ref is not None:
                    logits = logits + bias_ref[:, index : index + 1]
                probs = jnp.exp(logits - logs_all[row : row + 1, :])
                value_part = mm(probs.astype(BF), grads[head], NN)
                grad_probs = mm(values, grads[head], NT)
                if gates is not None:
                    value_part = value_part * gates[head]
                    grad_probs = grad_probs * gates[head]
                grad_logits = (probs * (grad_probs - delta_all[row : row + 1, :])).astype(BF)
                grad_value.append(value_part)
                grad_key.append(mm(grad_logits, queries[head], NN))
                grad_query.append(mm(grad_logits, keys, TN))
            total[...] += jnp.where(low, grad_query[0], grad_query[1])
            out_ref[pl.ds(0, depth), :] = (grad_key[0] + grad_key[1]).astype(BF)
            out_ref[pl.ds(depth, depth), :] = (grad_value[0] + grad_value[1]).astype(BF)

        @pl.when(live_ref[index] == 0)
        def _(out_ref=out_ref):
            out_ref[...] = jnp.zeros_like(out_ref)


def self_backward_kernel(
    live_ref, query_ref, grad_ref, out_ref, log_ref, own_ref, *refs
):
    near_refs, grad_refs = refs[:NEAR_PARTS], list(refs[NEAR_PARTS:-2])
    query_grad_ref, total = refs[-2:]
    set_refs = views(own_ref, near_refs) + grad_refs
    delta = head_sum(grad_ref[...].astype(F32) * out_ref[...])
    backward_sums(live_ref, query_ref, grad_ref, log_ref, delta, None, None, set_refs, total)
    query_grad_ref[...] = total[...] * SCALE


def text_backward_kernel(
    live_ref, gate_ref, query_ref, grad_ref, out_ref, log_ref, bias_ref, *refs
):
    *set_refs, query_grad_ref, gate_grad_ref, total = refs
    low = lanes(query_ref.shape[0]) < HD
    pair = pl.program_id(0)
    gates = (gate_ref[2 * pair], gate_ref[2 * pair + 1])
    dots = head_sum(grad_ref[...].astype(F32) * out_ref[...])
    gate_grad_ref[...] = jnp.broadcast_to(jnp.sum(dots, axis=0, keepdims=True), gate_grad_ref.shape)
    delta = jnp.where(low, gates[0], gates[1]) * dots
    backward_sums(live_ref, query_ref, grad_ref, log_ref, delta, bias_ref, gates, set_refs, total)
    query_grad_ref[...] = total[...] * SCALE


def params(limit=40):
    return pltpu.CompilerParams(vmem_limit_bytes=limit * 2**20)


def whole(kernel, outs, cost, *args):
    shapes = [jax.ShapeDtypeStruct(shape, dtype) for shape, dtype in outs]
    return pl.pallas_call(
        kernel,
        out_shape=shapes if len(shapes) > 1 else shapes[0],
        compiler_params=params(),
        cost_estimate=pl.CostEstimate(flops=cost, bytes_accessed=2 * cost // 10, transcendentals=0),
    )(*args)


def column(rows):
    return pl.BlockSpec((rows, PAIR), lambda pair: (0, pair))


def fixed(shape):
    return pl.BlockSpec(shape, lambda pair: (0, 0))


def prepare_near(pre, gains, cos, sin, sets):
    rows, width = pre[0].shape[0] // sets, gains.shape[1]
    depth = rows * len(pre)

    def block(count, columns):
        return pl.BlockSpec((count, columns), lambda k: (k, 0))

    return pl.pallas_call(
        near_prep_kernel,
        grid=(sets,),
        in_specs=[pl.BlockSpec(gains.shape, lambda k: (0, 0))]
        + [block(depth, PAIR)] * 2
        + [block(rows, 2 * width)] * len(pre),
        out_specs=block(2 * depth, width),
        out_shape=jax.ShapeDtypeStruct((sets * 2 * depth, width), BF),
        compiler_params=params(),
        cost_estimate=pl.CostEstimate(
            flops=40 * sets * depth * width,
            bytes_accessed=12 * sets * depth * width,
            transcendentals=0,
        ),
    )(gains, cos, sin, *pre)


def attend(kernel, scalars, columns, bias, sets, outs, passes, scratch, limit=56):
    rows, width = columns[0].shape
    keys = sets[0].shape[0] // 2
    smem = pl.BlockSpec(memory_space=pltpu.SMEM)
    return pl.pallas_call(
        kernel,
        grid=(width // PAIR,),
        in_specs=[smem] * len(scalars)
        + [column(value.shape[0]) for value in columns]
        + [fixed(value.shape) for value in bias]
        + [column(value.shape[0]) for value in sets],
        out_specs=[column(depth) for depth, _ in outs],
        out_shape=[jax.ShapeDtypeStruct((depth, width), dtype) for depth, dtype in outs],
        scratch_shapes=[pltpu.VMEM((rows, PAIR), F32)] * scratch,
        compiler_params=params(limit),
        cost_estimate=pl.CostEstimate(
            flops=passes * 16 * rows * keys * width,
            bytes_accessed=40 * rows * width,
            transcendentals=4 * rows * keys * width // HD,
        ),
    )(*scalars, *columns, *bias, *sets)


def local(
    tokens,
    caption,
    condition,
    cotangent,
    qkv_weight,
    proj_weight,
    text_weight,
    ffn_weight,
    down_weight,
    ada_weight,
    norm_gains,
    head_gains,
    ada_bias,
    cross_gate,
    group_map,
    grid_width,
    caption_len,
):
    dp_count = lax.axis_size("dp")
    mp_count = lax.axis_size("mp")
    dp_index = lax.axis_index("dp")
    mp_index = lax.axis_index("mp")
    row_count, width = tokens.shape
    seq_len = row_count * mp_count
    local_width = qkv_weight.shape[2]
    local_heads = local_width // HD
    text_len, text_dim = caption.shape[1:]
    units = ffn_weight.shape[2]
    shard = qkv_weight.shape[1]
    weight_scale = 1.0 / math.sqrt(seq_len * dp_count)
    is_odd = (dp_index % 2) == 1
    links = Links()

    qkv_shard = jnp.transpose(qkv_weight, (1, 0, 2)).reshape(shard, 3 * local_width)
    rest_shard = jnp.concatenate(
        [proj_weight.T, jnp.transpose(ffn_weight, (1, 0, 2)).reshape(shard, 2 * units), down_weight.T],
        axis=1,
    )
    qkv_full = lax.all_gather(qkv_shard, "dp", axis=0, tiled=True)
    rest = lax.all_gather(rest_shard, "dp", axis=0, tiled=True)
    cuts = (0, local_width, local_width + 2 * units, local_width + 3 * units)
    proj_full, ffn_full, down_full = [rest[:, low:high] for low, high in zip(cuts[:-1], cuts[1:])]

    text_shard = text_weight.shape[1]
    quarter_rows = text_len // mp_count
    my_rows = lax.dynamic_slice_in_dim(caption[0], mp_index * quarter_rows, quarter_rows, axis=0)
    text_matrix = jnp.transpose(text_weight, (1, 0, 2)).reshape(text_shard, 2 * local_width)
    my_rows = jnp.transpose(my_rows.reshape(quarter_rows, dp_count, text_shard), (1, 0, 2))

    def modulate_all():
        value = jax.nn.silu(condition).astype(BF)
        for bit in all_bits(dp_count):
            (other,) = yield [(value, "dp", swap_pairs("dp", bit))]
            value = in_order((dp_index & bit) != 0, value, other, 0).reshape(2 * bit, width)
        cond_mine = lax.dynamic_slice_in_dim(value, dp_index * shard, shard, axis=1)
        value = mm(cond_mine, ada_weight, NN)
        for bit in all_bits(dp_count):
            (other,) = yield [(value, "dp", swap_pairs("dp", bit))]
            value = value + other
        bias_part = lax.dynamic_slice_in_dim(ada_bias, mp_index * width, width)
        value = (value + bias_part[None, :])[None]
        for bit in all_bits(mp_count):
            (other,) = yield [(value, "mp", swap_pairs("mp", bit))]
            value = in_order((mp_index & bit) != 0, value, other, 0).reshape(2 * bit, dp_count, width)
        return cond_mine, value

    def caption_features():
        value = yield from exchange_blocks(my_rows, dp_index)
        far, near = yield [(value, "mp", swap_pairs("mp", bit)) for bit in (2, 1)]
        (last,) = yield [(far, "mp", swap_pairs("mp", 1))]
        return jnp.concatenate([value, near, far, last], axis=1)

    mod_chain, caption_chain = Chain(modulate_all()), Chain(caption_features())
    token_chain = Chain(send_sets(tokens, is_odd))
    links.finish(mod_chain, caption_chain, token_chain)
    cond_mine, modulation = mod_chain.result
    text_all = caption_chain.result.reshape(dp_count * text_len, text_shard)

    origins = dp_index + set_offsets(is_odd)
    chosen = jnp.arange(dp_count)[None, :] == origins[:, None]

    def looked_up(table):
        return jnp.sum(jnp.where(chosen, table[None, :], 0), axis=1)

    inside = (origins >= 0) & (origins < dp_count)
    first_slot = jnp.sum(jnp.where(jnp.arange(dp_count) == dp_index, group_map, 0))
    grid = jnp.sum(jnp.where(jnp.arange(dp_count) == dp_index, grid_width, 0))
    live = (inside & (looked_up(group_map) == first_slot)).astype(jnp.int32)
    lengths = looked_up(caption_len)

    near_scales = jnp.sum(
        jnp.where(chosen[1:, :, None], modulation[0][None], 0.0), axis=1
    )
    scale_attn, gate_attn, scale_ffn, gate_ffn = [
        lax.dynamic_index_in_dim(modulation, dp_index, 1, False)[k] for k in range(4)
    ]
    gains = [norm_gains[k] for k in range(4)]
    act_rows = tokens.astype(F32)
    first_in, first_pull = jax.vjp(modulate, act_rows, gains[0], scale_attn)
    near_tokens = jnp.stack(token_chain.result[1:]).astype(F32)
    near_in = modulate(near_tokens, gains[0], near_scales[:, None, :]).astype(BF)
    near_sets = near_in.shape[0]

    text_part = mm(text_all, text_matrix, NN).astype(BF)
    text_part = text_part.reshape(dp_count, text_len, 2 * local_width)
    text_sum = Chain(
        scatter_blocks([text_part[..., :local_width], text_part[..., local_width:]], dp_index)
    )
    first_chain = Chain(slots_from_mp(first_in.astype(BF)))
    near_chains = [
        Chain(slots_from_mp(near_in[k : k + 2].reshape(2 * row_count, width)))
        for k in range(0, near_sets, 2)
    ]
    links.stage(text_sum, first_chain, near_chains[0])
    links.stage(text_sum, first_chain, *near_chains[:2])
    first_low = jnp.concatenate(first_chain.result, axis=0)

    blocks = mp_index ^ jnp.arange(mp_count, dtype=jnp.int32)
    token_ids = (blocks[:, None] * row_count + jnp.arange(row_count, dtype=jnp.int32)).reshape(-1)
    text_ids = (blocks[:, None] * quarter_rows + jnp.arange(quarter_rows, dtype=jnp.int32)).reshape(-1)
    positions = ((origins - first_slot)[:, None] * seq_len + token_ids[None, :]).reshape(-1)
    quarter = HD // 4
    lane = jnp.arange(PAIR, dtype=jnp.int32)
    freqs = jnp.exp((lane % quarter).astype(F32) * (-math.log(10000.0) / quarter))
    place = jnp.where((lane % HD < HD // 2)[None, :], (positions // grid)[:, None], (positions % grid)[:, None])
    angles = place.astype(F32) * freqs[None, :]
    cos = jnp.cos(angles)
    sin = jnp.sin(angles) * jnp.where((lane % (2 * quarter)) < quarter, -1.0, 1.0)[None, :]
    local_gains = lax.dynamic_slice_in_dim(head_gains, mp_index * local_width, local_width, axis=1)
    tanh_gate = jnp.tanh(lax.dynamic_slice_in_dim(cross_gate, mp_index * local_heads, local_heads))

    bias = jnp.where(text_ids[None, :] < lengths[:, None], 0.0, NEG).astype(F32)
    bias = jnp.concatenate([bias, bias[:1]], axis=0)

    def project(tie):
        qkv_pre = mm(tie(first_low), qkv_full, NN)
        prepared = whole(
            prep_kernel,
            [((3 * seq_len, local_width), BF)],
            20 * seq_len * 3 * local_width,
            qkv_pre,
            local_gains,
            cos[:seq_len],
            sin[:seq_len],
        )
        return qkv_pre, prepared

    part_sets = near_sets // NEAR_PARTS
    part_rows = part_sets * seq_len

    def project_near(tie, k):
        pre = [mm(tie(slot), qkv_full[:, local_width:], NN) for slot in near_chains[k].result]
        there = slice(seq_len + k * part_rows, seq_len + (k + 1) * part_rows)
        return prepare_near(pre, local_gains, cos[there], sin[there], part_sets)

    (qkv_pre, prepared), near_first = links.stage(
        text_sum, *near_chains, work=lambda tie: (project(tie), project_near(tie, 0))
    )
    query = prepared[:seq_len]
    links.finish(text_sum)
    text_pre = jnp.concatenate(text_sum.result, axis=1)
    text_set = whole(
        text_prep_kernel,
        [((2 * text_len, local_width), BF)],
        20 * text_len * 2 * local_width,
        text_pre,
        local_gains,
    )
    text_sets_chain = Chain(send_sets(text_set, is_odd))
    near_second = links.stage(
        text_sets_chain, *near_chains, work=lambda tie: project_near(tie, 1)
    )
    links.finish(*near_chains)
    near_third = links.stage(text_sets_chain, work=lambda tie: project_near(tie, 2))
    self_sets = [prepared[seq_len:], near_first, near_second, near_third]

    def attend_self(tie):
        return attend(
            self_forward_kernel, [live], [tie(query)], [], self_sets, [(seq_len, F32)] * 2, 2, 2
        )

    out_self, log_self = links.stage(text_sets_chain, work=attend_self)
    text_sets = text_sets_chain.result

    def attend_text(tie):
        attn_low, out_text, log_text = attend(
            text_forward_kernel,
            [live, tanh_gate],
            [tie(query), out_self],
            [bias],
            text_sets,
            [(seq_len, BF), (seq_len, F32), (seq_len, F32)],
            2,
            2,
        )
        return attn_low, out_text, log_text

    attn_low, out_text, log_text = links.stage(work=attend_text)
    attn_rows = sum_to_mp(mm(attn_low, proj_full, NT))
    middle, middle_pull = jax.vjp(gated_add, attn_rows, gains[1], gate_attn, act_rows)
    second_in, second_pull = jax.vjp(modulate, middle, gains[2], scale_ffn)
    second_low = rows_from_mp(second_in.astype(BF))
    ffn_pre = mm(second_low, ffn_full, NN)
    hidden_f, swiglu_pull = jax.vjp(swiglu, ffn_pre[:, :units], ffn_pre[:, units:])
    hidden_low = hidden_f.astype(BF)
    ffn_rows = sum_to_mp(mm(hidden_low, down_full, NT))
    result, result_pull = jax.vjp(gated_add, ffn_rows, gains[3], gate_ffn, middle)


    grad_out = cotangent.astype(F32)
    grad_ffn_rows, grad_gain_four, grad_gate_ffn, grad_middle_a = result_pull(grad_out)
    grad_ffn_all = rows_from_mp(grad_ffn_rows.astype(BF))
    grad_hidden = mm(grad_ffn_all, down_full, NN)
    grad_gate_pre, grad_up_pre = swiglu_pull(grad_hidden)
    grad_pre_low = jnp.concatenate([grad_gate_pre, grad_up_pre], axis=1).astype(BF)
    second_part = mm(grad_pre_low, ffn_full, NT).astype(BF)

    def ffn_backward(tie):
        grad_second = sum_to_mp(second_part)
        terms = [mm(second_low, grad_pre_low, TN), mm(grad_ffn_all, hidden_low, TN)]
        return grad_second, jnp.concatenate([term.astype(BF) for term in terms], axis=1)

    grad_second, ffn_terms = links.stage(work=ffn_backward)
    ffn_sum = lax.psum_scatter(ffn_terms, "dp", scatter_dimension=0, tiled=True)
    grad_middle_b, grad_gain_three, grad_scale_ffn = second_pull(grad_second)
    grad_attn_rows, grad_gain_two, grad_gate_attn, grad_act_a = middle_pull(
        grad_middle_a + grad_middle_b
    )
    grad_attn_all = links.stage(
        work=lambda tie: rows_from_mp(tie(grad_attn_rows.astype(BF)))
    )

    def text_backward(tie):
        grad_attn_low = mm(tie(grad_attn_all), proj_full, NN).astype(BF)
        return grad_attn_low, attend(
            text_backward_kernel,
            [live, tanh_gate],
            [query, grad_attn_low, out_text, log_text],
            [bias.T],
            text_sets,
            [(2 * text_len, BF)] * len(text_sets) + [(seq_len, F32), (8, F32)],
            5,
            1,
        )

    def self_backward(tie):
        return attend(
            self_backward_kernel,
            [live],
            [query, tie(grad_attn_low), out_self, log_self],
            [],
            self_sets,
            [(2 * seq_len, BF)] * (near_sets + 1) + [(seq_len, F32)],
            5,
            1,
        )

    grad_attn_low, text_grads = links.stage(work=text_backward)
    gate_dots = text_grads[-1]
    text_return = Chain(return_sets(text_grads[: len(text_sets)], is_odd))
    self_grads = links.stage(text_return, work=self_backward)
    self_return = Chain(return_sets(self_grads[:-1], is_odd))

    def query_backward(tie):
        grad_query_low, head_query = whole(
            query_back_kernel,
            [((seq_len, local_width), BF), ((8, local_width), F32)],
            20 * seq_len * local_width,
            qkv_pre,
            local_gains,
            cos[:seq_len],
            sin[:seq_len],
            tie(self_grads[-1]),
            text_grads[-2],
        )
        return (
            grad_query_low,
            head_query,
            mm(first_low, grad_query_low, TN).astype(BF),
            mm(grad_attn_all, attn_low, TN).astype(BF),
        )

    grad_query_low, head_query, grad_query_weight, grad_proj = links.stage(
        text_return, self_return, work=query_backward
    )

    links.stage(text_return, self_return)
    own_text = text_return.result

    def text_rows_backward(tie):
        return whole(
            text_back_kernel,
            [((text_len, 2 * local_width), BF), ((8, local_width), F32)],
            20 * text_len * 2 * local_width,
            text_pre,
            local_gains,
            *own_text,
        )

    grad_text_low, head_text = text_rows_backward(lambda value: value)
    text_back = Chain(
        gather_blocks([grad_text_low[:, :local_width], grad_text_low[:, local_width:]], dp_index)
    )
    links.finish_only(self_return, (text_back,))
    own_self, ffn_sum = lax.optimization_barrier((self_return.result, ffn_sum))

    def key_backward(tie):
        grad_key_low, head_key = whole(
            key_back_kernel,
            [((seq_len, 2 * local_width), BF), ((8, local_width), F32)],
            20 * seq_len * 2 * local_width,
            qkv_pre,
            local_gains,
            cos[:seq_len],
            sin[:seq_len],
            *own_self,
        )
        first_part = mm(grad_query_low, qkv_full[:, :local_width], NT) + mm(
            grad_key_low, qkv_full[:, local_width:], NT
        )
        return grad_key_low, head_key, first_part.astype(BF)

    def blocks(value):
        return value.reshape(dp_count, shard, local_width)

    def sum_rows(tie):
        first_blocks = [first_part[k * row_count : (k + 1) * row_count] for k in range(mp_count)]
        moved = swap(first_blocks[3], "mp", 1)
        far_rows = plus(first_blocks[2], moved).astype(BF)
        grad_first = plus(first_blocks[0], swap(first_blocks[1], "mp", 1), swap(far_rows, "mp", 2))
        grad_keys = mm(first_low, after(grad_key_low, far_rows), TN).astype(BF)
        terms = [
            grad_query_weight,
            grad_keys[:, :local_width],
            grad_keys[:, local_width:],
            grad_proj,
        ]
        terms = jnp.stack([blocks(term) for term in terms], axis=1)
        attn_terms.append(terms.reshape(-1, shard, local_width))
        return grad_first

    grad_key_low, head_key, first_part = links.stage(text_back, work=key_backward)
    attn_terms = []
    grad_first = links.stage(text_back, work=sum_rows)
    attn_sum = lax.psum_scatter(attn_terms[0], "dp", scatter_dimension=0, tiled=True)
    grad_act_b, grad_gain_one, grad_scale_attn = first_pull(grad_first)
    grad_tokens = grad_act_a + grad_act_b
    mod_grads = jnp.stack([grad_scale_attn, grad_gate_attn, grad_scale_ffn, grad_gate_ffn])
    links.finish(text_back)
    text_rows = jnp.concatenate(text_back.result, axis=1)

    def gather_mod_grads(tie):
        mod_sum = sum_all(tie(mod_grads), "mp")
        mine = jnp.arange(mp_count)[:, None] == mp_index
        grad_mod_low = jnp.sum(jnp.where(mine, mod_sum, 0.0), axis=0)[None].astype(BF)
        return grad_mod_low, gather_in_order(grad_mod_low, "dp", dp_index)

    caption_part = mm(text_rows, text_matrix, NT).astype(BF)
    caption_part = caption_part.reshape(dp_count, mp_count, quarter_rows, text_shard)
    caption_part = jnp.transpose(caption_part, (1, 0, 2, 3)).reshape(-1, text_shard)
    (grad_mod_low, grad_mod_all), caption_mine = links.stage(
        work=lambda tie: (gather_mod_grads(tie), sum_to_mp(caption_part).astype(BF))
    )

    row_grads = jnp.stack([grad_gain_one, grad_gain_two, grad_gain_three, grad_gain_four])
    grad_ada = mm(cond_mine, grad_mod_all, TN) * weight_scale
    cond_part = mm(grad_mod_all, ada_weight, NT)
    zeros = functools.partial(jnp.zeros, dtype=F32)
    cond_rows = lax.dynamic_update_slice_in_dim(
        zeros((dp_count, width)), cond_part, dp_index * shard, 1
    )
    head_local = jnp.concatenate([head_query[:1], head_key[:1], head_text[:1]], axis=0)
    head_rows = lax.dynamic_update_slice_in_dim(
        zeros((3, width)), head_local, mp_index * local_width, 1
    )
    bias_rows = jnp.where(
        jnp.arange(mp_count)[:, None] == mp_index, grad_mod_low.astype(F32), 0.0
    )
    gate_local = gate_dots[0].reshape(local_heads, HD)[:, 0] * (1.0 - tanh_gate * tanh_gate)
    gate_row = lax.dynamic_update_slice_in_dim(
        zeros((1, width)), gate_local[None], mp_index * local_heads, 1
    )
    parts = [row_grads, head_rows, bias_rows, gate_row, cond_rows]
    count = sum(part.shape[0] for part in parts)
    small, start = 0.0, 0
    for part in parts:
        end = start + part.shape[0]
        small = small + jnp.pad(part, ((start, count - end), (0, 0)))
        start = end
    block = text_dim // mp_count

    def sum_small():
        value = yield from chain_sum(small, "mp")
        return (yield from chain_sum(value, "dp"))

    def send_captions():
        columns = yield from exchange_blocks(
            caption_mine.reshape(dp_count, quarter_rows, text_shard), dp_index
        )
        columns = jnp.transpose(columns, (1, 0, 2)).reshape(quarter_rows, text_dim)
        pieces = [
            lax.dynamic_slice_in_dim(columns, (mp_index ^ k) * block, block, axis=1)
            for k in range(mp_count)
        ]
        moved = yield [(pieces[k], "mp", swap_pairs("mp", k)) for k in range(1, mp_count)]
        return [pieces[0]] + list(moved)

    small_chain, caption_back = Chain(sum_small()), Chain(send_captions())
    links.finish(small_chain, caption_back)
    small = small_chain.result
    grad_caption = jnp.zeros((text_len, block), F32)
    for k, piece in enumerate(caption_back.result):
        grad_caption = lax.dynamic_update_slice_in_dim(
            grad_caption, piece.astype(F32), (mp_index ^ k) * quarter_rows, 0
        )
    grad_text = mm(text_all, text_rows, TN) * weight_scale
    ffn_sum = ffn_sum.astype(F32) * weight_scale
    attn_sum = attn_sum.astype(F32) * weight_scale
    cond_width = width // mp_count
    cond_sum = lax.dynamic_slice(small[12:], (dp_index, mp_index * cond_width), (1, cond_width))
    cond_cols = lax.dynamic_slice_in_dim(condition, mp_index * cond_width, cond_width, axis=1)
    silu_vals, silu_pull = jax.vjp(jax.nn.silu, cond_cols)
    grad_condition = silu_pull(cond_sum)[0] * (1.0 / math.sqrt(seq_len))
    scaled = small[:12] * weight_scale

    def parted(values, parts):
        return jnp.transpose(values.reshape(values.shape[0], parts, -1), (1, 0, 2))

    return (
        result.astype(BF),
        grad_tokens,
        grad_caption[None],
        grad_condition,
        attn_sum[:3],
        attn_sum[3].T,
        parted(grad_text, 2),
        parted(ffn_sum[:, : 2 * units], 2),
        ffn_sum[:, 2 * units :].T,
        grad_ada,
        scaled[:4],
        scaled[4:7],
        scaled[7:11].reshape(-1),
        scaled[11, :HEADS],
    )


def solution(mesh):
    return jax.shard_map(
        local,
        mesh=mesh,
        in_specs=(
            P(("dp", "mp"), None),
            P("dp", None, None),
            P("dp", None),
            P(("dp", "mp"), None),
            P(None, "dp", "mp"),
            P("mp", "dp"),
            P(None, "dp", "mp"),
            P(None, "dp", "mp"),
            P("mp", "dp"),
            P("dp", "mp"),
            P(),
            P(),
            P(),
            P(),
            P(),
            P(),
            P(),
        ),
        out_specs=(
            P(("dp", "mp"), None),
            P(("dp", "mp"), None),
            P("dp", None, "mp"),
            P("dp", "mp"),
            P(None, "dp", "mp"),
            P("mp", "dp"),
            P(None, "dp", "mp"),
            P(None, "dp", "mp"),
            P("mp", "dp"),
            P("dp", "mp"),
            P(),
            P(),
            P(),
            P(),
        ),
        check_vma=False,
    )
```
